32 devices in a mesh: member: 2 (over x), row: 16 (over z, y, core).
Axes of the slice: x: 2, y: 2, z: 4, core: 2. Of those that a mesh axis runs over, the one named last changes fastest.
Arguments:
- innovation: bfloat16 [8, 1024, 2048], P('member', 'row'), parts along dimension 0, may hold values from -6 to 6
- background: bfloat16 [8, 1024, 2048], P('member', 'row'), parts along dimension 0, may hold values from -6 to 6
- level_weight: float32 [4], replicated, may hold values from 0.25 to 4
Outputs:
- displacement: float32 [4, 1024, 2048], P('member', 'row'), parts along dimension 0
The draws below stay inside these ranges and needn't reach their ends.
There are 2 independent parts, one for each index of `member`. The reference program is written for one: setup_inputs(seed, part) draws one part's arguments, and reference() takes and returns one part's arrays. A program takes and returns all parts, laid end to end along the dimension named above; an argument that names none is the same for every part. Nothing has to cross between parts.
All inputs are finite; a program needn't handle non-finite values.
Results may differ from the reference program's by a relative error of at most 0.0003.
Values may be sent and summed in bfloat16 or wider, within the bound.
No kernel may reach another device: no remote copies, remote signals or barrier semaphores. Data moves between devices by JAX's collectives and lax.ppermute only.
A program may use at most 64 MiB of HBM per device.

```python
import math
import jax
import jax.numpy as jnp
from jax import lax

LEV = 4
NX = 2048
HALF = 64
SIGMA = 64
NY = 1024


def steps_of(rng, shape, split, least, top_value):
    def one(dim, shards_of):
        steps = jax.random.uniform(jax.random.fold_in(jax.random.fold_in(rng, 6), dim), (shards_of,), jnp.float32, least / len(split), top_value / len(split))
        return jnp.repeat(jnp.exp(steps), shape[dim] // shards_of).reshape((-1,) + (1,) * (len(shape) - dim - 1))

    gain = one(*split[0])
    for cut in split[1:]:
        gain = gain * one(*cut)
    return gain


def noise(own_key, dims, scale, most, pieces=(), kind=jnp.bfloat16):
    level = steps_of(own_key, dims, pieces, -0.22, 0.18) if pieces else 1.0
    values = jax.random.normal(own_key, dims, jnp.float32) * scale * level
    return jnp.minimum(jnp.maximum(values, -most), most).astype(kind)


def setup_inputs(seed: int = 0, part: int = 0) -> dict:
    key_of = jax.random.split(jax.random.key(seed), 4)
    part_splits = jax.random.split(jax.random.fold_in(key_of[3], part), 4)
    innovation = noise(part_splits[0], (LEV, NY, NX), 1.0, 6.0, ((1, 16),))
    background = noise(part_splits[1], (LEV, NY, NX), 1.0, 6.0, ((1, 16),))
    level_weight = jnp.clip(jnp.exp(jax.random.uniform(key_of[2], (LEV,), jnp.float32, math.log(0.25), math.log(4.0))), 0.25, 4.0)
    return dict(innovation=innovation, background=background, level_weight=level_weight)


def tap_at(offset):
    grid = jnp.arange(-HALF, HALF + 1).astype(jnp.float32)
    spread = jnp.float32(SIGMA)
    total = jnp.sqrt(jnp.sum(jnp.exp(-grid * grid / (spread * spread))))
    off = offset.astype(jnp.float32)
    value = jnp.exp(-off * off / (2.0 * spread * spread)) / total
    return jnp.where(jnp.abs(offset) <= HALF, value, jnp.float32(0.0))

def band_blocks():
    inner = jnp.arange(128)[:, None]
    outer = jnp.arange(128)[None, :]
    return [tap_at(128 * shift + inner - outer) for shift in (-1, 0, 1)]

def smooth_last(values, blocks):
    lead = values.shape[:-1]
    length = values.shape[-1]
    nblocks = length // 128
    widths = [(0, 0)] * (values.ndim - 1) + [(128, 128)]
    padded = jnp.pad(values, widths).reshape(lead + (nblocks + 2, 128))
    total = jnp.zeros(lead + (nblocks, 128), jnp.float32)
    for index in range(3):
        part = padded[..., index:index + nblocks, :]
        total = total + jnp.dot(part, blocks[index], precision=lax.Precision.HIGHEST, preferred_element_type=jnp.float32)
    return total.reshape(lead + (length,))

def smooth_mid(values, blocks):
    chans, length, width = values.shape
    nblocks = length // 128
    padded = jnp.pad(values, ((0, 0), (128, 128), (0, 0))).reshape(chans, nblocks + 2, 128, width)
    total = jnp.zeros((chans, nblocks, 128, width), jnp.float32)
    for index in range(3):
        part = padded[:, index:index + nblocks]
        total = total + jnp.einsum('cbix,io->cbox', part, blocks[index], precision=lax.Precision.HIGHEST, preferred_element_type=jnp.float32)
    return total.reshape(chans, length, width)

def reference(innovation, background, level_weight):
    ny = innovation.shape[1]
    nx = innovation.shape[2]

    def level_step(carry, inputs):
        numer_y, numer_x, denom = carry
        inno, back, lw = inputs
        inno = inno.astype(jnp.float32)
        back = back.astype(jnp.float32)
        padded = jnp.pad(back, 1)
        grad_y = 0.5 * (padded[2:, 1:-1] - padded[:-2, 1:-1])
        grad_x = 0.5 * (padded[1:-1, 2:] - padded[1:-1, :-2])
        numer_y = numer_y + lw * inno * grad_y
        numer_x = numer_x + lw * inno * grad_x
        denom = denom + lw * (grad_y * grad_y + grad_x * grad_x)
        return ((numer_y, numer_x, denom), None)
    zeros = jnp.zeros((ny, nx), jnp.float32)
    start = (zeros, zeros, zeros + jnp.float32(1.0))
    (numer_y, numer_x, denom), _ = lax.scan(level_step, start, (innovation, background, level_weight))
    raw = jnp.stack([numer_y / denom, numer_x / denom])
    blocks = band_blocks()
    zonal = smooth_last(raw, blocks)
    return smooth_mid(zonal, blocks)
```

```python
import functools
import math

import jax
import jax.numpy as jnp
import numpy as np
from jax import lax
from jax.experimental import pallas as pl
from jax.experimental.pallas import tpu as pltpu
from jax.sharding import PartitionSpec as P

HALF = 64
SIGMA = 64
LANES = 128
GROUP_Y = 4
GROUP_X = 8
F32 = jnp.float32
BF16 = jnp.bfloat16
NORM = math.sqrt(sum(math.exp(-k * k / (SIGMA * SIGMA)) for k in range(-HALF, HALF + 1)))


def split(values):
    high = values.astype(BF16)
    return high, (values - high.astype(F32)).astype(BF16)


def dot(left, right):
    return jnp.dot(left, right, preferred_element_type=F32)


def iota(shape, dim):
    return lax.broadcasted_iota(jnp.int32, shape, dim)


def taps(offset):
    off = offset.astype(F32)
    value = jnp.exp(off * off * (-0.5 / (SIGMA * SIGMA))) * (1.0 / NORM)
    return jnp.where(jnp.abs(offset) <= HALF, value, 0.0)


def zonal_band():
    offset = np.arange(4 * LANES)[:, None] - LANES - np.arange(2 * LANES)[None, :]
    band = np.exp(-offset * offset / (2.0 * SIGMA * SIGMA)) / NORM
    band = np.where(np.abs(offset) <= HALF, band, 0.0).astype(np.float32)
    high = band.astype(BF16)
    return np.stack([high, (band - high.astype(np.float32)).astype(BF16)])


def windows(nblocks):
    for first in range(0, nblocks, 2):
        low, high = max(first - 1, 0), min(first + 3, nblocks)
        yield first, low, high, (low - first + 1) * LANES, (high - first + 1) * LANES


def raw_kernel(lw_ref, inno_ref, back_ref, near_ref, far_ref, raw_ref, *msg_refs):
    levels, rows, width = inno_ref.shape
    nblocks = width // LANES
    even = lax.rem(lax.axis_index("row"), 2) == 0
    row, col = iota((rows, rows), 0), iota((rows, rows), 1)
    diff_y = ((col == row + 1).astype(F32) - (col == row - 1).astype(F32)).astype(BF16)
    shape = (4 * LANES, 2 * LANES)
    off = iota(shape, 0) - LANES - iota(shape, 1)
    diff_x = ((off == 1).astype(F32) - (off == -1).astype(F32)).astype(BF16)
    at = iota((rows, 2 * LANES), 0)
    for first, low, high, top, bottom in windows(nblocks):
        here = pl.ds(first * LANES, 2 * LANES)
        numer_y = numer_x = 0.0
        denom = 1.0
        for level in range(levels):
            weight = lw_ref[level]
            near, far = near_ref[level, :, here].astype(F32), far_ref[level, :, here].astype(F32)
            above = jnp.where(even, far, near)
            below = jnp.where(even, near, far)
            grad_y = dot(diff_y, back_ref[level, :, here])
            grad_y += jnp.where(at == 0, -above, 0.0) + jnp.where(at == rows - 1, below, 0.0)
            around = back_ref[level, :, low * LANES : high * LANES]
            grad_x = dot(around, diff_x[top:bottom])
            scaled = inno_ref[level, :, here].astype(F32) * (0.5 * weight)
            numer_y += scaled * grad_y
            numer_x += scaled * grad_x
            denom += (0.25 * weight) * (grad_y * grad_y + grad_x * grad_x)
        inverse = 1.0 / denom
        for comp, numer in enumerate((numer_y, numer_x)):
            raw = numer * inverse
            for k in range(2):
                raw_ref[first + k, comp * rows : (comp + 1) * rows, :] = raw[:, k * LANES : (k + 1) * LANES]
    per = nblocks // len(msg_refs)
    both = 2 * rows
    shape = (per * LANES, per * LANES // GROUP_X)
    sum_x = (iota(shape, 0) // GROUP_X == iota(shape, 1)).astype(F32).astype(BF16)
    shape = (both // GROUP_Y, both)
    sum_y = (iota(shape, 1) // GROUP_Y == iota(shape, 0)).astype(F32).astype(BF16)
    for index, msg_ref in enumerate(msg_refs):
        total = 0.0
        for k in range(per):
            high, low = split(raw_ref[index * per + k])
            msg_ref[k * both : (k + 1) * both, :] = high
            total += dot(low, sum_x[k * LANES : (k + 1) * LANES])
        msg_ref[per * both :, :] = dot(sum_y, total.astype(BF16)).astype(BF16)


def shifted_taps(rows, shift):
    return taps(iota((rows, rows), 1) - iota((rows, rows), 0) + shift)


def near_kernel(raw_ref, near_ref, out_ref):
    nblocks, both, _ = raw_ref.shape
    rows = both // 2
    side = 1 - 2 * lax.rem(lax.axis_index("row"), 2)
    high, low = split(
        jnp.concatenate([shifted_taps(rows, 0), shifted_taps(rows, side * rows)], axis=1)
    )
    two = jnp.concatenate([high, low], axis=0)
    for first in range(0, nblocks, 2):
        for comp in range(2):
            here = pl.ds(comp * rows, rows)
            pairs = []
            for k in (first, first + 1):
                pairs.append(jnp.concatenate([raw_ref[k, here, :], near_ref[k, here, :]], axis=0))
            high_x, low_x = split(jnp.concatenate(pairs, axis=1))
            part = dot(two, high_x)
            part = part[:rows] + part[rows:] + dot(high, low_x)
            for k in range(2):
                out_ref[first + k, here, :] = part[:, k * LANES : (k + 1) * LANES]


def far_kernel(band_ref, part_ref, *refs):
    *msg_refs, out_ref, high_ref, low_ref = refs
    nblocks, both, _ = part_ref.shape
    rows = both // 2
    side = 1 - 2 * lax.rem(lax.axis_index("row"), 2)
    taps_far = shifted_taps(rows, -side * rows)
    high, low = split(taps_far)
    two = jnp.concatenate([high, low], axis=0)
    shape = (rows, rows // GROUP_Y)
    mean_y = jnp.where(iota(shape, 0) // GROUP_Y == iota(shape, 1), 1.0 / GROUP_Y, 0.0).astype(BF16)
    taps_group = dot(high, mean_y).astype(BF16)
    per = nblocks // len(msg_refs)
    shape = (per * LANES // GROUP_X, per * LANES)
    mean_x = jnp.where(iota(shape, 1) // GROUP_X == iota(shape, 0), 1.0 / GROUP_X, 0.0).astype(BF16)
    groups = rows // GROUP_Y
    for index, msg_ref in enumerate(msg_refs):
        rest = []
        for comp in range(2):
            start = per * both + comp * groups
            rest.append(dot(taps_group, msg_ref[start : start + groups, :]))
        rest = jnp.concatenate(rest, axis=0).astype(BF16)
        for first in range(0, per, 2):
            spread = dot(rest, mean_x[:, first * LANES : (first + 2) * LANES])
            for comp in range(2):
                here = pl.ds(comp * rows, rows)
                got = [
                    msg_ref[k * both + comp * rows : k * both + (comp + 1) * rows, :]
                    for k in (first, first + 1)
                ]
                part = dot(two, jnp.concatenate(got, axis=1))
                part = part[:rows] + part[rows:] + spread[comp * rows : (comp + 1) * rows]
                for k in range(2):
                    block = index * per + first + k
                    total = part_ref[block, here, :] + part[:, k * LANES : (k + 1) * LANES]
                    high_ref[block, here, :], low_ref[block, here, :] = split(total)
    for first, low_, high_, top, bottom in windows(nblocks):
        upper = jnp.concatenate([high_ref[k] for k in range(low_, high_)], axis=1)
        lower = jnp.concatenate([low_ref[k] for k in range(low_, high_)], axis=1)
        band = band_ref[0, top:bottom, :]
        result = dot(upper, band) + dot(lower, band) + dot(upper, band_ref[1, top:bottom, :])
        here = pl.ds(first * LANES, 2 * LANES)
        out_ref[0, :, here] = result[:rows]
        out_ref[1, :, here] = result[rows:]


VMEM = pl.BlockSpec(memory_space=pltpu.VMEM)
SMEM = pl.BlockSpec(memory_space=pltpu.SMEM)
PARAMS = pltpu.CompilerParams(vmem_limit_bytes=40 * 1024 * 1024)
CHUNKS = 2


def body(innovation, background, level_weight):
    levels, rows, width = innovation.shape
    if rows != HALF or width % (8 * LANES * CHUNKS):
        raise NotImplementedError("slab shape")
    nblocks = width // LANES
    both = 2 * rows
    count = lax.axis_size("row")
    chip = [(i, i ^ 1) for i in range(count) if i ^ 1 < count]
    away = [(i, j) for i in range(count) for j in [((i + 1) ^ 1) - 1] if 0 <= j < count]
    even = lax.rem(lax.axis_index("row"), 2) == 0
    first, last = background[:, :1], background[:, rows - 1 :]
    edge_near = lax.ppermute(jnp.where(even, last, first), "row", chip)
    edge_far = lax.ppermute(jnp.where(even, first, last), "row", away)
    per = nblocks // CHUNKS
    msg = jax.ShapeDtypeStruct((per * both + both // GROUP_Y * per * LANES // GROUP_X // LANES, LANES), BF16)
    blocks = jax.ShapeDtypeStruct((nblocks, both, LANES), F32)
    raw, *msgs = pl.pallas_call(
        raw_kernel,
        out_shape=[blocks] + [msg] * CHUNKS,
        in_specs=[SMEM] + [VMEM] * 4,
        out_specs=[VMEM] * (1 + CHUNKS),
        compiler_params=PARAMS,
    )(level_weight, innovation, background, edge_near, edge_far)
    msgs = [lax.ppermute(m, "row", away) for m in msgs]
    raw_near = lax.ppermute(raw, "row", chip)
    part = pl.pallas_call(
        near_kernel,
        out_shape=blocks,
        in_specs=[VMEM] * 2,
        out_specs=VMEM,
        compiler_params=PARAMS,
        cost_estimate=pl.CostEstimate(flops=10**9, bytes_accessed=3 * 2**20, transcendentals=0),
    )(raw, raw_near)
    return pl.pallas_call(
        far_kernel,
        out_shape=jax.ShapeDtypeStruct((2, rows, width), F32),
        in_specs=[VMEM] * (2 + CHUNKS),
        out_specs=VMEM,
        scratch_shapes=[pltpu.VMEM((nblocks, both, LANES), BF16)] * 2,
        compiler_params=PARAMS,
    )(jnp.asarray(zonal_band()), part, *msgs)


def solution(mesh):
    placed = (P("member", "row", None), P("member", "row", None), P())
    return jax.shard_map(
        body, mesh=mesh, in_specs=placed, out_specs=P("member", "row", None), check_vma=False
    )
```

```python
import math

import jax
import jax.numpy as jnp
import numpy as np
from jax import lax
from jax.experimental import pallas as pl
from jax.experimental.pallas import tpu as pltpu
from jax.sharding import PartitionSpec as P

HALF = 64
SIGMA = 64
LANES = 128
GROUP_Y = 4
GROUP_X = 8
SPAN = LANES * GROUP_X
TILE = 16
QUARTERS = 4
F32 = jnp.float32
BF16 = jnp.bfloat16
NORM = math.sqrt(sum(math.exp(-k * k / (SIGMA * SIGMA)) for k in range(-HALF, HALF + 1)))

VMEM = pl.BlockSpec(memory_space=pltpu.VMEM)
SMEM = pl.BlockSpec(memory_space=pltpu.SMEM)
ANY = pl.BlockSpec(memory_space=pl.ANY)
PARAMS = pltpu.CompilerParams(vmem_limit_bytes=40 * 1024 * 1024)


def split(values):
    high = values.astype(BF16)
    return high, (values - high.astype(F32)).astype(BF16)


def dot(left, right):
    return jnp.dot(left, right, preferred_element_type=F32)


def iota(shape, dim):
    return lax.broadcasted_iota(jnp.int32, shape, dim)


def one_hot(mask, value=1.0):
    return jnp.where(mask, value, 0.0).astype(BF16)


def taps(offset):
    off = offset.astype(F32)
    value = jnp.exp(off * off * (-0.5 / (SIGMA * SIGMA))) * (1.0 / NORM)
    return jnp.where(jnp.abs(offset) <= HALF, value, 0.0)


def zonal_band():
    offset = np.arange(4 * LANES)[:, None] - LANES - np.arange(2 * LANES)[None, :]
    band = np.exp(-offset * offset / (2.0 * SIGMA * SIGMA)) / NORM
    band = np.where(np.abs(offset) <= HALF, band, 0.0).astype(np.float32)
    high = band.astype(BF16)
    return np.stack([high, (band - high.astype(np.float32)).astype(BF16)])


def window(first, nblocks):
    low, high = max(first - 1, 0), min(first + 3, nblocks)
    return low, high, (low - first + 1) * LANES, (high - first + 1) * LANES


def parity():
    return lax.rem(lax.axis_index("row"), 2)


def message_rows(rows, nblocks, with_edge):
    spans = -(-nblocks * LANES // SPAN)
    return nblocks * rows + spans * (rows // GROUP_Y) + (nblocks * TILE if with_edge else 0)


def raw_half(upper, lw_ref, inno_hbm, back_hbm, inno_buf, back_buf, sems, raw_ref, msgs, cut, edge, extra):
    levels, half, width = inno_buf.shape
    rows, deep = 2 * half, half + TILE
    nblocks = width // LANES
    start = jnp.where(upper, 0, half)
    from_row = jnp.where(upper, 0, rows - deep)
    part = width // QUARTERS
    copies = []
    for q in range(QUARTERS):
        cols = pl.ds(q * part, part)
        copies.append(
            [
                pltpu.make_async_copy(
                    back_hbm.at[:, pl.ds(pl.multiple_of(from_row, TILE), deep), cols],
                    back_buf.at[:, :, cols],
                    sems.at[0, q],
                ),
                pltpu.make_async_copy(
                    inno_hbm.at[:, pl.ds(pl.multiple_of(start, TILE), half), cols],
                    inno_buf.at[:, :, cols],
                    sems.at[1, q],
                ),
            ]
        )
    for pair in copies:
        for copy in pair:
            copy.start()
    off = iota((half, deep), 1) - iota((half, deep), 0) + jnp.where(upper, 0, half - deep)
    diff_y = (jnp.where(off == 1, 1.0, 0.0) - jnp.where(off == -1, 1.0, 0.0)).astype(BF16)
    off = iota((4 * LANES, 2 * LANES), 0) - LANES - iota((4 * LANES, 2 * LANES), 1)
    diff_x = (jnp.where(off == 1, 1.0, 0.0) - jnp.where(off == -1, 1.0, 0.0)).astype(BF16)
    shape = (SPAN, LANES)
    sum_x = one_hot(iota(shape, 0) // GROUP_X == iota(shape, 1))
    shape = (rows // GROUP_Y, rows)
    sum_y = one_hot(iota(shape, 1) // GROUP_Y == iota(shape, 0))
    keep = iota((half, 2 * LANES), 0) != cut
    inner = half // TILE * TILE - (deep - half)
    waited = 0
    block = 0
    for msg_ref, per, with_edge in msgs:
        base = per * rows
        spans = -(-per * LANES // SPAN)
        total = None
        for k in range(0, per, 2):
            first = block + k
            low, high, top, bottom = window(first, nblocks)
            while waited * part < high * LANES:
                for copy in copies[waited]:
                    copy.wait()
                waited += 1
            here = pl.ds(first * LANES, 2 * LANES)
            around = back_buf[:, :, low * LANES : high * LANES]
            around = jnp.where(upper, around[:, :half], around[:, deep - half :])
            grad_xs = dot(around.reshape(levels * half, -1), diff_x[top:bottom])
            numer_y = numer_x = 0.0
            denom = 1.0
            for level in range(levels):
                weight = lw_ref[level]
                grad_y = dot(diff_y, back_buf[level, :, here])
                if extra is not None:
                    grad_y += extra(level, here)
                grad_x = grad_xs[level * half : (level + 1) * half]
                scaled = inno_buf[level, :, here].astype(F32) * (0.5 * weight)
                numer_y += scaled * grad_y
                numer_x += scaled * grad_x
                denom += (0.25 * weight) * (grad_y * grad_y + grad_x * grad_x)
            inverse = 1.0 / denom
            lows = []
            for comp, numer in enumerate((numer_y, numer_x)):
                raw = jnp.where(keep, numer * inverse, 0.0) if with_edge else numer * inverse
                upto, rest = split(raw)
                lows.append(rest)
                for j in range(2):
                    cols = slice(j * LANES, (j + 1) * LANES)
                    raw_ref[first + j, pl.ds(pl.multiple_of(comp * rows + start, 8), half), :] = raw[:, cols]
                    msg_ref[pl.ds((k + j) * rows + comp * half, half), :] = upto[:, cols]
            place = k * LANES % SPAN
            part_sum = dot(jnp.concatenate(lows, axis=0), sum_x[place : place + 2 * LANES])
            total = part_sum if place == 0 else total + part_sum
            if place + 2 * LANES == SPAN or k + 2 == per:
                at = base + k * LANES // SPAN * (rows // GROUP_Y)
                msg_ref[pl.ds(at, rows // GROUP_Y), :] = dot(sum_y, total.astype(BF16)).astype(BF16)
            if with_edge:
                tile = edge(here)
                for j in range(2):
                    at = base + spans * (rows // GROUP_Y) + (k + j) * TILE
                    msg_ref[pl.ds(at, TILE), :] = tile[:, j * LANES : (j + 1) * LANES]
        block += per


def outer_kernel(lw_ref, inno_hbm, back_hbm, raw_ref, msg_ref, inno_buf, back_buf, sems):
    levels, half, width = inno_buf.shape
    deep = half + TILE
    par = parity()
    upper = par == 0
    shape = (TILE, levels * TILE)
    kind, level = iota(shape, 0) // levels, iota(shape, 0) % levels
    at = iota(shape, 1) - level * TILE
    outermost = jnp.where(upper, 0, TILE - 1)
    next_row = jnp.where(upper, 1, TILE - 2)
    of_back = one_hot(((kind == 0) & (at == outermost)) | ((kind == 1) & (at == next_row)))
    of_inno = one_hot((kind == 2) & (at == outermost))

    def edge(here):
        back = jnp.where(upper, back_buf[:, :TILE, here], back_buf[:, deep - TILE :, here])
        inno = jnp.where(upper, inno_buf[:, :TILE, here], inno_buf[:, half - TILE :, here])
        tile = dot(of_back, back.reshape(levels * TILE, -1)) + dot(of_inno, inno.reshape(levels * TILE, -1))
        return tile.astype(BF16)

    cut = jnp.where(upper, 0, half - 1)
    msgs = [(msg_ref, width // LANES, True)]
    raw_half(upper, lw_ref, inno_hbm, back_hbm, inno_buf, back_buf, sems, raw_ref, msgs, cut, edge, None)


def edge_kernel(back_hbm, raw_hbm, out_ref, buf, sem):
    levels, _, _ = buf.shape
    rows = back_hbm.shape[1]
    upper = parity() == 1
    at = pl.multiple_of(jnp.where(upper, 0, rows - TILE), TILE)
    copy = pltpu.make_async_copy(back_hbm.at[:, pl.ds(at, TILE), :], buf, sem)
    copy.start()
    shape = (TILE, levels * TILE)
    row = jnp.where(upper, 0, TILE - 1)
    pick = one_hot(iota(shape, 1) == iota(shape, 0) * TILE + row)
    copy.wait()
    out_ref[...] = dot(pick, buf[...].reshape(levels * TILE, -1)).astype(BF16)


def inner_kernel(lw_ref, inno_hbm, back_hbm, row_ref, raw_in, raw_ref, *refs):
    *msg_refs, inno_buf, back_buf, sems = refs
    levels, half, width = inno_buf.shape
    upper = parity() == 1
    at = iota((half, 2 * LANES), 0) == jnp.where(upper, 0, half - 1)
    sign = jnp.where(upper, -1.0, 1.0)

    def extra(level, here):
        return jnp.where(at, row_ref[level : level + 1, here].astype(F32) * sign, 0.0)

    msgs = [(ref, ref.shape[0] // (2 * half), False) for ref in msg_refs]
    raw_half(upper, lw_ref, inno_hbm, back_hbm, inno_buf, back_buf, sems, raw_ref, msgs, -1, None, extra)


def far_row_kernel(lw_ref, own_ref, got_ref, raw_in, raw_ref, far_ref):
    nblocks, both, _ = raw_ref.shape
    rows = both // 2
    levels = lw_ref.shape[0]
    base = own_ref.shape[0] - nblocks * TILE
    sign = jnp.where(parity() == 0, -1.0, 1.0)
    own = jnp.concatenate([own_ref[pl.ds(base + k * TILE, TILE), :] for k in range(nblocks)], axis=1)
    got = jnp.concatenate([got_ref[pl.ds(base + k * TILE, TILE), :] for k in range(nblocks)], axis=1)
    own, got = own.astype(F32), got.astype(F32)
    lane = iota((levels, nblocks * LANES), 1)

    def raw_row(mine, beyond, sign):
        here = mine[:levels]
        grad_y = (beyond[:levels] - mine[levels : 2 * levels]) * sign
        left = jnp.where(lane == 0, 0.0, pltpu.roll(here, 1, 1))
        right = jnp.where(lane == nblocks * LANES - 1, 0.0, pltpu.roll(here, nblocks * LANES - 1, 1))
        grad_x = right - left
        inno = mine[2 * levels : 3 * levels]
        numer_y = numer_x = 0.0
        denom = 1.0
        for level in range(levels):
            weight = lw_ref[level]
            one = slice(level, level + 1)
            scaled = inno[one] * (0.5 * weight)
            numer_y += scaled * grad_y[one]
            numer_x += scaled * grad_x[one]
            denom += (0.25 * weight) * (grad_y[one] * grad_y[one] + grad_x[one] * grad_x[one])
        return numer_y / denom, numer_x / denom

    first = parity() == 0
    for comp, row in enumerate(raw_row(own, got, sign)):
        for k in range(nblocks):
            for y, here in ((0, first), (rows - 1, jnp.logical_not(first))):
                at = pl.ds(comp * rows + y, 1)
                raw_ref[k, at, :] = jnp.where(here, row[:, k * LANES : (k + 1) * LANES], raw_ref[k, at, :])
    for comp, row in enumerate(raw_row(got, own, -sign)):
        far_ref[comp : comp + 1, :] = row


def far_taps(rows, part):
    side = 2 * parity() - 1
    half = rows // 2
    start = jnp.where(part == 0, jnp.where(side < 0, half, 0), jnp.where(side < 0, 0, half))
    return taps(iota((rows, half), 1) + start - iota((rows, half), 0) + side * rows)


def spread_rest(values, msg_ref, nblocks):
    rows = values.shape[0]
    half = rows // 2
    shape = (half, half // GROUP_Y)
    mean_y = one_hot(iota(shape, 0) // GROUP_Y == iota(shape, 1), 1.0 / GROUP_Y)
    group_taps = dot(values.astype(BF16), mean_y).astype(BF16)
    spans = -(-nblocks * LANES // SPAN)
    found = []
    for span in range(spans):
        at = nblocks * rows + span * (rows // GROUP_Y)
        tile = msg_ref[pl.ds(at, rows // GROUP_Y), :]
        groups = half // GROUP_Y
        found.append(jnp.concatenate([dot(group_taps, tile[:groups]), dot(group_taps, tile[groups:])], axis=0).astype(BF16))
    return found


def mean_over_x():
    shape = (LANES, SPAN)
    return one_hot(iota(shape, 1) // GROUP_X == iota(shape, 0), 1.0 / GROUP_X)


def far_part(two, rest, mean_x, msg_ref, k, rows):
    half = rows // 2
    place = k * LANES % SPAN
    spread = dot(rest[k * LANES // SPAN], mean_x[:, place : place + 2 * LANES])
    parts = []
    for comp in range(2):
        got = [msg_ref[pl.ds((k + j) * rows + comp * half, half), :] for j in range(2)]
        part = dot(two, jnp.concatenate(got, axis=1))
        parts.append(part[:rows] + part[rows:] + spread[comp * rows : (comp + 1) * rows])
    return parts


def near_kernel(raw_ref, near_ref, far_ref, msg_ref, out_ref):
    nblocks, both, _ = raw_ref.shape
    rows = both // 2
    par = parity()
    side = 1 - 2 * par
    offset = iota((rows, rows), 1) - iota((rows, rows), 0)
    high, low = split(jnp.concatenate([taps(offset), taps(offset + side * rows)], axis=1))
    two = jnp.concatenate([high, low], axis=0)
    values = far_taps(rows, 0)
    two_far = jnp.concatenate(split(values), axis=0)
    rest = spread_rest(values, msg_ref, nblocks)
    mean_x = mean_over_x()
    column = iota((rows, 2 * LANES), 0)
    edge_taps = taps(jnp.where(par == 0, -1, rows) - column)
    for first in range(0, nblocks, 2):
        added = far_part(two_far, rest, mean_x, msg_ref, first, rows)
        for comp in range(2):
            here = pl.ds(comp * rows, rows)
            pairs = []
            for k in (first, first + 1):
                pairs.append(jnp.concatenate([raw_ref[k, here, :], near_ref[k, here, :]], axis=0))
            high_x, low_x = split(jnp.concatenate(pairs, axis=1))
            part = dot(two, high_x)
            part = part[:rows] + part[rows:] + dot(high, low_x) + added[comp]
            part += edge_taps * far_ref[comp : comp + 1, pl.ds(first * LANES, 2 * LANES)]
            for j in range(2):
                out_ref[first + j, here, :] = part[:, j * LANES : (j + 1) * LANES]


def finish(band_ref, part_ref, msg_ref, total_ref, out_hbm, high_ref, low_ref, buf, sem, begin, per, firsts):
    nblocks, both, _ = part_ref.shape
    rows = both // 2
    values = far_taps(rows, 1)
    two = jnp.concatenate(split(values), axis=0)
    rest = spread_rest(values, msg_ref, per)
    mean_x = mean_over_x()
    for k in range(begin - 3 if begin else 0, begin):
        high_ref[k], low_ref[k] = split(part_ref[k])
    copies = []
    ready = begin
    for first in firsts:
        low, high, top, bottom = window(first, nblocks)
        while ready < high:
            added = far_part(two, rest, mean_x, msg_ref, ready - begin, rows)
            for comp in range(2):
                here = pl.ds(comp * rows, rows)
                for j in range(2):
                    total = part_ref[ready + j, here, :] + added[comp][:, j * LANES : (j + 1) * LANES]
                    if total_ref is not None and ready + j >= begin + per - 3:
                        total_ref[ready + j, here, :] = total
                    high_ref[ready + j, here, :], low_ref[ready + j, here, :] = split(total)
            ready += 2
        upper = jnp.concatenate([high_ref[k] for k in range(low, high)], axis=1)
        lower = jnp.concatenate([low_ref[k] for k in range(low, high)], axis=1)
        band = band_ref[0, top:bottom, :]
        result = dot(upper, band) + dot(lower, band) + dot(upper, band_ref[1, top:bottom, :])
        here = pl.ds(first * LANES, 2 * LANES)
        buf[0, :, here] = result[:rows]
        buf[1, :, here] = result[rows:]
        copy = pltpu.make_async_copy(buf.at[:, :, here], out_hbm.at[:, :, here], sem.at[first // 2])
        copy.start()
        copies.append(copy)
    for copy in copies:
        copy.wait()


def first_kernel(band_ref, part_ref, msg_ref, out_hbm, total_ref, high_ref, low_ref, buf, sem):
    per = msg_ref.shape[0] // part_ref.shape[1] * 2
    per = blocks_of(msg_ref.shape[0], part_ref.shape[1] // 2)
    firsts = range(0, per - 2, 2)
    finish(band_ref, part_ref, msg_ref, total_ref, out_hbm, high_ref, low_ref, buf, sem, 0, per, firsts)


def last_kernel(band_ref, part_ref, msg_ref, out_in, out_hbm, high_ref, low_ref, buf, sem):
    nblocks = part_ref.shape[0]
    per = blocks_of(msg_ref.shape[0], part_ref.shape[1] // 2)
    begin = nblocks - per
    firsts = range(begin - 2, nblocks, 2)
    finish(band_ref, part_ref, msg_ref, None, out_hbm, high_ref, low_ref, buf, sem, begin, per, firsts)


def blocks_of(size, rows):
    return next(k for k in range(2, size, 2) if message_rows(rows, k, False) == size)


def body(innovation, background, level_weight):
    levels, rows, width = innovation.shape
    if rows != HALF or width % (4 * SPAN // 2) or 3 * levels > TILE:
        raise NotImplementedError("slab shape")
    nblocks = width // LANES
    both, half = 2 * rows, rows // 2
    count = lax.axis_size("row")
    chip = [(i, i ^ 1) for i in range(count) if i ^ 1 < count]
    away = [(i, j) for i in range(count) for j in [((i + 1) ^ 1) - 1] if 0 <= j < count]
    blocks = jax.ShapeDtypeStruct((nblocks, both, LANES), F32)
    per = nblocks * 5 // 16 * 2
    pers = [per, nblocks - per]

    def message(nblocks, with_edge):
        return jax.ShapeDtypeStruct((message_rows(rows, nblocks, with_edge), LANES), BF16)

    scratch = [
        pltpu.VMEM((levels, half, width), BF16),
        pltpu.VMEM((levels, half + TILE, width), BF16),
        pltpu.SemaphoreType.DMA((2, QUARTERS)),
    ]
    raw, outer = pl.pallas_call(
        outer_kernel,
        out_shape=[blocks, message(nblocks, True)],
        in_specs=[SMEM, ANY, ANY],
        out_specs=[VMEM, VMEM],
        scratch_shapes=scratch,
        compiler_params=PARAMS,
        name="outer_half",
    )(level_weight, innovation, background)
    outer_got = lax.ppermute(outer, "row", away)
    edge = pl.pallas_call(
        edge_kernel,
        out_shape=jax.ShapeDtypeStruct((TILE, width), BF16),
        in_specs=[ANY, ANY],
        out_specs=VMEM,
        scratch_shapes=[pltpu.VMEM((levels, TILE, width), BF16), pltpu.SemaphoreType.DMA],
        compiler_params=PARAMS,
        name="edge_row",
    )(background, raw)
    edge = lax.ppermute(edge, "row", chip)
    raw, *msgs = pl.pallas_call(
        inner_kernel,
        out_shape=[blocks] + [message(k, False) for k in pers],
        in_specs=[SMEM, ANY, ANY, VMEM, VMEM],
        out_specs=[VMEM] * 3,
        scratch_shapes=scratch,
        input_output_aliases={4: 0},
        compiler_params=PARAMS,
        name="inner_half",
    )(level_weight, innovation, background, edge, raw)
    msgs = [lax.ppermute(m, "row", away) for m in msgs]
    raw, far = pl.pallas_call(
        far_row_kernel,
        out_shape=[blocks, jax.ShapeDtypeStruct((8, width), F32)],
        in_specs=[SMEM] + [VMEM] * 3,
        out_specs=[VMEM] * 2,
        input_output_aliases={3: 0},
        compiler_params=PARAMS,
        name="far_row",
    )(level_weight, outer, outer_got, raw)
    near = lax.ppermute(raw, "row", chip)
    part = pl.pallas_call(
        near_kernel,
        out_shape=blocks,
        in_specs=[VMEM] * 4,
        out_specs=VMEM,
        compiler_params=PARAMS,
        name="near_part",
    )(raw, near, far, outer_got)
    band = jnp.asarray(zonal_band())
    scratch = [
        pltpu.VMEM((nblocks, both, LANES), BF16),
        pltpu.VMEM((nblocks, both, LANES), BF16),
        pltpu.VMEM((2, rows, width), F32),
        pltpu.SemaphoreType.DMA((nblocks // 2,)),
    ]
    result = jax.ShapeDtypeStruct((2, rows, width), F32)
    out, part = pl.pallas_call(
        first_kernel,
        out_shape=[result, blocks],
        in_specs=[VMEM] * 3,
        out_specs=[ANY, VMEM],
        scratch_shapes=scratch,
        input_output_aliases={1: 1},
        compiler_params=PARAMS,
        name="first_columns",
    )(band, part, msgs[0])
    return pl.pallas_call(
        last_kernel,
        out_shape=result,
        in_specs=[VMEM] * 3 + [ANY],
        out_specs=ANY,
        scratch_shapes=scratch,
        input_output_aliases={3: 0},
        compiler_params=PARAMS,
        name="last_columns",
    )(band, part, msgs[1], out)


def solution(mesh):
    placed = (P("member", "row", None), P("member", "row", None), P())
    return jax.shard_map(
        body, mesh=mesh, in_specs=placed, out_specs=P("member", "row", None), check_vma=False
    )
```

```python
import math

import jax
import jax.numpy as jnp
import numpy as np
from jax import lax
from jax.experimental import pallas as pl
from jax.experimental.pallas import tpu as pltpu
from jax.sharding import PartitionSpec as P

HALF = 64
SIGMA = 64
LANES = 128
GROUP_Y = 4
GROUP_X = 8
SPAN = LANES * GROUP_X
TILE = 16
QUARTERS = 4
PIECES = 4
F32 = jnp.float32
BF16 = jnp.bfloat16
NORM = math.sqrt(sum(math.exp(-k * k / (SIGMA * SIGMA)) for k in range(-HALF, HALF + 1)))

VMEM = pl.BlockSpec(memory_space=pltpu.VMEM)
SMEM = pl.BlockSpec(memory_space=pltpu.SMEM)
HBM = pl.BlockSpec(memory_space=pltpu.HBM)
PARAMS = pltpu.CompilerParams(vmem_limit_bytes=40 * 1024 * 1024)


def split(values):
    high = values.astype(BF16)
    return high, (values - high.astype(F32)).astype(BF16)


def dot(left, right):
    return jnp.dot(left, right, preferred_element_type=F32)


def iota(shape, dim):
    return lax.broadcasted_iota(jnp.int32, shape, dim)


def one_hot(mask, value=1.0):
    return jnp.where(mask, value, 0.0).astype(BF16)


def taps(offset):
    off = offset.astype(F32)
    value = jnp.exp(off * off * (-0.5 / (SIGMA * SIGMA))) * (1.0 / NORM)
    return jnp.where(jnp.abs(offset) <= HALF, value, 0.0)


def zonal_band():
    offset = np.arange(4 * LANES)[:, None] - LANES - np.arange(2 * LANES)[None, :]
    band = np.exp(-offset * offset / (2.0 * SIGMA * SIGMA)) / NORM
    band = np.where(np.abs(offset) <= HALF, band, 0.0).astype(np.float32)
    high = band.astype(BF16)
    return np.stack([high, (band - high.astype(np.float32)).astype(BF16)])


def window(first, nblocks):
    low, high = max(first - 1, 0), min(first + 3, nblocks)
    return low, high, (low - first + 1) * LANES, (high - first + 1) * LANES


def parity():
    return lax.rem(lax.axis_index("row"), 2)


def message_rows(rows, nblocks, with_edge):
    spans = -(-nblocks * LANES // SPAN)
    return nblocks * rows + spans * (rows // GROUP_Y) + (nblocks * TILE if with_edge else 0)


def block_of(refs, k):
    per = refs[0].shape[0]
    return refs[k // per].at[k % per]


def raw_half(upper, lw_hbm, inno_hbm, back_hbm, lw_ref, inno_buf, back_buf, sems, lw_sem, raw_refs, msgs, cut, edge, extra):
    levels, half, width = inno_buf.shape
    rows, deep = 2 * half, half + TILE
    nblocks = width // LANES
    start = jnp.where(upper, 0, half)
    from_row = jnp.where(upper, 0, rows - deep)
    part = width // QUARTERS
    copies = []
    for q in range(QUARTERS):
        cols = pl.ds(q * part, part)
        copies.append(
            [
                pltpu.make_async_copy(
                    back_hbm.at[:, pl.ds(pl.multiple_of(from_row, TILE), deep), cols],
                    back_buf.at[:, :, cols],
                    sems.at[0, q],
                ),
                pltpu.make_async_copy(
                    inno_hbm.at[:, pl.ds(pl.multiple_of(start, TILE), half), cols],
                    inno_buf.at[:, :, cols],
                    sems.at[1, q],
                ),
            ]
        )
    weights = pltpu.make_async_copy(lw_hbm, lw_ref, lw_sem)
    weights.start()
    for pair in copies:
        for copy in pair:
            copy.start()
    off = iota((half, deep), 1) - iota((half, deep), 0) + jnp.where(upper, 0, half - deep)
    diff_y = (jnp.where(off == 1, 1.0, 0.0) - jnp.where(off == -1, 1.0, 0.0)).astype(BF16)
    off = iota((4 * LANES, 2 * LANES), 0) - LANES - iota((4 * LANES, 2 * LANES), 1)
    diff_x = (jnp.where(off == 1, 1.0, 0.0) - jnp.where(off == -1, 1.0, 0.0)).astype(BF16)
    shape = (SPAN, LANES)
    sum_x = one_hot(iota(shape, 0) // GROUP_X == iota(shape, 1))
    shape = (rows // GROUP_Y, rows)
    sum_y = one_hot(iota(shape, 1) // GROUP_Y == iota(shape, 0))
    keep = iota((half, 2 * LANES), 0) != cut
    weights.wait()
    waited = 0
    block = 0
    for msg_ref, per, with_edge in msgs:
        base = per * rows
        spans = -(-per * LANES // SPAN)
        total = None
        for k in range(0, per, 2):
            first = block + k
            low, high, top, bottom = window(first, nblocks)
            while waited * part < high * LANES:
                for copy in copies[waited]:
                    copy.wait()
                waited += 1
            here = pl.ds(first * LANES, 2 * LANES)
            skip = pl.multiple_of(jnp.where(upper, 0, deep - half), TILE)
            around = back_buf[:, pl.ds(skip, half), low * LANES : high * LANES]
            grad_xs = dot(around.reshape(levels * half, -1), diff_x[top:bottom])
            numer_y = numer_x = 0.0
            denom = 1.0
            for level in range(levels):
                weight = lw_ref[level]
                grad_y = dot(diff_y, back_buf[level, :, here])
                if extra is not None:
                    grad_y += extra(level, here)
                grad_x = grad_xs[level * half : (level + 1) * half]
                scaled = inno_buf[level, :, here].astype(F32) * (0.5 * weight)
                numer_y += scaled * grad_y
                numer_x += scaled * grad_x
                denom += (0.25 * weight) * (grad_y * grad_y + grad_x * grad_x)
            inverse = 1.0 / denom
            lows = []
            for comp, numer in enumerate((numer_y, numer_x)):
                raw = jnp.where(keep, numer * inverse, 0.0) if with_edge else numer * inverse
                upto, rest = split(raw)
                lows.append(rest)
                for j in range(2):
                    cols = slice(j * LANES, (j + 1) * LANES)
                    at = pl.ds(pl.multiple_of(comp * rows + start, 8), half)
                    block_of(raw_refs, first + j)[at, :] = raw[:, cols]
                    msg_ref[pl.ds((k + j) * rows + comp * half, half), :] = upto[:, cols]
            place = k * LANES % SPAN
            part_sum = dot(jnp.concatenate(lows, axis=0), sum_x[place : place + 2 * LANES])
            total = part_sum if place == 0 else total + part_sum
            if place + 2 * LANES == SPAN or k + 2 == per:
                at = base + k * LANES // SPAN * (rows // GROUP_Y)
                msg_ref[pl.ds(at, rows // GROUP_Y), :] = dot(sum_y, total.astype(BF16)).astype(BF16)
            if with_edge:
                tile = edge(here)
                for j in range(2):
                    at = base + spans * (rows // GROUP_Y) + (k + j) * TILE
                    msg_ref[pl.ds(at, TILE), :] = tile[:, j * LANES : (j + 1) * LANES]
        block += per


def outer_kernel(lw_hbm, inno_hbm, back_hbm, *refs):
    *raw_refs, msg_ref, lw_ref, inno_buf, back_buf, sems, lw_sem = refs
    levels, half, width = inno_buf.shape
    deep = half + TILE
    par = parity()
    upper = par == 0
    shape = (TILE, levels * TILE)
    kind, level = iota(shape, 0) // levels, iota(shape, 0) % levels
    at = iota(shape, 1) - level * TILE
    outermost = jnp.where(upper, 0, TILE - 1)
    next_row = jnp.where(upper, 1, TILE - 2)
    of_back = one_hot(((kind == 0) & (at == outermost)) | ((kind == 1) & (at == next_row)))
    of_inno = one_hot((kind == 2) & (at == outermost))

    def edge(here):
        back = back_buf[:, pl.ds(pl.multiple_of(jnp.where(upper, 0, deep - TILE), TILE), TILE), here]
        inno = inno_buf[:, pl.ds(pl.multiple_of(jnp.where(upper, 0, half - TILE), TILE), TILE), here]
        tile = dot(of_back, back.reshape(levels * TILE, -1)) + dot(of_inno, inno.reshape(levels * TILE, -1))
        return tile.astype(BF16)

    cut = jnp.where(upper, 0, half - 1)
    msgs = [(msg_ref, width // LANES, True)]
    raw_half(upper, lw_hbm, inno_hbm, back_hbm, lw_ref, inno_buf, back_buf, sems, lw_sem, raw_refs, msgs, cut, edge, None)


def edge_kernel(back_hbm, raw_hbm, out_ref, buf, sem):
    levels, _, _ = buf.shape
    rows = back_hbm.shape[1]
    upper = parity() == 1
    at = pl.multiple_of(jnp.where(upper, 0, rows - TILE), TILE)
    copy = pltpu.make_async_copy(back_hbm.at[:, pl.ds(at, TILE), :], buf, sem)
    copy.start()
    shape = (TILE, levels * TILE)
    row = jnp.where(upper, 0, TILE - 1)
    pick = one_hot(iota(shape, 1) == iota(shape, 0) * TILE + row)
    copy.wait()
    out_ref[...] = dot(pick, buf[...].reshape(levels * TILE, -1)).astype(BF16)


def inner_kernel(lw_hbm, inno_hbm, back_hbm, row_ref, *refs):
    raw_refs = refs[PIECES : 2 * PIECES]
    *msg_refs, lw_ref, inno_buf, back_buf, sems, lw_sem = refs[2 * PIECES :]
    levels, half, width = inno_buf.shape
    upper = parity() == 1
    at = iota((half, 2 * LANES), 0) == jnp.where(upper, 0, half - 1)
    sign = jnp.where(upper, -1.0, 1.0)

    def extra(level, here):
        return jnp.where(at, row_ref[level : level + 1, here].astype(F32) * sign, 0.0)

    msgs = [(ref, ref.shape[0] // (2 * half), False) for ref in msg_refs]
    raw_half(upper, lw_hbm, inno_hbm, back_hbm, lw_ref, inno_buf, back_buf, sems, lw_sem, raw_refs, msgs, -1, None, extra)


def far_row_kernel(lw_ref, own_ref, got_ref, out_ref):
    nblocks = out_ref.shape[1] // LANES
    levels = lw_ref.shape[0]
    base = own_ref.shape[0] - nblocks * TILE
    sign = jnp.where(parity() == 0, -1.0, 1.0)
    own = jnp.concatenate([own_ref[pl.ds(base + k * TILE, TILE), :] for k in range(nblocks)], axis=1)
    got = jnp.concatenate([got_ref[pl.ds(base + k * TILE, TILE), :] for k in range(nblocks)], axis=1)
    own, got = own.astype(F32), got.astype(F32)
    lane = iota((levels, nblocks * LANES), 1)

    def raw_row(mine, beyond, sign):
        here = mine[:levels]
        grad_y = (beyond[:levels] - mine[levels : 2 * levels]) * sign
        left = jnp.where(lane == 0, 0.0, pltpu.roll(here, 1, 1))
        right = jnp.where(lane == nblocks * LANES - 1, 0.0, pltpu.roll(here, nblocks * LANES - 1, 1))
        grad_x = right - left
        inno = mine[2 * levels : 3 * levels]
        numer_y = numer_x = 0.0
        denom = 1.0
        for level in range(levels):
            weight = lw_ref[level]
            one = slice(level, level + 1)
            scaled = inno[one] * (0.5 * weight)
            numer_y += scaled * grad_y[one]
            numer_x += scaled * grad_x[one]
            denom += (0.25 * weight) * (grad_y[one] * grad_y[one] + grad_x[one] * grad_x[one])
        return numer_y / denom, numer_x / denom

    rows = (*raw_row(own, got, sign), *raw_row(got, own, -sign))
    for index, row in enumerate(rows):
        out_ref[index : index + 1, :] = row


def far_taps(rows, part):
    side = 2 * parity() - 1
    half = rows // 2
    start = jnp.where(part == 0, jnp.where(side < 0, half, 0), jnp.where(side < 0, 0, half))
    return taps(iota((rows, half), 1) + start - iota((rows, half), 0) + side * rows)


def spread_rest(values, msg_ref, nblocks):
    rows = values.shape[0]
    half = rows // 2
    shape = (half, half // GROUP_Y)
    mean_y = one_hot(iota(shape, 0) // GROUP_Y == iota(shape, 1), 1.0 / GROUP_Y)
    group_taps = dot(values.astype(BF16), mean_y).astype(BF16)
    spans = -(-nblocks * LANES // SPAN)
    found = []
    for span in range(spans):
        at = nblocks * rows + span * (rows // GROUP_Y)
        tile = msg_ref[pl.ds(at, rows // GROUP_Y), :]
        groups = half // GROUP_Y
        found.append(jnp.concatenate([dot(group_taps, tile[:groups]), dot(group_taps, tile[groups:])], axis=0).astype(BF16))
    return found


def mean_over_x():
    shape = (LANES, SPAN)
    return one_hot(iota(shape, 1) // GROUP_X == iota(shape, 0), 1.0 / GROUP_X)


def far_part(two, rest, mean_x, msg_ref, k, rows):
    half = rows // 2
    place = k * LANES % SPAN
    spread = dot(rest[k * LANES // SPAN], mean_x[:, place : place + 2 * LANES])
    parts = []
    for comp in range(2):
        got = [msg_ref[pl.ds((k + j) * rows + comp * half, half), :] for j in range(2)]
        part = dot(two, jnp.concatenate(got, axis=1))
        parts.append(part[:rows] + part[rows:] + spread[comp * rows : (comp + 1) * rows])
    return parts


def near_kernel(*refs):
    raw_refs, near_refs = refs[:PIECES], refs[PIECES : 2 * PIECES]
    edges_ref, msg_ref, out_ref = refs[2 * PIECES :]
    nblocks, both, _ = out_ref.shape
    rows = both // 2
    par = parity()
    side = 1 - 2 * par
    offset = iota((rows, rows), 1) - iota((rows, rows), 0)
    high, low = split(jnp.concatenate([taps(offset), taps(offset + side * rows)], axis=1))
    two = jnp.concatenate([high, low], axis=0)
    values = far_taps(rows, 0)
    two_far = jnp.concatenate(split(values), axis=0)
    rest = spread_rest(values, msg_ref, nblocks)
    mean_x = mean_over_x()
    column = iota((rows, 2 * LANES), 0)
    own_taps = taps(jnp.where(par == 0, 0, rows - 1) - column)
    edge_taps = taps(jnp.where(par == 0, -1, rows) - column)
    for first in range(0, nblocks, 2):
        added = far_part(two_far, rest, mean_x, msg_ref, first, rows)
        for comp in range(2):
            here = pl.ds(comp * rows, rows)
            pairs = []
            for k in (first, first + 1):
                pairs.append(jnp.concatenate([block_of(raw_refs, k)[here, :], block_of(near_refs, k)[here, :]], axis=0))
            high_x, low_x = split(jnp.concatenate(pairs, axis=1))
            part = dot(two, high_x)
            part = part[:rows] + part[rows:] + dot(high, low_x) + added[comp]
            cols = pl.ds(first * LANES, 2 * LANES)
            part += own_taps * edges_ref[comp : comp + 1, cols] + edge_taps * edges_ref[2 + comp : 3 + comp, cols]
            for j in range(2):
                out_ref[first + j, here, :] = part[:, j * LANES : (j + 1) * LANES]


def finish(band_ref, part_ref, edges_ref, msg_ref, total_ref, out_hbm, high_ref, low_ref, buf, sem, begin, per, firsts):
    nblocks, both, _ = part_ref.shape
    rows = both // 2
    values = far_taps(rows, 1)
    two = jnp.concatenate(split(values), axis=0)
    rest = spread_rest(values, msg_ref, per)
    mean_x = mean_over_x()
    side = 1 - 2 * parity()
    edge = jnp.where(side > 0, 2 * rows - 1, -rows)
    edge_taps = taps(edge - iota((rows, LANES), 0))
    for k in range(begin - 3 if begin else 0, begin):
        high_ref[k], low_ref[k] = split(part_ref[k])
    copies = []
    ready = begin
    for first in firsts:
        low, high, top, bottom = window(first, nblocks)
        while ready < high:
            added = far_part(two, rest, mean_x, msg_ref, ready - begin, rows)
            for comp in range(2):
                here = pl.ds(comp * rows, rows)
                for j in range(2):
                    total = part_ref[ready + j, here, :] + added[comp][:, j * LANES : (j + 1) * LANES]
                    total += edge_taps * edges_ref[comp : comp + 1, pl.ds((ready + j) * LANES, LANES)]
                    if total_ref is not None and ready + j >= begin + per - 3:
                        total_ref[ready + j, here, :] = total
                    high_ref[ready + j, here, :], low_ref[ready + j, here, :] = split(total)
            ready += 2
        upper = jnp.concatenate([high_ref[k] for k in range(low, high)], axis=1)
        lower = jnp.concatenate([low_ref[k] for k in range(low, high)], axis=1)
        band = band_ref[0, top:bottom, :]
        result = dot(upper, band) + dot(lower, band) + dot(upper, band_ref[1, top:bottom, :])
        here = pl.ds(first * LANES, 2 * LANES)
        buf[0, :, here] = result[:rows]
        buf[1, :, here] = result[rows:]
        copy = pltpu.make_async_copy(buf.at[:, :, here], out_hbm.at[:, :, here], sem.at[first // 2])
        copy.start()
        copies.append(copy)
    for copy in copies:
        copy.wait()


def first_kernel(band_ref, part_ref, edges_ref, msg_ref, out_hbm, total_ref, high_ref, low_ref, buf, sem):
    per = blocks_of(msg_ref.shape[0], part_ref.shape[1] // 2)
    firsts = range(0, per - 2, 2)
    finish(band_ref, part_ref, edges_ref, msg_ref, total_ref, out_hbm, high_ref, low_ref, buf, sem, 0, per, firsts)


def last_kernel(band_ref, part_ref, edges_ref, msg_ref, out_in, out_hbm, high_ref, low_ref, buf, sem):
    nblocks = part_ref.shape[0]
    per = blocks_of(msg_ref.shape[0], part_ref.shape[1] // 2)
    begin = nblocks - per
    firsts = range(begin - 2, nblocks, 2)
    finish(band_ref, part_ref, edges_ref, msg_ref, None, out_hbm, high_ref, low_ref, buf, sem, begin, per, firsts)


def blocks_of(size, rows):
    return next(k for k in range(2, size, 2) if message_rows(rows, k, False) == size)


def body(innovation, background, level_weight):
    levels, rows, width = innovation.shape
    if rows != HALF or width % (4 * SPAN // 2) or 3 * levels > TILE:
        raise NotImplementedError("slab shape")
    nblocks = width // LANES
    both, half = 2 * rows, rows // 2
    count = lax.axis_size("row")
    chip = [(i, i ^ 1) for i in range(count) if i ^ 1 < count]
    away = [(i, j) for i in range(count) for j in [((i + 1) ^ 1) - 1] if 0 <= j < count]
    innovation = pltpu.with_memory_space_constraint(innovation, pltpu.HBM)
    background = pltpu.with_memory_space_constraint(background, pltpu.HBM)
    level_weight = pltpu.with_memory_space_constraint(level_weight, pltpu.HBM)
    blocks = jax.ShapeDtypeStruct((nblocks, both, LANES), F32)
    per = nblocks * 5 // 16 * 2
    pers = [per, nblocks - per]

    def message(nblocks, with_edge):
        return jax.ShapeDtypeStruct((message_rows(rows, nblocks, with_edge), LANES), BF16)

    scratch = [
        pltpu.SMEM((levels,), F32),
        pltpu.VMEM((levels, half, width), BF16),
        pltpu.VMEM((levels, half + TILE, width), BF16),
        pltpu.SemaphoreType.DMA((2, QUARTERS)),
        pltpu.SemaphoreType.DMA,
    ]
    piece = jax.ShapeDtypeStruct((nblocks // PIECES, both, LANES), F32)
    *raws, outer = pl.pallas_call(
        outer_kernel,
        out_shape=[piece] * PIECES + [message(nblocks, True)],
        in_specs=[HBM] * 3,
        out_specs=[VMEM] * (PIECES + 1),
        scratch_shapes=scratch,
        compiler_params=PARAMS,
        name="outer_half",
    )(level_weight, innovation, background)
    outer_got = lax.ppermute(outer, "row", away)
    edge = pl.pallas_call(
        edge_kernel,
        out_shape=jax.ShapeDtypeStruct((TILE, width), BF16),
        in_specs=[HBM, HBM],
        out_specs=VMEM,
        scratch_shapes=[pltpu.VMEM((levels, TILE, width), BF16), pltpu.SemaphoreType.DMA],
        compiler_params=PARAMS,
        name="edge_row",
    )(background, raws[0])
    edge = lax.ppermute(edge, "row", chip)
    found = pl.pallas_call(
        inner_kernel,
        out_shape=[piece] * PIECES + [message(k, False) for k in pers],
        in_specs=[HBM] * 3 + [VMEM] * (PIECES + 1),
        out_specs=[VMEM] * (PIECES + 2),
        scratch_shapes=scratch,
        input_output_aliases={4 + k: k for k in range(PIECES)},
        compiler_params=PARAMS,
        name="inner_half",
    )(level_weight, innovation, background, edge, *raws)
    raws = found[:PIECES]
    msgs = [lax.ppermute(m, "row", away) for m in found[PIECES:]]
    nears = [lax.ppermute(r, "row", chip) for r in raws]
    edges = pl.pallas_call(
        far_row_kernel,
        out_shape=jax.ShapeDtypeStruct((4, width), F32),
        in_specs=[SMEM] + [VMEM] * 2,
        out_specs=VMEM,
        compiler_params=PARAMS,
        name="outermost_rows",
    )(level_weight, outer, outer_got)
    edges_near = lax.ppermute(edges, "row", chip)
    part = pl.pallas_call(
        near_kernel,
        out_shape=blocks,
        in_specs=[VMEM] * (2 * PIECES + 2),
        out_specs=VMEM,
        compiler_params=PARAMS,
        name="near_part",
    )(*raws, *nears, edges, outer_got)
    band = jnp.asarray(zonal_band())
    scratch = [
        pltpu.VMEM((nblocks, both, LANES), BF16),
        pltpu.VMEM((nblocks, both, LANES), BF16),
        pltpu.VMEM((2, rows, width), F32),
        pltpu.SemaphoreType.DMA((nblocks // 2,)),
    ]
    result = jax.ShapeDtypeStruct((2, rows, width), F32)
    out, part = pl.pallas_call(
        first_kernel,
        out_shape=[result, blocks],
        in_specs=[VMEM] * 4,
        out_specs=[HBM, VMEM],
        scratch_shapes=scratch,
        input_output_aliases={1: 1},
        compiler_params=PARAMS,
        name="first_columns",
    )(band, part, edges_near, msgs[0])
    return pl.pallas_call(
        last_kernel,
        out_shape=result,
        in_specs=[VMEM] * 4 + [HBM],
        out_specs=HBM,
        scratch_shapes=scratch,
        input_output_aliases={4: 0},
        compiler_params=PARAMS,
        name="last_columns",
    )(band, part, edges_near, msgs[1], out)


def solution(mesh):
    placed = (P("member", "row", None), P("member", "row", None), P())
    return jax.shard_map(
        body, mesh=mesh, in_specs=placed, out_specs=P("member", "row", None), check_vma=False
    )
```

```python
import math

import jax
import jax.numpy as jnp
import numpy as np
from jax import lax
from jax.experimental import pallas as pl
from jax.experimental.pallas import tpu as pltpu
from jax.sharding import PartitionSpec as P

HALF = 64
SIGMA = 64
LANES = 128
TILE = 16
SHIFT_Y, SHIFT_X, SHIFT_Z = 2, 3, 4
SPAN = LANES << SHIFT_X
PACK = 4
QUARTERS = 4
PIECES = 4
F32 = jnp.float32
BF16 = jnp.bfloat16
NORM = math.sqrt(sum(math.exp(-k * k / (SIGMA * SIGMA)) for k in range(-HALF, HALF + 1)))

VMEM = pl.BlockSpec(memory_space=pltpu.VMEM)
SMEM = pl.BlockSpec(memory_space=pltpu.SMEM)
HBM = pl.BlockSpec(memory_space=pltpu.HBM)
PARAMS = pltpu.CompilerParams(vmem_limit_bytes=40 * 1024 * 1024)


def split(values):
    high = values.astype(BF16)
    return high, (values - high.astype(F32)).astype(BF16)


def dot(left, right):
    return jnp.dot(left, right, preferred_element_type=F32)


def iota(shape, dim):
    return lax.broadcasted_iota(jnp.int32, shape, dim)


def one_hot(mask, value=1.0):
    return jnp.where(mask, value, 0.0).astype(BF16)


def difference(off):
    return (jnp.where(off == 1, 1.0, 0.0) - jnp.where(off == -1, 1.0, 0.0)).astype(BF16)


def taps(offset):
    off = offset.astype(F32)
    value = jnp.exp(off * off * (-0.5 / (SIGMA * SIGMA))) * (1.0 / NORM)
    return jnp.where(jnp.abs(offset) <= HALF, value, 0.0)


def zonal_band():
    offset = np.arange(4 * LANES)[:, None] - LANES - np.arange(2 * LANES)[None, :]
    band = np.exp(-offset * offset / (2.0 * SIGMA * SIGMA)) / NORM
    band = np.where(np.abs(offset) <= HALF, band, 0.0).astype(np.float32)
    high = band.astype(BF16)
    return np.stack([high, (band - high.astype(np.float32)).astype(BF16)])


def window(first, nblocks):
    low, high = max(first - 1, 0), min(first + 3, nblocks)
    return low, high, (low - first + 1) * LANES, (high - first + 1) * LANES


def smooth_x(band_ref, high_ref, low_ref, first, nblocks):
    low, high, top, bottom = window(first, nblocks)
    upper = jnp.concatenate([high_ref[k] for k in range(low, high)], axis=1)
    lower = jnp.concatenate([low_ref[k] for k in range(low, high)], axis=1)
    band = band_ref[0, top:bottom, :]
    return dot(upper, band) + dot(lower, band) + dot(upper, band_ref[1, top:bottom, :])


def parity():
    return lax.rem(lax.axis_index("row"), 2)


def block_of(refs, k):
    per = refs[0].shape[0]
    return refs[k // per].at[k % per]


def tile_at(row):
    return pl.ds(pl.multiple_of(row, TILE), TILE)


def raw_pair(first, lw_ref, inno, back, diff_y, diff_x, extra):
    levels, half, width = inno.shape
    upper, back_ref, at = back
    here = pl.ds(first * LANES, 2 * LANES)
    low, high, top, bottom = window(first, width // LANES)
    deep = pl.ds(pl.multiple_of(at, TILE), half + TILE)
    exact = pl.ds(pl.multiple_of(at + jnp.where(upper, 0, TILE), TILE), half)
    around = back_ref[:, exact, low * LANES : high * LANES]
    grad_xs = dot(around.reshape(levels * half, -1), diff_x[top:bottom])
    numer_y = numer_x = 0.0
    denom = 1.0
    for level in range(levels):
        weight = lw_ref[level]
        grad_y = dot(diff_y, back_ref[level, deep, here])
        if extra is not None:
            grad_y += extra(level, here)
        grad_x = grad_xs[level * half : (level + 1) * half]
        scaled = inno[level, :, here].astype(F32) * (0.5 * weight)
        numer_y += scaled * grad_y
        numer_x += scaled * grad_x
        denom += (0.25 * weight) * (grad_y * grad_y + grad_x * grad_x)
    inverse = 1.0 / denom
    return numer_y * inverse, numer_x * inverse


def differences(upper, half):
    deep = half + TILE
    diff_y = difference(iota((half, deep), 1) - iota((half, deep), 0) - jnp.where(upper, 0, TILE))
    shape = (4 * LANES, 2 * LANES)
    return diff_y, difference(iota(shape, 0) - LANES - iota(shape, 1))


def outer_kernel(lw_hbm, inno_hbm, back_hbm, *refs):
    *raw_refs, msg_ref, row_ref, lw_ref, inno_buf, back_buf, low_ref, row_buf, sems, lw_sem, row_sem = refs
    levels, half, width = inno_buf.shape
    rows, deep = 2 * half, half + TILE
    nblocks = width // LANES
    upper = parity() == 0
    start = jnp.where(upper, 0, half)
    copies = []
    part = width // QUARTERS
    back_rows = pl.ds(pl.multiple_of(jnp.where(upper, 0, rows - deep), TILE), deep)
    inno_rows = pl.ds(pl.multiple_of(start, TILE), half)
    for q in range(QUARTERS):
        cols = pl.ds(q * part, part)
        copies.append(
            [
                pltpu.make_async_copy(back_hbm.at[:, back_rows, cols], back_buf.at[:, :, cols], sems.at[0, q]),
                pltpu.make_async_copy(inno_hbm.at[:, inno_rows, cols], inno_buf.at[:, :, cols], sems.at[1, q]),
            ]
        )
    weights = pltpu.make_async_copy(lw_hbm, lw_ref, lw_sem)
    near = pltpu.make_async_copy(back_hbm.at[:, tile_at(jnp.where(upper, rows - TILE, 0)), :], row_buf, row_sem)
    weights.start()
    for pair in copies:
        for copy in pair:
            copy.start()
    near.start()
    diff_y, diff_x = differences(upper, half)
    keep = iota((half, 2 * LANES), 0) != jnp.where(upper, 0, half - 1)
    weights.wait()
    waited = 0
    for first in range(0, nblocks, 2):
        while waited * part < window(first, nblocks)[1] * LANES:
            for copy in copies[waited]:
                copy.wait()
            waited += 1
        pair = raw_pair(first, lw_ref, inno_buf, (upper, back_buf, 0), diff_y, diff_x, None)
        for comp, raw in enumerate(pair):
            raw = jnp.where(keep, raw, 0.0)
            high, low = split(raw)
            low_ref[comp * half : (comp + 1) * half, first * LANES : (first + 2) * LANES] = low
            for j in range(2):
                cols = slice(j * LANES, (j + 1) * LANES)
                at = pl.ds(pl.multiple_of(comp * rows + start, 8), half)
                block_of(raw_refs, first + j)[at, :] = raw[:, cols]
                msg_ref[pl.ds((first + j) * rows + comp * half, half), :] = high[:, cols]
    shape = (SPAN, LANES)
    sum_x = one_hot(iota(shape, 0) >> SHIFT_X == iota(shape, 1))
    groups = rows >> SHIFT_Y
    shape = (groups, rows)
    sum_y = one_hot(iota(shape, 1) >> SHIFT_Y == iota(shape, 0))
    at = nblocks * rows
    for span in range(0, width, SPAN):
        total = dot(low_ref[:, span : span + SPAN], sum_x)
        msg_ref[pl.ds(at, groups), :] = dot(sum_y, total.astype(BF16)).astype(BF16)
        at += groups
    kinds = 3 * levels
    shape = (PACK * kinds, PACK * levels * TILE)
    row, col = iota(shape, 0), iota(shape, 1)
    want = row - (col >> 6) * kinds
    level = (col >> 4) & (levels - 1)
    place = col & (TILE - 1)
    outermost = place == jnp.where(upper, 0, TILE - 1)
    next_row = place == jnp.where(upper, 1, TILE - 2)
    of_back = one_hot(((want == level) & outermost) | ((want == levels + level) & next_row))
    of_inno = one_hot((want == 2 * levels + level) & outermost)
    back_at = tile_at(jnp.where(upper, 0, deep - TILE))
    inno_at = tile_at(jnp.where(upper, 0, half - TILE))
    for first in range(0, nblocks, PACK):
        back, inno = [], []
        for k in range(first, first + PACK):
            here = pl.ds(k * LANES, LANES)
            back.append(back_buf[:, back_at, here].reshape(levels * TILE, LANES))
            inno.append(inno_buf[:, inno_at, here].reshape(levels * TILE, LANES))
        tile = dot(of_back, jnp.concatenate(back, axis=0)) + dot(of_inno, jnp.concatenate(inno, axis=0))
        msg_ref[pl.ds(at, PACK * kinds), :] = tile.astype(BF16)
        at += PACK * kinds
    near.wait()
    shape = (TILE, levels * TILE)
    pick = one_hot(iota(shape, 1) == iota(shape, 0) * TILE + jnp.where(upper, TILE - 1, 0))
    row_ref[...] = dot(pick, row_buf[...].reshape(levels * TILE, -1)).astype(BF16)


def outer_rows(rows, nblocks, levels):
    return nblocks * rows + (nblocks * LANES // SPAN) * (rows >> SHIFT_Y) + nblocks * 3 * levels


def inner_kernel(lw_ref, inno_ref, back_ref, row_ref, band_ref, *refs):
    raw_refs = refs[PIECES : 2 * PIECES]
    msg_ref, high_ref, low_ref = refs[2 * PIECES :]
    levels, rows, width = inno_ref.shape
    half = rows // 2
    nblocks = width // LANES
    upper = parity() == 1
    start = jnp.where(upper, 0, half)
    diff_y, diff_x = differences(upper, half)
    at = iota((half, 2 * LANES), 0) == jnp.where(upper, 0, half - 1)
    sign = jnp.where(upper, -1.0, 1.0)

    def extra(level, here):
        return jnp.where(at, row_ref[level : level + 1, here].astype(F32) * sign, 0.0)

    inno = inno_ref.at[:, pl.ds(pl.multiple_of(start, TILE), half), :]
    back = (upper, back_ref, jnp.where(upper, 0, half - TILE))
    for first in range(0, nblocks, 2):
        pair = raw_pair(first, lw_ref, inno, back, diff_y, diff_x, extra)
        for comp, raw in enumerate(pair):
            high, low = split(raw)
            for j in range(2):
                cols = slice(j * LANES, (j + 1) * LANES)
                here = pl.ds(pl.multiple_of(comp * rows + start, 8), half)
                block_of(raw_refs, first + j)[here, :] = raw[:, cols]
                here = pl.ds(comp * half, half)
                high_ref[first + j, here, :], low_ref[first + j, here, :] = high[:, cols], low[:, cols]
    groups = rows >> SHIFT_Z
    shape = (2 * groups, rows)
    sum_y = one_hot(iota(shape, 1) >> SHIFT_Z == iota(shape, 0))
    sums = []
    for first in range(0, nblocks, 2):
        high, low = split(smooth_x(band_ref, high_ref, low_ref, first, nblocks))
        sums.append(dot(sum_y, low)[:groups])
        for j in range(2):
            msg_ref[pl.ds((first + j) * rows, rows), :] = high[:, j * LANES : (j + 1) * LANES]
    per = TILE // (2 * groups)
    for first in range(0, len(sums), per):
        parts = [s[:, j * LANES : (j + 1) * LANES] for j in range(2) for s in sums[first : first + per]]
        at = nblocks * rows + first // per * TILE
        msg_ref[pl.ds(at, TILE), :] = jnp.concatenate(parts, axis=0).astype(BF16)


def inner_rows(rows, nblocks):
    return nblocks * rows + nblocks * (rows >> SHIFT_Z)


def outermost_kernel(lw_ref, own_ref, got_ref, out_ref):
    nblocks = out_ref.shape[1] // LANES
    levels = lw_ref.shape[0]
    kinds = 3 * levels
    base = own_ref.shape[0] - nblocks * kinds

    def unpacked(ref):
        packs = [ref[pl.ds(base + k * kinds, PACK * kinds), :].astype(F32) for k in range(0, nblocks, PACK)]
        return [
            jnp.concatenate(
                [p[j * kinds + kind * levels : j * kinds + (kind + 1) * levels] for p in packs for j in range(PACK)], axis=1
            )
            for kind in range(3)
        ]

    own, got = unpacked(own_ref), unpacked(got_ref)
    here = jnp.concatenate([own[0], got[0]], axis=0)
    beyond = jnp.concatenate([got[0], own[0]], axis=0)
    before = jnp.concatenate([own[1], got[1]], axis=0)
    inno = jnp.concatenate([own[2], got[2]], axis=0)
    shape = here.shape
    first_core = parity() == 0
    grad_y = jnp.where((iota(shape, 0) < levels) == first_core, before - beyond, beyond - before)
    lane = iota(shape, 1)
    left = jnp.where(lane == 0, 0.0, pltpu.roll(here, 1, 1))
    right = jnp.where(lane == shape[1] - 1, 0.0, pltpu.roll(here, shape[1] - 1, 1))
    grad_x = right - left
    row = iota((2 * levels, 1), 0)
    weight = jnp.zeros((2 * levels, 1), F32)
    for level in range(levels):
        weight = jnp.where(row % levels == level, lw_ref[level], weight)
    scaled = inno * (0.5 * weight)

    def total(values):
        return [sum(values[k : k + 1] for k in range(f, f + levels)) for f in (0, levels)]

    numer_y, numer_x = total(scaled * grad_y), total(scaled * grad_x)
    denom = total((0.25 * weight) * (grad_y * grad_y + grad_x * grad_x))
    for k in range(2):
        inverse = 1.0 / (1.0 + denom[k])
        out_ref[2 * k : 2 * k + 1, :] = numer_y[k] * inverse
        out_ref[2 * k + 1 : 2 * k + 2, :] = numer_x[k] * inverse


def far_taps(rows, towards):
    side = 2 * parity() - 1
    half = rows // 2
    start = jnp.where((side < 0) == towards, half, 0)
    return taps(iota((rows, half), 1) + start - iota((rows, half), 0) + side * rows)


def near_kernel(*refs):
    raw_refs, near_refs = refs[:PIECES], refs[PIECES : 2 * PIECES]
    edges_ref, near_edges_ref, msg_ref, band_ref, out_ref, high_ref, low_ref = refs[2 * PIECES :]
    _, rows, width = out_ref.shape
    nblocks = width // LANES
    half = rows // 2
    par = parity()
    side = 1 - 2 * par
    offset = iota((rows, rows), 1) - iota((rows, rows), 0)
    near_high, near_low = split(jnp.concatenate([taps(offset), taps(offset + side * rows)], axis=1))
    near_two = jnp.concatenate([near_high, near_low], axis=0)
    far_high, far_low = split(far_taps(rows, True))
    far_two = jnp.concatenate([far_high, far_low], axis=0)
    groups = half >> SHIFT_Y
    shape = (half, groups)
    mean_y = one_hot(iota(shape, 0) >> SHIFT_Y == iota(shape, 1), 1.0 / (1 << SHIFT_Y))
    group_taps = dot(far_high, mean_y).astype(BF16)
    shape = (LANES, SPAN)
    mean_x = one_hot(iota(shape, 1) >> SHIFT_X == iota(shape, 0), 1.0 / (1 << SHIFT_X))
    rest = []
    for span in range(width // SPAN):
        tile = msg_ref[pl.ds(nblocks * rows + span * 2 * groups, 2 * groups), :]
        rest.append(jnp.concatenate([dot(group_taps, tile[:groups]), dot(group_taps, tile[groups:])], axis=0).astype(BF16))
    column = iota((rows, 2 * LANES), 0)
    own_taps = taps(jnp.where(par == 0, 0, rows - 1) - column)
    far_edge_taps = taps(jnp.where(par == 0, -1, rows) - column)
    near_edge_taps = taps(jnp.where(par == 0, 2 * rows - 1, -rows) - column)
    done = 0
    for first in range(0, nblocks, 2):
        while done < min(first + 3, nblocks):
            cols = pl.ds(done * LANES, 2 * LANES)
            place = done * LANES % SPAN
            spread = dot(rest[done * LANES // SPAN], mean_x[:, place : place + 2 * LANES])
            for comp in range(2):
                here = pl.ds(comp * rows, rows)
                pairs, got = [], []
                for k in (done, done + 1):
                    pairs.append(jnp.concatenate([block_of(raw_refs, k)[here, :], block_of(near_refs, k)[here, :]], axis=0))
                    got.append(msg_ref[pl.ds(k * rows + comp * half, half), :])
                high, low = split(jnp.concatenate(pairs, axis=1))
                part = dot(near_two, high) + dot(far_two, jnp.concatenate(got, axis=1))
                part = part[:rows] + part[rows:] + dot(near_high, low) + spread[comp * rows : (comp + 1) * rows]
                part += own_taps * edges_ref[comp : comp + 1, cols]
                part += far_edge_taps * edges_ref[2 + comp : 3 + comp, cols]
                part += near_edge_taps * near_edges_ref[comp : comp + 1, cols]
                high, low = split(part)
                for j in range(2):
                    cut = slice(j * LANES, (j + 1) * LANES)
                    high_ref[done + j, here, :], low_ref[done + j, here, :] = high[:, cut], low[:, cut]
            done += 2
        result = smooth_x(band_ref, high_ref, low_ref, first, nblocks)
        here = pl.ds(first * LANES, 2 * LANES)
        out_ref[0, :, here] = result[:rows]
        out_ref[1, :, here] = result[rows:]


def last_kernel(part_ref, msg_ref, out_hbm, buf, sem):
    _, rows, width = part_ref.shape
    nblocks = width // LANES
    half = rows // 2
    high, low = split(far_taps(rows, False))
    two = jnp.concatenate([high, low], axis=0)
    groups = rows >> SHIFT_Z
    per = TILE // (2 * groups)
    shape = (rows, groups)
    mean_y = one_hot(iota((half, groups), 0) >> SHIFT_Z == iota((half, groups), 1), 1.0 / (1 << SHIFT_Z))
    mean_other = one_hot((iota((half, groups), 0) >> SHIFT_Z) + groups // 2 == iota((half, groups), 1), 1.0 / (1 << SHIFT_Z))
    group_taps = jnp.concatenate([dot(high, mean_y), dot(high, mean_other)], axis=0).astype(BF16)
    copies = []
    for index, first in enumerate(range(0, nblocks, 2)):
        here = pl.ds(first * LANES, 2 * LANES)
        tile = msg_ref[pl.ds(nblocks * rows + index // per * TILE, TILE), :].astype(F32)
        slot = index % per
        sums = [tile[(j * per + slot) * groups : (j * per + slot + 1) * groups] for j in range(2)]
        rest = dot(group_taps, jnp.concatenate(sums, axis=1).astype(BF16))
        for comp in range(2):
            got = [msg_ref[pl.ds((first + j) * rows + comp * half, half), :] for j in range(2)]
            part = dot(two, jnp.concatenate(got, axis=1))
            part = part[:rows] + part[rows:] + rest[comp * rows : (comp + 1) * rows]
            buf[comp, :, here] = part_ref[comp, :, here] + part
        copy = pltpu.make_async_copy(buf.at[:, :, here], out_hbm.at[:, :, here], sem.at[index])
        copy.start()
        copies.append(copy)
    for copy in copies:
        copy.wait()


def body(innovation, background, level_weight):
    levels, rows, width = innovation.shape
    if rows != HALF or width % SPAN or levels != 4:
        raise NotImplementedError("slab shape")
    nblocks = width // LANES
    both, half = 2 * rows, rows // 2
    count = lax.axis_size("row")
    chip = [(i, i ^ 1) for i in range(count) if i ^ 1 < count]
    away = [(i, j) for i in range(count) for j in [((i + 1) ^ 1) - 1] if 0 <= j < count]
    hbm = [pltpu.with_memory_space_constraint(x, pltpu.HBM) for x in (level_weight, innovation, background)]
    band = jnp.asarray(zonal_band())
    piece = jax.ShapeDtypeStruct((nblocks // PIECES, both, LANES), F32)
    result = jax.ShapeDtypeStruct((2, rows, width), F32)
    *raws, outer, row = pl.pallas_call(
        outer_kernel,
        out_shape=[piece] * PIECES
        + [
            jax.ShapeDtypeStruct((outer_rows(rows, nblocks, levels), LANES), BF16),
            jax.ShapeDtypeStruct((TILE, width), BF16),
        ],
        in_specs=[HBM] * 3,
        out_specs=[VMEM] * (PIECES + 2),
        scratch_shapes=[
            pltpu.SMEM((levels,), F32),
            pltpu.VMEM((levels, half, width), BF16),
            pltpu.VMEM((levels, half + TILE, width), BF16),
            pltpu.VMEM((rows, width), BF16),
            pltpu.VMEM((levels, TILE, width), BF16),
            pltpu.SemaphoreType.DMA((2, QUARTERS)),
            pltpu.SemaphoreType.DMA,
            pltpu.SemaphoreType.DMA,
        ],
        compiler_params=PARAMS,
        name="outer_half",
    )(*hbm)
    outer_got = lax.ppermute(outer, "row", away)
    row = lax.ppermute(row, "row", chip)
    *raws, inner = pl.pallas_call(
        inner_kernel,
        out_shape=[piece] * PIECES + [jax.ShapeDtypeStruct((inner_rows(rows, nblocks), LANES), BF16)],
        in_specs=[SMEM] + [VMEM] * (4 + PIECES),
        out_specs=[VMEM] * (PIECES + 1),
        scratch_shapes=[pltpu.VMEM((nblocks, rows, LANES), BF16)] * 2,
        input_output_aliases={5 + k: k for k in range(PIECES)},
        compiler_params=PARAMS,
        name="inner_half",
    )(level_weight, innovation, background, row, band, *raws)
    inner_got = lax.ppermute(inner, "row", away)
    nears = [lax.ppermute(r, "row", chip) for r in raws]
    edges = pl.pallas_call(
        outermost_kernel,
        out_shape=jax.ShapeDtypeStruct((4, width), F32),
        in_specs=[SMEM] + [VMEM] * 2,
        out_specs=VMEM,
        compiler_params=PARAMS,
        name="outermost_rows",
    )(level_weight, outer, outer_got)
    near_edges = lax.ppermute(edges, "row", chip)
    part = pl.pallas_call(
        near_kernel,
        out_shape=result,
        in_specs=[VMEM] * (2 * PIECES + 4),
        out_specs=VMEM,
        scratch_shapes=[pltpu.VMEM((nblocks, both, LANES), BF16)] * 2,
        compiler_params=PARAMS,
        name="near_part",
    )(*raws, *nears, edges, near_edges, outer_got, band)
    return pl.pallas_call(
        last_kernel,
        out_shape=result,
        in_specs=[VMEM] * 2,
        out_specs=HBM,
        scratch_shapes=[pltpu.VMEM((2, rows, width), F32), pltpu.SemaphoreType.DMA((nblocks // 2,))],
        compiler_params=PARAMS,
        name="last_part",
    )(part, inner_got)


def solution(mesh):
    placed = (P("member", "row", None), P("member", "row", None), P())
    return jax.shard_map(
        body, mesh=mesh, in_specs=placed, out_specs=P("member", "row", None), check_vma=False
    )
```

```python
import math

import jax
import jax.numpy as jnp
import numpy as np
from jax import lax
from jax.experimental import pallas as pl
from jax.experimental.pallas import tpu as pltpu
from jax.sharding import PartitionSpec as P

HALF = 64
SIGMA = 64
LANES = 128
TILE = 16
SHIFT_Y, SHIFT_X, SHIFT_Z = 2, 3, 4
SPAN = LANES << SHIFT_X
PACK = 4
QUARTERS = 4
PIECES = 4
F32 = jnp.float32
BF16 = jnp.bfloat16
NORM = math.sqrt(sum(math.exp(-k * k / (SIGMA * SIGMA)) for k in range(-HALF, HALF + 1)))

VMEM = pl.BlockSpec(memory_space=pltpu.VMEM)
HBM = pl.BlockSpec(memory_space=pltpu.HBM)
PARAMS = pltpu.CompilerParams(vmem_limit_bytes=40 * 1024 * 1024)


def split(values):
    high = values.astype(BF16)
    return high, (values - high.astype(F32)).astype(BF16)


def dot(left, right):
    return jnp.dot(left, right, preferred_element_type=F32)


def iota(shape, dim):
    return lax.broadcasted_iota(jnp.int32, shape, dim)


def one_hot(mask, value=1.0):
    return jnp.where(mask, value, 0.0).astype(BF16)


def difference(off):
    return (jnp.where(off == 1, 1.0, 0.0) - jnp.where(off == -1, 1.0, 0.0)).astype(BF16)


def taps(offset):
    off = offset.astype(F32)
    value = jnp.exp(off * off * (-0.5 / (SIGMA * SIGMA))) * (1.0 / NORM)
    return jnp.where(jnp.abs(offset) <= HALF, value, 0.0)


def zonal_band():
    offset = np.arange(4 * LANES)[:, None] - LANES - np.arange(2 * LANES)[None, :]
    band = np.exp(-offset * offset / (2.0 * SIGMA * SIGMA)) / NORM
    band = np.where(np.abs(offset) <= HALF, band, 0.0).astype(np.float32)
    high = band.astype(BF16)
    return np.stack([high, (band - high.astype(np.float32)).astype(BF16)])


def window(first, nblocks):
    low, high = max(first - 1, 0), min(first + 3, nblocks)
    return low, high, (low - first + 1) * LANES, (high - first + 1) * LANES


def smooth_x(band_ref, load, first, nblocks):
    low, high, top, bottom = window(first, nblocks)
    both = jnp.concatenate([load(k) for k in range(low, high)], axis=1)
    rows = both.shape[0] // 2
    found = dot(both, band_ref[0, top:bottom, :])
    return found[:rows] + found[rows:] + dot(both[:rows], band_ref[1, top:bottom, :])


def parity():
    return lax.rem(lax.axis_index("row"), 2)


def block_of(refs, k):
    per = refs[0].shape[0]
    return refs[k // per].at[k % per]


def tile_at(row):
    return pl.ds(pl.multiple_of(row, TILE), TILE)


def half_of(ref, comp_rows, start, part):
    half = comp_rows // 2
    return [ref[part, pl.ds(pl.multiple_of(comp * comp_rows + start, TILE), half), :] for comp in range(2)]


def raw_pair(first, weight, inno_ref, back_ref, upper, diff_y, diff_x, extra, raw_refs):
    levels, rows, width = inno_ref.shape
    half = rows // 2
    start = pl.multiple_of(jnp.where(upper, 0, half), TILE)
    exact = pl.ds(start, half)
    deep = pl.ds(pl.multiple_of(jnp.where(upper, 0, half - TILE), TILE), half + TILE)
    here = pl.ds(first * LANES, 2 * LANES)
    low, high, top, bottom = window(first, width // LANES)
    around = back_ref[:, exact, low * LANES : high * LANES]
    grad_xs = dot(around.reshape(levels * half, -1), diff_x[top:bottom])
    numer_y = numer_x = 0.0
    denom = 1.0
    for level in range(levels):
        grad_y = dot(diff_y, back_ref[level, deep, here])
        if extra is not None:
            grad_y += extra(level, here)
        grad_x = grad_xs[level * half : (level + 1) * half]
        scaled = inno_ref[level, exact, here].astype(F32) * (0.5 * weight(level))
        numer_y += scaled * grad_y
        numer_x += scaled * grad_x
        denom += (0.25 * weight(level)) * (grad_y * grad_y + grad_x * grad_x)
    inverse = 1.0 / denom
    found = []
    for comp, numer in enumerate((numer_y, numer_x)):
        raw = numer * inverse
        if extra is None:
            raw = jnp.where(iota(raw.shape, 0) == jnp.where(upper, 0, half - 1), 0.0, raw)
        found.append(split(raw))
        at = pl.ds(pl.multiple_of(comp * rows + start, TILE), half)
        for part, values in enumerate(found[-1]):
            for j in range(2):
                block_of(raw_refs, first + j)[part, at, :] = values[:, j * LANES : (j + 1) * LANES]
    return found


def differences(upper, half):
    deep = half + TILE
    diff_y = difference(iota((half, deep), 1) - iota((half, deep), 0) - jnp.where(upper, 0, TILE))
    shape = (4 * LANES, 2 * LANES)
    return diff_y, difference(iota(shape, 0) - LANES - iota(shape, 1))


def outer_kernel(lw_hbm, inno_hbm, back_hbm, *refs):
    *raw_refs, msg_ref, row_ref, inno_ref, back_ref, weight_ref, lw_ref, sum_ref, sems, rest_sems, lw_sem = refs
    levels, rows, width = inno_ref.shape
    half = rows // 2
    deep = half + TILE
    nblocks = width // LANES
    upper = parity() == 0
    start = jnp.where(upper, 0, half)
    part = width // QUARTERS

    def bring(sem, which, at, size, cols):
        index = (slice(None), pl.ds(pl.multiple_of(at, TILE), size), cols)
        source, target = ((inno_hbm, inno_ref), (back_hbm, back_ref))[which]
        return pltpu.make_async_copy(source.at[index], target.at[index], sem)

    weights = pltpu.make_async_copy(lw_hbm, lw_ref, lw_sem)
    copies = []
    for q in range(QUARTERS):
        cols = pl.ds(q * part, part)
        copies.append(
            [
                bring(sems.at[1, q], 1, jnp.where(upper, 0, rows - deep), deep, cols),
                bring(sems.at[0, q], 0, start, half, cols),
            ]
        )
    others = [
        bring(rest_sems.at[1], 1, jnp.where(upper, deep, 0), rows - deep, pl.ds(0, width)),
        bring(rest_sems.at[0], 0, half - start, half, pl.ds(0, width)),
    ]
    weights.start()
    for copy in sum(copies, []) + others:
        copy.start()
    diff_y, diff_x = differences(upper, half)
    sum_ref[...] = one_hot(iota(sum_ref.shape, 0) >> SHIFT_X == iota(sum_ref.shape, 1))
    groups = rows >> SHIFT_Y
    shape = (groups, rows)
    sum_y = one_hot(iota(shape, 1) >> SHIFT_Y == iota(shape, 0))
    weights.wait()
    waited = 0
    at = nblocks * rows
    for first in range(0, nblocks, 2):
        while waited * part < window(first, nblocks)[1] * LANES:
            for copy in copies[waited]:
                copy.wait()
            waited += 1
        found = raw_pair(first, lambda k: lw_ref[k], inno_ref, back_ref, upper, diff_y, diff_x, None, raw_refs)
        for comp, (high, _) in enumerate(found):
            for j in range(2):
                msg_ref[pl.ds((first + j) * rows + comp * half, half), :] = high[:, j * LANES : (j + 1) * LANES]
        if (first + 2) * LANES % SPAN == 0:
            blocks = range(first + 2 - SPAN // LANES, first + 2)
            lows = [jnp.concatenate(half_of(block_of(raw_refs, k), rows, start, 1), axis=0) for k in blocks]
            total = dot(jnp.concatenate(lows, axis=1), sum_ref[...])
            msg_ref[pl.ds(at, groups), :] = dot(sum_y, total.astype(BF16)).astype(BF16)
            at += groups
    kinds = 3 * levels
    shape = (PACK * kinds, PACK * levels * TILE)
    row, col = iota(shape, 0), iota(shape, 1)
    want = row - (col >> 6) * kinds
    level = (col >> 4) & (levels - 1)
    place = col & (TILE - 1)
    outermost = place == jnp.where(upper, 0, TILE - 1)
    next_row = place == jnp.where(upper, 1, TILE - 2)
    of_back = one_hot(((want == level) & outermost) | ((want == levels + level) & next_row))
    of_inno = one_hot((want == 2 * levels + level) & outermost)
    edge_at = tile_at(jnp.where(upper, 0, rows - TILE))
    for first in range(0, nblocks, PACK):
        back, inno = [], []
        for k in range(first, first + PACK):
            here = pl.ds(k * LANES, LANES)
            back.append(back_ref[:, edge_at, here].reshape(levels * TILE, LANES))
            inno.append(inno_ref[:, edge_at, here].reshape(levels * TILE, LANES))
        tile = dot(of_back, jnp.concatenate(back, axis=0)) + dot(of_inno, jnp.concatenate(inno, axis=0))
        msg_ref[pl.ds(at, PACK * kinds), :] = tile.astype(BF16)
        at += PACK * kinds
    for level in range(2 * levels):
        weight_ref[level : level + 1, :] = jnp.full((1, weight_ref.shape[1]), lw_ref[level % levels])
    for copy in others:
        copy.wait()
    shape = (TILE, levels * TILE)
    pick = one_hot(iota(shape, 1) == iota(shape, 0) * TILE + jnp.where(upper, TILE - 1, 0))
    near_rows = back_ref[:, tile_at(jnp.where(upper, rows - TILE, 0)), :]
    row_ref[...] = dot(pick, near_rows.reshape(levels * TILE, -1)).astype(BF16)


def outer_rows(rows, nblocks, levels):
    return nblocks * rows + (nblocks * LANES // SPAN) * (rows >> SHIFT_Y) + nblocks * 3 * levels


def inner_kernel(weight_ref, inno_ref, back_ref, row_ref, band_ref, *refs):
    raw_refs = refs[PIECES : 2 * PIECES]
    msg_ref = refs[2 * PIECES]
    _, rows, width = inno_ref.shape
    half = rows // 2
    nblocks = width // LANES
    upper = parity() == 1
    start = jnp.where(upper, 0, half)
    diff_y, diff_x = differences(upper, half)
    at = iota((half, 2 * LANES), 0) == jnp.where(upper, 0, half - 1)
    sign = jnp.where(upper, -1.0, 1.0)

    def extra(level, here):
        return jnp.where(at, row_ref[level : level + 1, here].astype(F32) * sign, 0.0)

    def weight(level):
        return weight_ref[level : level + 1, :]

    def load(k):
        block = block_of(raw_refs, k)
        return jnp.concatenate(half_of(block, rows, start, 0) + half_of(block, rows, start, 1), axis=0)

    groups = rows >> SHIFT_Z
    shape = (2 * groups, rows)
    sum_y = one_hot(iota(shape, 1) >> SHIFT_Z == iota(shape, 0))
    sums = []
    per = TILE // (2 * groups)
    done = 0
    for first in range(0, nblocks, 2):
        while done < min(first + 3, nblocks):
            raw_pair(done, weight, inno_ref, back_ref, upper, diff_y, diff_x, extra, raw_refs)
            done += 2
        high, low = split(smooth_x(band_ref, load, first, nblocks))
        sums.append(dot(sum_y, low)[:groups])
        for j in range(2):
            msg_ref[pl.ds((first + j) * rows, rows), :] = high[:, j * LANES : (j + 1) * LANES]
        if len(sums) == per:
            parts = [x[:, j * LANES : (j + 1) * LANES] for j in range(2) for x in sums]
            tile = nblocks * rows + first // (2 * per) * TILE
            msg_ref[pl.ds(tile, TILE), :] = jnp.concatenate(parts, axis=0).astype(BF16)
            sums = []


def inner_rows(rows, nblocks):
    return nblocks * rows + nblocks * (rows >> SHIFT_Z)


def outermost_kernel(weight_ref, own_ref, got_ref, out_ref):
    nblocks = out_ref.shape[1] // LANES
    levels = weight_ref.shape[0] // 2
    kinds = 3 * levels
    base = own_ref.shape[0] - nblocks * kinds

    def unpacked(ref):
        packs = [ref[pl.ds(base + k * kinds, PACK * kinds), :].astype(F32) for k in range(0, nblocks, PACK)]
        return [
            jnp.concatenate(
                [p[j * kinds + kind * levels : j * kinds + (kind + 1) * levels] for p in packs for j in range(PACK)], axis=1
            )
            for kind in range(3)
        ]

    own, got = unpacked(own_ref), unpacked(got_ref)
    here = jnp.concatenate([own[0], got[0]], axis=0)
    beyond = jnp.concatenate([got[0], own[0]], axis=0)
    before = jnp.concatenate([own[1], got[1]], axis=0)
    inno = jnp.concatenate([own[2], got[2]], axis=0)
    shape = here.shape
    first_core = parity() == 0
    grad_y = jnp.where((iota(shape, 0) < levels) == first_core, before - beyond, beyond - before)
    lane = iota(shape, 1)
    left = jnp.where(lane == 0, 0.0, pltpu.roll(here, 1, 1))
    right = jnp.where(lane == shape[1] - 1, 0.0, pltpu.roll(here, shape[1] - 1, 1))
    grad_x = right - left
    weight = jnp.concatenate([weight_ref[:, :LANES]] * nblocks, axis=1)
    scaled = inno * (0.5 * weight)

    def total(values):
        return [sum(values[k : k + 1] for k in range(f, f + levels)) for f in (0, levels)]

    numer_y, numer_x = total(scaled * grad_y), total(scaled * grad_x)
    denom = total((0.25 * weight) * (grad_y * grad_y + grad_x * grad_x))
    found = []
    for k in range(2):
        inverse = 1.0 / (1.0 + denom[k])
        found += [numer_y[k] * inverse, numer_x[k] * inverse]
    high, low = split(jnp.concatenate(found, axis=0))
    none = jnp.zeros((TILE - 8, shape[1]), F32)
    out_ref[...] = jnp.concatenate([high.astype(F32), low.astype(F32), none], axis=0).astype(BF16)


def far_taps(rows, towards):
    side = 2 * parity() - 1
    half = rows // 2
    start = jnp.where((side < 0) == towards, half, 0)
    return taps(iota((rows, half), 1) + start - iota((rows, half), 0) + side * rows)


def near_kernel(*refs):
    raw_refs, near_refs = refs[:PIECES], refs[PIECES : 2 * PIECES]
    edges_ref, near_edges_ref, msg_ref, band_ref, out_ref, total_ref = refs[2 * PIECES :]
    _, rows, width = out_ref.shape
    nblocks = width // LANES
    half = rows // 2
    par = parity()
    side = 1 - 2 * par
    offset = iota((rows, rows), 1) - iota((rows, rows), 0)
    near_taps = jnp.concatenate([taps(offset), taps(offset + side * rows)], axis=1)
    near_high = near_taps.astype(BF16)
    toward = far_taps(rows, True)
    shape = (rows, TILE)
    kind = iota(shape, 1)
    own_at = jnp.where(par == 0, 0, rows - 1)
    far_at = jnp.where(par == 0, -1, rows)
    near_at = jnp.where(par == 0, 2 * rows - 1, -rows)
    own_edges = taps(jnp.where(kind & 2 == 0, own_at, far_at) - iota(shape, 0))
    near_edges = jnp.where(kind & 2 == 0, taps(near_at - iota(shape, 0)), 0.0)
    stacked = []
    for comp in range(2):
        here = (kind < 8) & (kind & 1 == comp)
        all_taps = [near_taps, toward, jnp.where(here, own_edges, 0.0), jnp.where(here, near_edges, 0.0)]
        stacked.append(jnp.concatenate(split(jnp.concatenate(all_taps, axis=1)), axis=0))
    groups = half >> SHIFT_Y
    shape = (half, groups)
    mean_y = one_hot(iota(shape, 0) >> SHIFT_Y == iota(shape, 1), 1.0 / (1 << SHIFT_Y))
    group_taps = dot(toward.astype(BF16), mean_y).astype(BF16)
    shape = (LANES, SPAN)
    mean_x = one_hot(iota(shape, 1) >> SHIFT_X == iota(shape, 0), 1.0 / (1 << SHIFT_X))
    rest = []
    for span in range(width // SPAN):
        tile = msg_ref[pl.ds(nblocks * rows + span * 2 * groups, 2 * groups), :]
        rest.append(jnp.concatenate([dot(group_taps, tile[:groups]), dot(group_taps, tile[groups:])], axis=0).astype(BF16))
    done = 0
    for first in range(0, nblocks, 2):
        while done < min(first + 3, nblocks):
            cols = pl.ds(done * LANES, 2 * LANES)
            place = done * LANES % SPAN
            spread = dot(rest[done * LANES // SPAN], mean_x[:, place : place + 2 * LANES])
            for comp in range(2):
                here = pl.ds(comp * rows, rows)
                highs, lows = [], []
                for k in (done, done + 1):
                    both = (block_of(raw_refs, k), block_of(near_refs, k))
                    got = msg_ref[pl.ds(k * rows + comp * half, half), :]
                    highs.append(jnp.concatenate([ref[0, here, :] for ref in both] + [got], axis=0))
                    lows.append(jnp.concatenate([ref[1, here, :] for ref in both], axis=0))
                edges = [edges_ref[:, cols], near_edges_ref[:, cols]]
                part = dot(stacked[comp], jnp.concatenate([jnp.concatenate(highs, axis=1)] + edges, axis=0))
                part = part[:rows] + part[rows:] + dot(near_high, jnp.concatenate(lows, axis=1))
                high, low = split(part + spread[comp * rows : (comp + 1) * rows])
                for j in range(2):
                    cut = slice(j * LANES, (j + 1) * LANES)
                    total_ref[done + j, pl.ds(comp * rows, rows), :] = high[:, cut]
                    total_ref[done + j, pl.ds((2 + comp) * rows, rows), :] = low[:, cut]
            done += 2
        result = smooth_x(band_ref, lambda k: total_ref[k], first, nblocks)
        here = pl.ds(first * LANES, 2 * LANES)
        out_ref[0, :, here] = result[:rows]
        out_ref[1, :, here] = result[rows:]


def last_kernel(part_ref, msg_ref, out_hbm, buf, sem):
    _, rows, width = part_ref.shape
    nblocks = width // LANES
    half = rows // 2
    high, low = split(far_taps(rows, False))
    two = jnp.concatenate([high, low], axis=0)
    groups = rows >> SHIFT_Z
    per = TILE // (2 * groups)
    shape = (rows, groups)
    mean_y = one_hot(iota((half, groups), 0) >> SHIFT_Z == iota((half, groups), 1), 1.0 / (1 << SHIFT_Z))
    mean_other = one_hot((iota((half, groups), 0) >> SHIFT_Z) + groups // 2 == iota((half, groups), 1), 1.0 / (1 << SHIFT_Z))
    group_taps = jnp.concatenate([dot(high, mean_y), dot(high, mean_other)], axis=0).astype(BF16)
    copies = []
    for index, first in enumerate(range(0, nblocks, 2)):
        here = pl.ds(first * LANES, 2 * LANES)
        tile = msg_ref[pl.ds(nblocks * rows + index // per * TILE, TILE), :].astype(F32)
        slot = index % per
        sums = [tile[(j * per + slot) * groups : (j * per + slot + 1) * groups] for j in range(2)]
        rest = dot(group_taps, jnp.concatenate(sums, axis=1).astype(BF16))
        for comp in range(2):
            got = [msg_ref[pl.ds((first + j) * rows + comp * half, half), :] for j in range(2)]
            part = dot(two, jnp.concatenate(got, axis=1))
            part = part[:rows] + part[rows:] + rest[comp * rows : (comp + 1) * rows]
            buf[comp, :, here] = part_ref[comp, :, here] + part
        copy = pltpu.make_async_copy(buf.at[:, :, here], out_hbm.at[:, :, here], sem.at[index])
        copy.start()
        copies.append(copy)
    for copy in copies:
        copy.wait()


def body(innovation, background, level_weight):
    levels, rows, width = innovation.shape
    if rows != HALF or width % SPAN or levels != 4:
        raise NotImplementedError("slab shape")
    nblocks = width // LANES
    both, half = 2 * rows, rows // 2
    count = lax.axis_size("row")
    chip = [(i, i ^ 1) for i in range(count) if i ^ 1 < count]
    away = [(i, j) for i in range(count) for j in [((i + 1) ^ 1) - 1] if 0 <= j < count]
    hbm = [pltpu.with_memory_space_constraint(x, pltpu.HBM) for x in (level_weight, innovation, background)]
    band = jnp.asarray(zonal_band())
    piece = jax.ShapeDtypeStruct((nblocks // PIECES, 2, both, LANES), BF16)
    result = jax.ShapeDtypeStruct((2, rows, width), F32)
    *raws, outer, row, inno, back, weight = pl.pallas_call(
        outer_kernel,
        out_shape=[piece] * PIECES
        + [
            jax.ShapeDtypeStruct((outer_rows(rows, nblocks, levels), LANES), BF16),
            jax.ShapeDtypeStruct((TILE, width), BF16),
            jax.ShapeDtypeStruct(innovation.shape, BF16),
            jax.ShapeDtypeStruct(background.shape, BF16),
            jax.ShapeDtypeStruct((2 * levels, 2 * LANES), F32),
        ],
        in_specs=[HBM] * 3,
        out_specs=[VMEM] * (PIECES + 5),
        scratch_shapes=[
            pltpu.SMEM((levels,), F32),
            pltpu.VMEM((SPAN, LANES), BF16),
            pltpu.SemaphoreType.DMA((2, QUARTERS)),
            pltpu.SemaphoreType.DMA((2,)),
            pltpu.SemaphoreType.DMA,
        ],
        compiler_params=PARAMS,
        name="outer_half",
    )(*hbm)
    outer_got = lax.ppermute(outer, "row", away)
    row = lax.ppermute(row, "row", chip)
    *raws, inner = pl.pallas_call(
        inner_kernel,
        out_shape=[piece] * PIECES + [jax.ShapeDtypeStruct((inner_rows(rows, nblocks), LANES), BF16)],
        in_specs=[VMEM] * (5 + PIECES),
        out_specs=[VMEM] * (PIECES + 1),
        input_output_aliases={5 + k: k for k in range(PIECES)},
        compiler_params=PARAMS,
        name="inner_half",
    )(weight, inno, back, row, band, *raws)
    inner_got = lax.ppermute(inner, "row", away)
    nears = [lax.ppermute(r, "row", chip) for r in raws]
    edges = pl.pallas_call(
        outermost_kernel,
        out_shape=jax.ShapeDtypeStruct((TILE, width), BF16),
        in_specs=[VMEM] * 3,
        out_specs=VMEM,
        compiler_params=PARAMS,
        name="outermost_rows",
    )(weight, outer, outer_got)
    near_edges = lax.ppermute(edges, "row", chip)
    part = pl.pallas_call(
        near_kernel,
        out_shape=result,
        in_specs=[VMEM] * (2 * PIECES + 4),
        out_specs=VMEM,
        scratch_shapes=[pltpu.VMEM((nblocks, 2 * both, LANES), BF16)],
        compiler_params=PARAMS,
        name="near_part",
    )(*raws, *nears, edges, near_edges, outer_got, band)
    return pl.pallas_call(
        last_kernel,
        out_shape=result,
        in_specs=[VMEM] * 2,
        out_specs=HBM,
        scratch_shapes=[pltpu.VMEM((2, rows, width), F32), pltpu.SemaphoreType.DMA((nblocks // 2,))],
        compiler_params=PARAMS,
        name="last_part",
    )(part, inner_got)


def solution(mesh):
    placed = (P("member", "row", None), P("member", "row", None), P())
    return jax.shard_map(
        body, mesh=mesh, in_specs=placed, out_specs=P("member", "row", None), check_vma=False
    )
```

```python
import math

import jax
import jax.numpy as jnp
import numpy as np
from jax import lax
from jax.experimental import pallas as pl
from jax.experimental.pallas import tpu as pltpu
from jax.sharding import PartitionSpec as P

HALF = 64
SIGMA = 64
LANES = 128
TILE = 16
SHIFT_Y, SHIFT_X, SHIFT_Z = 2, 3, 4
SPAN = LANES << SHIFT_X
PACK = 4
QUARTERS = 4
PIECES = 4
F32 = jnp.float32
BF16 = jnp.bfloat16
NORM = math.sqrt(sum(math.exp(-k * k / (SIGMA * SIGMA)) for k in range(-HALF, HALF + 1)))

VMEM = pl.BlockSpec(memory_space=pltpu.VMEM)
HBM = pl.BlockSpec(memory_space=pltpu.HBM)
PARAMS = pltpu.CompilerParams(vmem_limit_bytes=40 * 1024 * 1024)


def split(values):
    high = values.astype(BF16)
    return high, (values - high.astype(F32)).astype(BF16)


def dot(left, right):
    return jnp.dot(left, right, preferred_element_type=F32)


def iota(shape, dim):
    return lax.broadcasted_iota(jnp.int32, shape, dim)


def one_hot(mask, value=1.0):
    return jnp.where(mask, value, 0.0).astype(BF16)


def difference(off):
    return (jnp.where(off == 1, 1.0, 0.0) - jnp.where(off == -1, 1.0, 0.0)).astype(BF16)


def taps(offset):
    off = offset.astype(F32)
    value = jnp.exp(off * off * (-0.5 / (SIGMA * SIGMA))) * (1.0 / NORM)
    return jnp.where(jnp.abs(offset) <= HALF, value, 0.0)


def zonal_band():
    offset = np.arange(4 * LANES)[:, None] - LANES - np.arange(2 * LANES)[None, :]
    band = np.exp(-offset * offset / (2.0 * SIGMA * SIGMA)) / NORM
    band = np.where(np.abs(offset) <= HALF, band, 0.0).astype(np.float32)
    high = band.astype(BF16)
    return np.stack([high, (band - high.astype(np.float32)).astype(BF16)])


def window(first, nblocks):
    low, high = max(first - 1, 0), min(first + 3, nblocks)
    return low, high, (low - first + 1) * LANES, (high - first + 1) * LANES


def smooth_x(band_ref, load, first, nblocks):
    low, high, top, bottom = window(first, nblocks)
    both = jnp.concatenate([load(k) for k in range(low, high)], axis=1)
    rows = both.shape[0] // 2
    found = dot(both, band_ref[0, top:bottom, :])
    return found[:rows] + found[rows:] + dot(both[:rows], band_ref[1, top:bottom, :])


def parity():
    return lax.rem(lax.axis_index("row"), 2)


def block_of(refs, k):
    per = refs[0].shape[0]
    return refs[k // per].at[k % per]


def tile_at(row):
    return pl.ds(pl.multiple_of(row, TILE), TILE)


def half_of(ref, comp_rows, start, part):
    half = comp_rows // 2
    return [ref[part, pl.ds(pl.multiple_of(comp * comp_rows + start, TILE), half), :] for comp in range(2)]


def raw_pair(first, weight, inno_ref, back_ref, upper, diff_y, diff_x, extra, raw_refs):
    levels, rows, width = inno_ref.shape
    half = rows // 2
    start = pl.multiple_of(jnp.where(upper, 0, half), TILE)
    exact = pl.ds(start, half)
    deep = pl.ds(pl.multiple_of(jnp.where(upper, 0, half - TILE), TILE), half + TILE)
    here = pl.ds(first * LANES, 2 * LANES)
    low, high, top, bottom = window(first, width // LANES)
    around = back_ref[:, exact, low * LANES : high * LANES]
    grad_xs = dot(around.reshape(levels * half, -1), diff_x[top:bottom])
    numer_y = numer_x = 0.0
    denom = 1.0
    for level in range(levels):
        grad_y = dot(diff_y, back_ref[level, deep, here])
        if extra is not None:
            grad_y += extra(level, here)
        grad_x = grad_xs[level * half : (level + 1) * half]
        scaled = inno_ref[level, exact, here].astype(F32) * (0.5 * weight(level))
        numer_y += scaled * grad_y
        numer_x += scaled * grad_x
        denom += (0.25 * weight(level)) * (grad_y * grad_y + grad_x * grad_x)
    inverse = 1.0 / denom
    found = []
    for comp, numer in enumerate((numer_y, numer_x)):
        raw = numer * inverse
        if extra is None:
            raw = jnp.where(iota(raw.shape, 0) == jnp.where(upper, 0, half - 1), 0.0, raw)
        found.append(split(raw))
        at = pl.ds(pl.multiple_of(comp * rows + start, TILE), half)
        for part, values in enumerate(found[-1]):
            for j in range(2):
                block_of(raw_refs, first + j)[part, at, :] = values[:, j * LANES : (j + 1) * LANES]
    return found


def differences(upper, half):
    deep = half + TILE
    diff_y = difference(iota((half, deep), 1) - iota((half, deep), 0) - jnp.where(upper, 0, TILE))
    shape = (4 * LANES, 2 * LANES)
    return diff_y, difference(iota(shape, 0) - LANES - iota(shape, 1))


def outer_kernel(lw_hbm, inno_hbm, back_hbm, *refs):
    *raw_refs, msg_ref, row_ref, inno_ref, back_ref, weight_ref, lw_ref, sum_ref, sems, rest_sems, lw_sem = refs
    levels, rows, width = inno_ref.shape
    half = rows // 2
    deep = half + TILE
    nblocks = width // LANES
    upper = parity() == 0
    start = jnp.where(upper, 0, half)
    part = width // QUARTERS

    def bring(sem, which, at, size, cols):
        index = (slice(None), pl.ds(pl.multiple_of(at, TILE), size), cols)
        source, target = ((inno_hbm, inno_ref), (back_hbm, back_ref))[which]
        return pltpu.make_async_copy(source.at[index], target.at[index], sem)

    weights = pltpu.make_async_copy(lw_hbm, lw_ref, lw_sem)
    copies = []
    for q in range(QUARTERS):
        cols = pl.ds(q * part, part)
        copies.append(
            [
                bring(sems.at[1, q], 1, jnp.where(upper, 0, rows - deep), deep, cols),
                bring(sems.at[0, q], 0, start, half, cols),
            ]
        )
    others = [
        bring(rest_sems.at[1], 1, jnp.where(upper, deep, 0), rows - deep, pl.ds(0, width)),
        bring(rest_sems.at[0], 0, half - start, half, pl.ds(0, width)),
    ]
    weights.start()
    for copy in sum(copies, []) + others:
        copy.start()
    diff_y, diff_x = differences(upper, half)
    sum_ref[...] = one_hot(iota(sum_ref.shape, 0) >> SHIFT_X == iota(sum_ref.shape, 1))
    groups = rows >> SHIFT_Y
    shape = (groups, rows)
    sum_y = one_hot(iota(shape, 1) >> SHIFT_Y == iota(shape, 0))
    weights.wait()
    waited = 0
    at = nblocks * rows
    for first in range(0, nblocks, 2):
        while waited * part < window(first, nblocks)[1] * LANES:
            for copy in copies[waited]:
                copy.wait()
            waited += 1
        found = raw_pair(first, lambda k: lw_ref[k], inno_ref, back_ref, upper, diff_y, diff_x, None, raw_refs)
        for comp, (high, _) in enumerate(found):
            for j in range(2):
                msg_ref[pl.ds((first + j) * rows + comp * half, half), :] = high[:, j * LANES : (j + 1) * LANES]
    totals = []
    for span in range(0, nblocks, SPAN // LANES):
        blocks = range(span, span + SPAN // LANES)
        lows = [jnp.concatenate(half_of(block_of(raw_refs, k), rows, start, 1), axis=0) for k in blocks]
        totals.append(dot(jnp.concatenate(lows, axis=1), sum_ref[...]))
    for total in totals:
        msg_ref[pl.ds(at, groups), :] = dot(sum_y, total.astype(BF16)).astype(BF16)
        at += groups
    kinds = 3 * levels
    shape = (PACK * kinds, PACK * levels * TILE)
    row, col = iota(shape, 0), iota(shape, 1)
    want = row - (col >> 6) * kinds
    level = (col >> 4) & (levels - 1)
    place = col & (TILE - 1)
    outermost = place == jnp.where(upper, 0, TILE - 1)
    next_row = place == jnp.where(upper, 1, TILE - 2)
    of_back = one_hot(((want == level) & outermost) | ((want == levels + level) & next_row))
    of_inno = one_hot((want == 2 * levels + level) & outermost)
    edge_at = tile_at(jnp.where(upper, 0, rows - TILE))
    for first in range(0, nblocks, PACK):
        back, inno = [], []
        for k in range(first, first + PACK):
            here = pl.ds(k * LANES, LANES)
            back.append(back_ref[:, edge_at, here].reshape(levels * TILE, LANES))
            inno.append(inno_ref[:, edge_at, here].reshape(levels * TILE, LANES))
        tile = dot(of_back, jnp.concatenate(back, axis=0)) + dot(of_inno, jnp.concatenate(inno, axis=0))
        msg_ref[pl.ds(at, PACK * kinds), :] = tile.astype(BF16)
        at += PACK * kinds
    for level in range(2 * levels):
        weight_ref[level : level + 1, :] = jnp.full((1, weight_ref.shape[1]), lw_ref[level % levels])
    for copy in others:
        copy.wait()
    shape = (TILE, levels * TILE)
    pick = one_hot(iota(shape, 1) == iota(shape, 0) * TILE + jnp.where(upper, TILE - 1, 0))
    near_rows = back_ref[:, tile_at(jnp.where(upper, rows - TILE, 0)), :]
    row_ref[...] = dot(pick, near_rows.reshape(levels * TILE, -1)).astype(BF16)


def outer_rows(rows, nblocks, levels):
    return nblocks * rows + (nblocks * LANES // SPAN) * (rows >> SHIFT_Y) + nblocks * 3 * levels


def inner_kernel(weight_ref, inno_ref, back_ref, row_ref, band_ref, *refs):
    raw_refs = refs[PIECES : 2 * PIECES]
    msg_ref, rest_ref = refs[2 * PIECES :]
    _, rows, width = inno_ref.shape
    half = rows // 2
    nblocks = width // LANES
    upper = parity() == 1
    start = jnp.where(upper, 0, half)
    diff_y, diff_x = differences(upper, half)
    at = iota((half, 2 * LANES), 0) == jnp.where(upper, 0, half - 1)
    sign = jnp.where(upper, -1.0, 1.0)

    def extra(level, here):
        return jnp.where(at, row_ref[level : level + 1, here].astype(F32) * sign, 0.0)

    def weight(level):
        return weight_ref[level : level + 1, :]

    def load(k):
        block = block_of(raw_refs, k)
        return jnp.concatenate(half_of(block, rows, start, 0) + half_of(block, rows, start, 1), axis=0)

    groups = rows >> SHIFT_Z
    shape = (2 * groups, rows)
    sum_y = one_hot(iota(shape, 1) >> SHIFT_Z == iota(shape, 0))
    for first in range(0, nblocks, 2):
        raw_pair(first, weight, inno_ref, back_ref, upper, diff_y, diff_x, extra, raw_refs)
    for first in range(0, nblocks, 2):
        high, low = split(smooth_x(band_ref, load, first, nblocks))
        rest_ref[:, first * LANES : (first + 2) * LANES] = low
        for j in range(2):
            msg_ref[pl.ds((first + j) * rows, rows), :] = high[:, j * LANES : (j + 1) * LANES]
    sums = dot(sum_y, rest_ref[...])
    per = TILE // groups
    for first in range(0, nblocks, per):
        parts = [sums[:groups, k * LANES : (k + 1) * LANES] for k in range(first, first + per)]
        msg_ref[pl.ds(nblocks * rows + first // per * TILE, TILE), :] = jnp.concatenate(parts, axis=0).astype(BF16)


def inner_rows(rows, nblocks):
    return nblocks * rows + nblocks * (rows >> SHIFT_Z)


def outermost_kernel(weight_ref, own_ref, got_ref, out_ref):
    nblocks = out_ref.shape[1] // LANES
    levels = weight_ref.shape[0] // 2
    kinds = 3 * levels
    base = own_ref.shape[0] - nblocks * kinds

    def unpacked(ref):
        packs = [ref[pl.ds(base + k * kinds, PACK * kinds), :].astype(F32) for k in range(0, nblocks, PACK)]
        return [
            jnp.concatenate(
                [p[j * kinds + kind * levels : j * kinds + (kind + 1) * levels] for p in packs for j in range(PACK)], axis=1
            )
            for kind in range(3)
        ]

    own, got = unpacked(own_ref), unpacked(got_ref)
    here = jnp.concatenate([own[0], got[0]], axis=0)
    beyond = jnp.concatenate([got[0], own[0]], axis=0)
    before = jnp.concatenate([own[1], got[1]], axis=0)
    inno = jnp.concatenate([own[2], got[2]], axis=0)
    shape = here.shape
    first_core = parity() == 0
    grad_y = jnp.where((iota(shape, 0) < levels) == first_core, before - beyond, beyond - before)
    lane = iota(shape, 1)
    left = jnp.where(lane == 0, 0.0, pltpu.roll(here, 1, 1))
    right = jnp.where(lane == shape[1] - 1, 0.0, pltpu.roll(here, shape[1] - 1, 1))
    grad_x = right - left
    weight = jnp.concatenate([weight_ref[:, :LANES]] * nblocks, axis=1)
    scaled = inno * (0.5 * weight)

    def total(values):
        return [sum(values[k : k + 1] for k in range(f, f + levels)) for f in (0, levels)]

    numer_y, numer_x = total(scaled * grad_y), total(scaled * grad_x)
    denom = total((0.25 * weight) * (grad_y * grad_y + grad_x * grad_x))
    found = []
    for k in range(2):
        inverse = 1.0 / (1.0 + denom[k])
        found += [numer_y[k] * inverse, numer_x[k] * inverse]
    high, low = split(jnp.concatenate(found, axis=0))
    none = jnp.zeros((TILE - 8, shape[1]), F32)
    out_ref[...] = jnp.concatenate([high.astype(F32), low.astype(F32), none], axis=0).astype(BF16)


def far_taps(rows, towards):
    side = 2 * parity() - 1
    half = rows // 2
    start = jnp.where((side < 0) == towards, half, 0)
    return taps(iota((rows, half), 1) + start - iota((rows, half), 0) + side * rows)


def near_kernel(*refs):
    raw_refs, near_refs = refs[:PIECES], refs[PIECES : 2 * PIECES]
    edges_ref, near_edges_ref, msg_ref, band_ref, out_ref, total_ref = refs[2 * PIECES :]
    _, rows, width = out_ref.shape
    nblocks = width // LANES
    half = rows // 2
    par = parity()
    side = 1 - 2 * par
    offset = iota((rows, rows), 1) - iota((rows, rows), 0)
    near_taps = jnp.concatenate([taps(offset), taps(offset + side * rows)], axis=1)
    near_high = near_taps.astype(BF16)
    toward = far_taps(rows, True)
    shape = (rows, TILE)
    kind = iota(shape, 1)
    own_at = jnp.where(par == 0, 0, rows - 1)
    far_at = jnp.where(par == 0, -1, rows)
    near_at = jnp.where(par == 0, 2 * rows - 1, -rows)
    own_edges = taps(jnp.where(kind & 2 == 0, own_at, far_at) - iota(shape, 0))
    near_edges = jnp.where(kind & 2 == 0, taps(near_at - iota(shape, 0)), 0.0)
    stacked = []
    for comp in range(2):
        here = (kind < 8) & (kind & 1 == comp)
        all_taps = [near_taps, toward, jnp.where(here, own_edges, 0.0), jnp.where(here, near_edges, 0.0)]
        stacked.append(jnp.concatenate(split(jnp.concatenate(all_taps, axis=1)), axis=0))
    groups = half >> SHIFT_Y
    shape = (half, groups)
    mean_y = one_hot(iota(shape, 0) >> SHIFT_Y == iota(shape, 1), 1.0 / (1 << SHIFT_Y))
    group_taps = dot(toward.astype(BF16), mean_y).astype(BF16)
    shape = (LANES, SPAN)
    mean_x = one_hot(iota(shape, 1) >> SHIFT_X == iota(shape, 0), 1.0 / (1 << SHIFT_X))
    rest = []
    for span in range(width // SPAN):
        tile = msg_ref[pl.ds(nblocks * rows + span * 2 * groups, 2 * groups), :]
        rest.append(jnp.concatenate([dot(group_taps, tile[:groups]), dot(group_taps, tile[groups:])], axis=0).astype(BF16))
    for first in range(0, nblocks, 2):
        cols = pl.ds(first * LANES, 2 * LANES)
        place = first * LANES % SPAN
        spread = dot(rest[first * LANES // SPAN], mean_x[:, place : place + 2 * LANES])
        edges = [edges_ref[:, cols], near_edges_ref[:, cols]]
        for comp in range(2):
            here = pl.ds(comp * rows, rows)
            highs, lows = [], []
            for k in (first, first + 1):
                both = (block_of(raw_refs, k), block_of(near_refs, k))
                got = msg_ref[pl.ds(k * rows + comp * half, half), :]
                highs.append(jnp.concatenate([ref[0, here, :] for ref in both] + [got], axis=0))
                lows.append(jnp.concatenate([ref[1, here, :] for ref in both], axis=0))
            part = dot(stacked[comp], jnp.concatenate([jnp.concatenate(highs, axis=1)] + edges, axis=0))
            part = part[:rows] + part[rows:] + dot(near_high, jnp.concatenate(lows, axis=1))
            high, low = split(part + spread[comp * rows : (comp + 1) * rows])
            for j in range(2):
                cut = slice(j * LANES, (j + 1) * LANES)
                total_ref[first + j, pl.ds(comp * rows, rows), :] = high[:, cut]
                total_ref[first + j, pl.ds((2 + comp) * rows, rows), :] = low[:, cut]
    for first in range(0, nblocks, 2):
        result = smooth_x(band_ref, lambda k: total_ref[k], first, nblocks)
        here = pl.ds(first * LANES, 2 * LANES)
        out_ref[0, :, here] = result[:rows]
        out_ref[1, :, here] = result[rows:]


def last_kernel(part_ref, msg_ref, out_hbm, buf, sem):
    _, rows, width = part_ref.shape
    nblocks = width // LANES
    half = rows // 2
    high, low = split(far_taps(rows, False))
    two = jnp.concatenate([high, low], axis=0)
    groups = rows >> SHIFT_Z
    per = TILE // groups
    mean_y = one_hot(iota((half, groups), 0) >> SHIFT_Z == iota((half, groups), 1), 1.0 / (1 << SHIFT_Z))
    mean_other = one_hot((iota((half, groups), 0) >> SHIFT_Z) + groups // 2 == iota((half, groups), 1), 1.0 / (1 << SHIFT_Z))
    group_taps = jnp.concatenate([dot(high, mean_y), dot(high, mean_other)], axis=0).astype(BF16)
    copies = []
    for index, first in enumerate(range(0, nblocks, 2)):
        here = pl.ds(first * LANES, 2 * LANES)
        tile = msg_ref[pl.ds(nblocks * rows + first // per * TILE, TILE), :].astype(F32)
        sums = [tile[k % per * groups : (k % per + 1) * groups] for k in (first, first + 1)]
        rest = dot(group_taps, jnp.concatenate(sums, axis=1).astype(BF16))
        for comp in range(2):
            got = [msg_ref[pl.ds((first + j) * rows + comp * half, half), :] for j in range(2)]
            part = dot(two, jnp.concatenate(got, axis=1))
            part = part[:rows] + part[rows:] + rest[comp * rows : (comp + 1) * rows]
            buf[comp, :, here] = part_ref[comp, :, here] + part
        copy = pltpu.make_async_copy(buf.at[:, :, here], out_hbm.at[:, :, here], sem.at[index])
        copy.start()
        copies.append(copy)
    for copy in copies:
        copy.wait()


def body(innovation, background, level_weight):
    levels, rows, width = innovation.shape
    if rows != HALF or width % SPAN or levels != 4:
        raise NotImplementedError("slab shape")
    nblocks = width // LANES
    both, half = 2 * rows, rows // 2
    count = lax.axis_size("row")
    chip = [(i, i ^ 1) for i in range(count) if i ^ 1 < count]
    away = [(i, j) for i in range(count) for j in [((i + 1) ^ 1) - 1] if 0 <= j < count]
    hbm = [pltpu.with_memory_space_constraint(x, pltpu.HBM) for x in (level_weight, innovation, background)]
    band = jnp.asarray(zonal_band())
    piece = jax.ShapeDtypeStruct((nblocks // PIECES, 2, both, LANES), BF16)
    result = jax.ShapeDtypeStruct((2, rows, width), F32)
    *raws, outer, row, inno, back, weight = pl.pallas_call(
        outer_kernel,
        out_shape=[piece] * PIECES
        + [
            jax.ShapeDtypeStruct((outer_rows(rows, nblocks, levels), LANES), BF16),
            jax.ShapeDtypeStruct((TILE, width), BF16),
            jax.ShapeDtypeStruct(innovation.shape, BF16),
            jax.ShapeDtypeStruct(background.shape, BF16),
            jax.ShapeDtypeStruct((2 * levels, 2 * LANES), F32),
        ],
        in_specs=[HBM] * 3,
        out_specs=[VMEM] * (PIECES + 5),
        scratch_shapes=[
            pltpu.SMEM((levels,), F32),
            pltpu.VMEM((SPAN, LANES), BF16),
            pltpu.SemaphoreType.DMA((2, QUARTERS)),
            pltpu.SemaphoreType.DMA((2,)),
            pltpu.SemaphoreType.DMA,
        ],
        compiler_params=PARAMS,
        name="outer_half",
    )(*hbm)
    outer_got = lax.ppermute(outer, "row", away)
    row = lax.ppermute(row, "row", chip)
    *raws, inner = pl.pallas_call(
        inner_kernel,
        out_shape=[piece] * PIECES + [jax.ShapeDtypeStruct((inner_rows(rows, nblocks), LANES), BF16)],
        in_specs=[VMEM] * (5 + PIECES),
        out_specs=[VMEM] * (PIECES + 1),
        scratch_shapes=[pltpu.VMEM((rows, width), BF16)],
        input_output_aliases={5 + k: k for k in range(PIECES)},
        compiler_params=PARAMS,
        name="inner_half",
    )(weight, inno, back, row, band, *raws)
    inner_got = lax.ppermute(inner, "row", away)
    nears = [lax.ppermute(r, "row", chip) for r in raws]
    edges = pl.pallas_call(
        outermost_kernel,
        out_shape=jax.ShapeDtypeStruct((TILE, width), BF16),
        in_specs=[VMEM] * 3,
        out_specs=VMEM,
        compiler_params=PARAMS,
        name="outermost_rows",
    )(weight, outer, outer_got)
    near_edges = lax.ppermute(edges, "row", chip)
    part = pl.pallas_call(
        near_kernel,
        out_shape=result,
        in_specs=[VMEM] * (2 * PIECES + 4),
        out_specs=VMEM,
        scratch_shapes=[pltpu.VMEM((nblocks, 2 * both, LANES), BF16)],
        compiler_params=PARAMS,
        name="near_part",
    )(*raws, *nears, edges, near_edges, outer_got, band)
    return pl.pallas_call(
        last_kernel,
        out_shape=result,
        in_specs=[VMEM] * 2,
        out_specs=HBM,
        scratch_shapes=[pltpu.VMEM((2, rows, width), F32), pltpu.SemaphoreType.DMA((nblocks // 2,))],
        compiler_params=PARAMS,
        name="last_part",
    )(part, inner_got)


def solution(mesh):
    placed = (P("member", "row", None), P("member", "row", None), P())
    return jax.shard_map(
        body, mesh=mesh, in_specs=placed, out_specs=P("member", "row", None), check_vma=False
    )
```

```python
import math

import jax
import jax.numpy as jnp
import numpy as np
from jax import lax
from jax.experimental import pallas as pl
from jax.experimental.pallas import tpu as pltpu
from jax.sharding import PartitionSpec as P

HALF = 64
SIGMA = 64
LANES = 128
TILE = 16
SHIFT_Y, SHIFT_X, SHIFT_Z = 2, 3, 4
SPAN = LANES << SHIFT_X
PACK = 4
CUTS = (0, 8, 16)
PIECES = 4
F32 = jnp.float32
BF16 = jnp.bfloat16
NORM = math.sqrt(sum(math.exp(-k * k / (SIGMA * SIGMA)) for k in range(-HALF, HALF + 1)))

VMEM = pl.BlockSpec(memory_space=pltpu.VMEM)
HBM = pl.BlockSpec(memory_space=pltpu.HBM)
PARAMS = pltpu.CompilerParams(vmem_limit_bytes=40 * 1024 * 1024)


def split(values):
    high = values.astype(BF16)
    return high, (values - high.astype(F32)).astype(BF16)


def dot(left, right):
    return jnp.dot(left, right, preferred_element_type=F32)


def iota(shape, dim):
    return lax.broadcasted_iota(jnp.int32, shape, dim)


def one_hot(mask, value=1.0):
    return jnp.where(mask, value, 0.0).astype(BF16)


def difference(off):
    return (jnp.where(off == 1, 1.0, 0.0) - jnp.where(off == -1, 1.0, 0.0)).astype(BF16)


def taps(offset):
    off = offset.astype(F32)
    value = jnp.exp(off * off * (-0.5 / (SIGMA * SIGMA))) * (1.0 / NORM)
    return jnp.where(jnp.abs(offset) <= HALF, value, 0.0)


def zonal_band():
    offset = np.arange(4 * LANES)[:, None] - LANES - np.arange(2 * LANES)[None, :]
    band = np.exp(-offset * offset / (2.0 * SIGMA * SIGMA)) / NORM
    band = np.where(np.abs(offset) <= HALF, band, 0.0).astype(np.float32)
    high = band.astype(BF16)
    return np.stack([high, (band - high.astype(np.float32)).astype(BF16)])


def window(first, nblocks):
    low, high = max(first - 1, 0), min(first + 3, nblocks)
    return low, high, (low - first + 1) * LANES, (high - first + 1) * LANES


def smooth_x(band_ref, load, first, nblocks):
    low, high, top, bottom = window(first, nblocks)
    both = jnp.concatenate([load(k) for k in range(low, high)], axis=1)
    rows = both.shape[0] // 2
    found = dot(both, band_ref[0, top:bottom, :])
    return found[:rows] + found[rows:] + dot(both[:rows], band_ref[1, top:bottom, :])


def parity():
    return lax.rem(lax.axis_index("row"), 2)


def block_of(refs, k):
    per = refs[0].shape[0]
    return refs[k // per].at[k % per]


def tile_at(row):
    return pl.ds(pl.multiple_of(row, TILE), TILE)


def half_of(ref, comp_rows, start, part):
    half = comp_rows // 2
    return [ref[part, pl.ds(pl.multiple_of(comp * comp_rows + start, TILE), half), :] for comp in range(2)]


def raw_pair(first, weight, inno_ref, back_ref, upper, diff_y, diff_x, extra, raw_refs):
    levels, rows, width = inno_ref.shape
    half = rows // 2
    start = pl.multiple_of(jnp.where(upper, 0, half), TILE)
    exact = pl.ds(start, half)
    deep = pl.ds(pl.multiple_of(jnp.where(upper, 0, half - TILE), TILE), half + TILE)
    here = pl.ds(first * LANES, 2 * LANES)
    low, high, top, bottom = window(first, width // LANES)
    around = back_ref[:, exact, low * LANES : high * LANES]
    grad_xs = dot(around.reshape(levels * half, -1), diff_x[top:bottom])
    numer_y = numer_x = 0.0
    denom = 1.0
    for level in range(levels):
        grad_y = dot(diff_y, back_ref[level, deep, here])
        if extra is not None:
            grad_y += extra(level, here)
        grad_x = grad_xs[level * half : (level + 1) * half]
        scaled = inno_ref[level, exact, here].astype(F32) * (0.5 * weight(level))
        numer_y += scaled * grad_y
        numer_x += scaled * grad_x
        denom += (0.25 * weight(level)) * (grad_y * grad_y + grad_x * grad_x)
    inverse = 1.0 / denom
    if extra is None:
        inverse = jnp.where(iota(inverse.shape, 0) == jnp.where(upper, 0, half - 1), 0.0, inverse)
    found = []
    for comp, numer in enumerate((numer_y, numer_x)):
        raw = numer * inverse
        found.append(split(raw))
        at = pl.ds(pl.multiple_of(comp * rows + start, TILE), half)
        for part, values in enumerate(found[-1]):
            for j in range(2):
                block_of(raw_refs, first + j)[part, at, :] = values[:, j * LANES : (j + 1) * LANES]
    return found


def differences(upper, half):
    deep = half + TILE
    diff_y = difference(iota((half, deep), 1) - iota((half, deep), 0) - jnp.where(upper, 0, TILE))
    shape = (4 * LANES, 2 * LANES)
    return diff_y, difference(iota(shape, 0) - LANES - iota(shape, 1))


def outer_kernel(lw_hbm, inno_hbm, back_hbm, *refs):
    *raw_refs, msg_ref, row_ref, inno_ref, back_ref, weight_ref, lw_ref, sum_ref, sems, rest_sems, lw_sem = refs
    levels, rows, width = inno_ref.shape
    half = rows // 2
    deep = half + TILE
    nblocks = width // LANES
    upper = parity() == 0
    start = jnp.where(upper, 0, half)
    cuts = [cut * nblocks // CUTS[-1] * LANES for cut in CUTS]

    def bring(sem, which, at, size, cols):
        index = (slice(None), pl.ds(pl.multiple_of(at, TILE), size), cols)
        source, target = ((inno_hbm, inno_ref), (back_hbm, back_ref))[which]
        return pltpu.make_async_copy(source.at[index], target.at[index], sem)

    weights = pltpu.make_async_copy(lw_hbm, lw_ref, lw_sem)
    copies = []
    for q, cut in enumerate(cuts[:-1]):
        cols = pl.ds(cut, cuts[q + 1] - cut)
        copies.append(
            [
                bring(sems.at[1, q], 1, jnp.where(upper, 0, rows - deep), deep, cols),
                bring(sems.at[0, q], 0, start, half, cols),
            ]
        )
    copies[-1].append(bring(rest_sems.at[1], 1, jnp.where(upper, deep, 0), rows - deep, pl.ds(0, width)))
    other = bring(rest_sems.at[0], 0, half - start, half, pl.ds(0, width))
    weights.start()
    for copy in sum(copies, []) + [other]:
        copy.start()
    diff_y, diff_x = differences(upper, half)
    sum_ref[...] = one_hot(iota(sum_ref.shape, 0) >> SHIFT_X == iota(sum_ref.shape, 1))
    groups = rows >> SHIFT_Y
    shape = (groups, rows)
    sum_y = one_hot(iota(shape, 1) >> SHIFT_Y == iota(shape, 0))
    weights.wait()
    waited = 0
    at = nblocks * rows
    for first in range(0, nblocks, 2):
        while cuts[waited] < window(first, nblocks)[1] * LANES:
            for copy in copies[waited]:
                copy.wait()
            waited += 1
        found = raw_pair(first, lambda k: lw_ref[k], inno_ref, back_ref, upper, diff_y, diff_x, None, raw_refs)
        for comp, (high, _) in enumerate(found):
            for j in range(2):
                msg_ref[pl.ds((first + j) * rows + comp * half, half), :] = high[:, j * LANES : (j + 1) * LANES]
    totals = []
    for span in range(0, nblocks, SPAN // LANES):
        blocks = range(span, span + SPAN // LANES)
        lows = [jnp.concatenate(half_of(block_of(raw_refs, k), rows, start, 1), axis=0) for k in blocks]
        totals.append(dot(jnp.concatenate(lows, axis=1), sum_ref[...]))
    for total in totals:
        msg_ref[pl.ds(at, groups), :] = dot(sum_y, total.astype(BF16)).astype(BF16)
        at += groups
    kinds = 3 * levels
    shape = (PACK * kinds, PACK * levels * TILE)
    row, col = iota(shape, 0), iota(shape, 1)
    want = row - (col >> 6) * kinds
    level = (col >> 4) & (levels - 1)
    place = col & (TILE - 1)
    outermost = place == jnp.where(upper, 0, TILE - 1)
    next_row = place == jnp.where(upper, 1, TILE - 2)
    of_back = one_hot(((want == level) & outermost) | ((want == levels + level) & next_row))
    of_inno = one_hot((want == 2 * levels + level) & outermost)
    edge_at = tile_at(jnp.where(upper, 0, rows - TILE))
    for first in range(0, nblocks, PACK):
        back, inno = [], []
        for k in range(first, first + PACK):
            here = pl.ds(k * LANES, LANES)
            back.append(back_ref[:, edge_at, here].reshape(levels * TILE, LANES))
            inno.append(inno_ref[:, edge_at, here].reshape(levels * TILE, LANES))
        tile = dot(of_back, jnp.concatenate(back, axis=0)) + dot(of_inno, jnp.concatenate(inno, axis=0))
        msg_ref[pl.ds(at, PACK * kinds), :] = tile.astype(BF16)
        at += PACK * kinds
    for level in range(2 * levels):
        weight_ref[level : level + 1, :] = jnp.full((1, weight_ref.shape[1]), lw_ref[level % levels])
    shape = (TILE, levels * TILE)
    pick = one_hot(iota(shape, 1) == iota(shape, 0) * TILE + jnp.where(upper, TILE - 1, 0))
    near_rows = back_ref[:, tile_at(jnp.where(upper, rows - TILE, 0)), :]
    row_ref[...] = dot(pick, near_rows.reshape(levels * TILE, -1)).astype(BF16)
    other.wait()


def outer_rows(rows, nblocks, levels):
    return nblocks * rows + (nblocks * LANES // SPAN) * (rows >> SHIFT_Y) + nblocks * 3 * levels


def inner_kernel(weight_ref, inno_ref, back_ref, row_ref, band_ref, *refs):
    raw_refs = refs[PIECES : 2 * PIECES]
    msg_ref, rest_ref = refs[2 * PIECES :]
    _, rows, width = inno_ref.shape
    half = rows // 2
    nblocks = width // LANES
    upper = parity() == 1
    start = jnp.where(upper, 0, half)
    diff_y, diff_x = differences(upper, half)
    at = iota((half, 2 * LANES), 0) == jnp.where(upper, 0, half - 1)
    sign = jnp.where(upper, -1.0, 1.0)

    def extra(level, here):
        return jnp.where(at, row_ref[level : level + 1, here].astype(F32) * sign, 0.0)

    def weight(level):
        return weight_ref[level : level + 1, :]

    def load(k):
        block = block_of(raw_refs, k)
        return jnp.concatenate(half_of(block, rows, start, 0) + half_of(block, rows, start, 1), axis=0)

    groups = rows >> SHIFT_Z
    shape = (2 * groups, rows)
    sum_y = one_hot(iota(shape, 1) >> SHIFT_Z == iota(shape, 0))
    for first in range(0, nblocks, 2):
        raw_pair(first, weight, inno_ref, back_ref, upper, diff_y, diff_x, extra, raw_refs)
    for first in range(0, nblocks, 2):
        high, low = split(smooth_x(band_ref, load, first, nblocks))
        rest_ref[:, first * LANES : (first + 2) * LANES] = low
        for j in range(2):
            msg_ref[pl.ds((first + j) * rows, rows), :] = high[:, j * LANES : (j + 1) * LANES]
    sums = dot(sum_y, rest_ref[...])
    per = TILE // groups
    for first in range(0, nblocks, 2 * per):
        for j in range(2):
            parts = [sums[:groups, k * LANES : (k + 1) * LANES] for k in range(first + j, first + 2 * per, 2)]
            tile = nblocks * rows + (first // per + j) * TILE
            msg_ref[pl.ds(tile, TILE), :] = jnp.concatenate(parts, axis=0).astype(BF16)


def inner_rows(rows, nblocks):
    return nblocks * rows + nblocks * (rows >> SHIFT_Z)


def outermost_kernel(weight_ref, own_ref, got_ref, out_ref):
    nblocks = out_ref.shape[1] // LANES
    levels = weight_ref.shape[0] // 2
    kinds = 3 * levels
    base = own_ref.shape[0] - nblocks * kinds

    def unpacked(ref):
        packs = [ref[pl.ds(base + k * kinds, PACK * kinds), :].astype(F32) for k in range(0, nblocks, PACK)]
        return [
            jnp.concatenate(
                [p[j * kinds + kind * levels : j * kinds + (kind + 1) * levels] for p in packs for j in range(PACK)], axis=1
            )
            for kind in range(3)
        ]

    own, got = unpacked(own_ref), unpacked(got_ref)
    here = jnp.concatenate([own[0], got[0]], axis=0)
    beyond = jnp.concatenate([got[0], own[0]], axis=0)
    before = jnp.concatenate([own[1], got[1]], axis=0)
    inno = jnp.concatenate([own[2], got[2]], axis=0)
    shape = here.shape
    first_core = parity() == 0
    grad_y = jnp.where((iota(shape, 0) < levels) == first_core, before - beyond, beyond - before)
    lane = iota(shape, 1)
    left = jnp.where(lane == 0, 0.0, pltpu.roll(here, 1, 1))
    right = jnp.where(lane == shape[1] - 1, 0.0, pltpu.roll(here, shape[1] - 1, 1))
    grad_x = right - left
    weight = jnp.concatenate([weight_ref[:, :LANES]] * nblocks, axis=1)
    scaled = inno * (0.5 * weight)

    def total(values):
        return [sum(values[k : k + 1] for k in range(f, f + levels)) for f in (0, levels)]

    numer_y, numer_x = total(scaled * grad_y), total(scaled * grad_x)
    denom = total((0.25 * weight) * (grad_y * grad_y + grad_x * grad_x))
    found = []
    for k in range(2):
        inverse = 1.0 / (1.0 + denom[k])
        found += [numer_y[k] * inverse, numer_x[k] * inverse]
    high, low = split(jnp.concatenate(found, axis=0))
    none = jnp.zeros((TILE - 8, shape[1]), F32)
    out_ref[...] = jnp.concatenate([high.astype(F32), low.astype(F32), none], axis=0).astype(BF16)


def far_taps(rows, towards):
    side = 2 * parity() - 1
    half = rows // 2
    start = jnp.where((side < 0) == towards, half, 0)
    return taps(iota((rows, half), 1) + start - iota((rows, half), 0) + side * rows)


def near_kernel(*refs):
    raw_refs, near_refs = refs[:PIECES], refs[PIECES : 2 * PIECES]
    edges_ref, near_edges_ref, msg_ref, band_ref, out_ref, taps_ref, total_ref = refs[2 * PIECES :]
    _, rows, width = out_ref.shape
    nblocks = width // LANES
    half = rows // 2
    par = parity()
    side = 1 - 2 * par
    offset = iota((rows, rows), 1) - iota((rows, rows), 0)
    near_taps = jnp.concatenate([taps(offset), taps(offset + side * rows)], axis=1)
    near_high = near_taps.astype(BF16)
    toward = far_taps(rows, True)
    shape = (rows, TILE)
    kind = iota(shape, 1)
    own_at = jnp.where(par == 0, 0, rows - 1)
    far_at = jnp.where(par == 0, -1, rows)
    near_at = jnp.where(par == 0, 2 * rows - 1, -rows)
    own_edges = taps(jnp.where(kind & 2 == 0, own_at, far_at) - iota(shape, 0))
    near_edges = jnp.where(kind & 2 == 0, taps(near_at - iota(shape, 0)), 0.0)
    stacked = []
    for comp in range(2):
        here = (kind < 8) & (kind & 1 == comp)
        all_taps = [near_taps, toward, jnp.where(here, own_edges, 0.0), jnp.where(here, near_edges, 0.0)]
        stacked.append(jnp.concatenate(split(jnp.concatenate(all_taps, axis=1)), axis=0))
    groups = half >> SHIFT_Y
    shape = (half, groups)
    mean_y = one_hot(iota(shape, 0) >> SHIFT_Y == iota(shape, 1), 1.0 / (1 << SHIFT_Y))
    group_taps = dot(toward.astype(BF16), mean_y).astype(BF16)
    shape = (LANES, SPAN)
    mean_x = one_hot(iota(shape, 1) >> SHIFT_X == iota(shape, 0), 1.0 / (1 << SHIFT_X))
    rest = []
    for span in range(width // SPAN):
        tile = msg_ref[pl.ds(nblocks * rows + span * 2 * groups, 2 * groups), :]
        rest.append(jnp.concatenate([dot(group_taps, tile[:groups]), dot(group_taps, tile[groups:])], axis=0).astype(BF16))
    for first in range(0, nblocks, 2):
        cols = pl.ds(first * LANES, 2 * LANES)
        place = first * LANES % SPAN
        spread = dot(rest[first * LANES // SPAN], mean_x[:, place : place + 2 * LANES])
        edges = [edges_ref[:, cols], near_edges_ref[:, cols]]
        for comp in range(2):
            here = pl.ds(comp * rows, rows)
            highs, lows = [], []
            for k in (first, first + 1):
                both = (block_of(raw_refs, k), block_of(near_refs, k))
                got = msg_ref[pl.ds(k * rows + comp * half, half), :]
                highs.append(jnp.concatenate([ref[0, here, :] for ref in both] + [got], axis=0))
                lows.append(jnp.concatenate([ref[1, here, :] for ref in both], axis=0))
            part = dot(stacked[comp], jnp.concatenate([jnp.concatenate(highs, axis=1)] + edges, axis=0))
            part = part[:rows] + part[rows:] + dot(near_high, jnp.concatenate(lows, axis=1))
            high, low = split(part + spread[comp * rows : (comp + 1) * rows])
            for j in range(2):
                cut = slice(j * LANES, (j + 1) * LANES)
                total_ref[first + j, pl.ds(comp * rows, rows), :] = high[:, cut]
                total_ref[first + j, pl.ds((2 + comp) * rows, rows), :] = low[:, cut]
    for first in range(0, nblocks, 2):
        result = smooth_x(band_ref, lambda k: total_ref[k], first, nblocks)
        here = pl.ds(first * LANES, 2 * LANES)
        out_ref[0, :, here] = result[:rows]
        out_ref[1, :, here] = result[rows:]
    for index, matrix in enumerate(last_taps(rows)):
        taps_ref[index] = matrix


def last_taps(rows):
    half = rows // 2
    away = far_taps(rows, False)
    high, low = split(away)
    groups = rows >> SHIFT_Z
    shape = (half, TILE)
    found = []
    for place in range(TILE // groups):
        for comp in range(2):
            of_group = (iota(shape, 0) >> SHIFT_Z) + place * groups + comp * (groups // 2) == iota(shape, 1)
            mean = dot(high, one_hot(of_group, 1.0 / (1 << SHIFT_Z))).astype(BF16)
            found.append(jnp.concatenate([high, low, mean], axis=1))
    return found


def last_kernel(taps_ref, part_ref, msg_ref, out_hbm, buf, sem):
    _, rows, width = part_ref.shape
    nblocks = width // LANES
    half = rows // 2
    places = TILE // (rows >> SHIFT_Z)
    copies = []
    for index, first in enumerate(range(0, nblocks, 2)):
        here = pl.ds(first * LANES, 2 * LANES)
        tiles = [
            msg_ref[pl.ds(nblocks * rows + (2 * (index // places) + j) * TILE, TILE), :] for j in range(2)
        ]
        sums = jnp.concatenate(tiles, axis=1)
        for comp in range(2):
            got = [msg_ref[pl.ds((first + j) * rows + comp * half, half), :] for j in range(2)]
            got = jnp.concatenate(got, axis=1)
            part = dot(taps_ref[index % places * 2 + comp], jnp.concatenate([got, got, sums], axis=0))
            buf[comp, :, here] = part_ref[comp, :, here] + part
        copy = pltpu.make_async_copy(buf.at[:, :, here], out_hbm.at[:, :, here], sem.at[index])
        copy.start()
        copies.append(copy)
    for copy in copies:
        copy.wait()


def body(innovation, background, level_weight):
    levels, rows, width = innovation.shape
    if rows != HALF or width % SPAN or levels != 4:
        raise NotImplementedError("slab shape")
    nblocks = width // LANES
    both, half = 2 * rows, rows // 2
    count = lax.axis_size("row")
    chip = [(i, i ^ 1) for i in range(count) if i ^ 1 < count]
    away = [(i, j) for i in range(count) for j in [((i + 1) ^ 1) - 1] if 0 <= j < count]
    hbm = [pltpu.with_memory_space_constraint(x, pltpu.HBM) for x in (level_weight, innovation, background)]
    band = jnp.asarray(zonal_band())
    piece = jax.ShapeDtypeStruct((nblocks // PIECES, 2, both, LANES), BF16)
    result = jax.ShapeDtypeStruct((2, rows, width), F32)
    *raws, outer, row, inno, back, weight = pl.pallas_call(
        outer_kernel,
        out_shape=[piece] * PIECES
        + [
            jax.ShapeDtypeStruct((outer_rows(rows, nblocks, levels), LANES), BF16),
            jax.ShapeDtypeStruct((TILE, width), BF16),
            jax.ShapeDtypeStruct(innovation.shape, BF16),
            jax.ShapeDtypeStruct(background.shape, BF16),
            jax.ShapeDtypeStruct((2 * levels, 2 * LANES), F32),
        ],
        in_specs=[HBM] * 3,
        out_specs=[VMEM] * (PIECES + 5),
        scratch_shapes=[
            pltpu.SMEM((levels,), F32),
            pltpu.VMEM((SPAN, LANES), BF16),
            pltpu.SemaphoreType.DMA((2, len(CUTS) - 1)),
            pltpu.SemaphoreType.DMA((2,)),
            pltpu.SemaphoreType.DMA,
        ],
        compiler_params=PARAMS,
        name="outer_half",
    )(*hbm)
    outer_got = lax.ppermute(outer, "row", away)
    row = lax.ppermute(row, "row", chip)
    *raws, inner = pl.pallas_call(
        inner_kernel,
        out_shape=[piece] * PIECES + [jax.ShapeDtypeStruct((inner_rows(rows, nblocks), LANES), BF16)],
        in_specs=[VMEM] * (5 + PIECES),
        out_specs=[VMEM] * (PIECES + 1),
        scratch_shapes=[pltpu.VMEM((rows, width), BF16)],
        input_output_aliases={5 + k: k for k in range(PIECES)},
        compiler_params=PARAMS,
        name="inner_half",
    )(weight, inno, back, row, band, *raws)
    inner_got = lax.ppermute(inner, "row", away)
    nears = [lax.ppermute(r, "row", chip) for r in raws]
    edges = pl.pallas_call(
        outermost_kernel,
        out_shape=jax.ShapeDtypeStruct((TILE, width), BF16),
        in_specs=[VMEM] * 3,
        out_specs=VMEM,
        compiler_params=PARAMS,
        name="outermost_rows",
    )(weight, outer, outer_got)
    near_edges = lax.ppermute(edges, "row", chip)
    part, last = pl.pallas_call(
        near_kernel,
        out_shape=[result, jax.ShapeDtypeStruct((2 * TILE // (rows >> SHIFT_Z), rows, rows + TILE), BF16)],
        in_specs=[VMEM] * (2 * PIECES + 4),
        out_specs=[VMEM] * 2,
        scratch_shapes=[pltpu.VMEM((nblocks, 2 * both, LANES), BF16)],
        compiler_params=PARAMS,
        name="near_part",
    )(*raws, *nears, edges, near_edges, outer_got, band)
    return pl.pallas_call(
        last_kernel,
        out_shape=result,
        in_specs=[VMEM] * 3,
        out_specs=HBM,
        scratch_shapes=[pltpu.VMEM((2, rows, width), F32), pltpu.SemaphoreType.DMA((nblocks // 2,))],
        compiler_params=PARAMS,
        name="last_part",
    )(last, part, inner_got)


def solution(mesh):
    placed = (P("member", "row", None), P("member", "row", None), P())
    return jax.shard_map(
        body, mesh=mesh, in_specs=placed, out_specs=P("member", "row", None), check_vma=False
    )
```

```python
import math

import jax
import jax.numpy as jnp
import numpy as np
from jax import lax
from jax.experimental import pallas as pl
from jax.experimental.pallas import tpu as pltpu
from jax.sharding import PartitionSpec as P

HALF = 64
SIGMA = 64
LANES = 128
TILE = 16
SHIFT_Y, SHIFT_X, SHIFT_Z = 2, 3, 4
SPAN = LANES << SHIFT_X
PACK = 8
CUTS = (0, 8, 16)
PIECES = 4
F32 = jnp.float32
BF16 = jnp.bfloat16
NORM = math.sqrt(sum(math.exp(-k * k / (SIGMA * SIGMA)) for k in range(-HALF, HALF + 1)))

VMEM = pl.BlockSpec(memory_space=pltpu.VMEM)
HBM = pl.BlockSpec(memory_space=pltpu.HBM)
PARAMS = pltpu.CompilerParams(vmem_limit_bytes=40 * 1024 * 1024)


def split(values):
    high = values.astype(BF16)
    return high, (values - high.astype(F32)).astype(BF16)


def dot(left, right):
    return jnp.dot(left, right, preferred_element_type=F32)


def iota(shape, dim):
    return lax.broadcasted_iota(jnp.int32, shape, dim)


def one_hot(mask, value=1.0):
    return jnp.where(mask, value, 0.0).astype(BF16)


def difference(off):
    return (jnp.where(off == 1, 1.0, 0.0) - jnp.where(off == -1, 1.0, 0.0)).astype(BF16)


def taps(offset):
    off = offset.astype(F32)
    value = jnp.exp(off * off * (-0.5 / (SIGMA * SIGMA))) * (1.0 / NORM)
    return jnp.where(jnp.abs(offset) <= HALF, value, 0.0)


def zonal_band():
    offset = np.arange(4 * LANES)[:, None] - LANES - np.arange(2 * LANES)[None, :]
    band = np.exp(-offset * offset / (2.0 * SIGMA * SIGMA)) / NORM
    band = np.where(np.abs(offset) <= HALF, band, 0.0).astype(np.float32)
    high = band.astype(BF16)
    return np.stack([high, (band - high.astype(np.float32)).astype(BF16)])


def window(first, nblocks):
    low, high = max(first - 1, 0), min(first + 3, nblocks)
    return low, high, (low - first + 1) * LANES, (high - first + 1) * LANES


def smooth_x(band_ref, load, first, nblocks):
    low, high, top, bottom = window(first, nblocks)
    both = jnp.concatenate([load(k) for k in range(low, high)], axis=1)
    rows = both.shape[0] // 2
    found = dot(both, band_ref[0, top:bottom, :])
    return found[:rows] + found[rows:] + dot(both[:rows], band_ref[1, top:bottom, :])


def parity():
    return lax.rem(lax.axis_index("row"), 2)


def block_of(refs, k):
    per = refs[0].shape[0]
    return refs[k // per].at[k % per]


def tile_at(row):
    return pl.ds(pl.multiple_of(row, TILE), TILE)


def half_of(ref, comp_rows, start, part):
    half = comp_rows // 2
    return [ref[part, pl.ds(pl.multiple_of(comp * comp_rows + start, TILE), half), :] for comp in range(2)]


def raw_pair(first, weight, inno_ref, back_ref, upper, diff_y, diff_x, extra, raw_refs):
    levels, rows, width = inno_ref.shape
    half = rows // 2
    start = pl.multiple_of(jnp.where(upper, 0, half), TILE)
    exact = pl.ds(start, half)
    deep = pl.ds(pl.multiple_of(jnp.where(upper, 0, half - TILE), TILE), half + TILE)
    here = pl.ds(first * LANES, 2 * LANES)
    low, high, top, bottom = window(first, width // LANES)
    around = back_ref[:, exact, low * LANES : high * LANES]
    grad_xs = dot(around.reshape(levels * half, -1), diff_x[top:bottom])
    numer_y = numer_x = 0.0
    denom = 1.0
    for level in range(levels):
        grad_y = dot(diff_y, back_ref[level, deep, here])
        if extra is not None:
            grad_y += extra(level, here)
        grad_x = grad_xs[level * half : (level + 1) * half]
        scaled = inno_ref[level, exact, here].astype(F32) * (0.5 * weight(level))
        numer_y += scaled * grad_y
        numer_x += scaled * grad_x
        denom += (0.25 * weight(level)) * (grad_y * grad_y + grad_x * grad_x)
    inverse = 1.0 / denom
    found = []
    for comp, numer in enumerate((numer_y, numer_x)):
        raw = numer * inverse
        if extra is None:
            other = inno_ref[comp, exact, here].astype(F32)
            raw = jnp.where(iota(raw.shape, 0) == jnp.where(upper, 0, half - 1), other, raw)
        found.append(split(raw))
        at = pl.ds(pl.multiple_of(comp * rows + start, TILE), half)
        for part, values in enumerate(found[-1]):
            for j in range(2):
                block_of(raw_refs, first + j)[part, at, :] = values[:, j * LANES : (j + 1) * LANES]
    return found


def differences(upper, half):
    deep = half + TILE
    diff_y = difference(iota((half, deep), 1) - iota((half, deep), 0) - jnp.where(upper, 0, TILE))
    shape = (4 * LANES, 2 * LANES)
    return diff_y, difference(iota(shape, 0) - LANES - iota(shape, 1))


def outer_kernel(lw_hbm, inno_hbm, back_hbm, *refs):
    *raw_refs, msg_ref, row_ref, inno_ref, back_ref, weight_ref, lw_ref, sum_ref, sems, rest_sems, lw_sem = refs
    levels, rows, width = inno_ref.shape
    half = rows // 2
    deep = half + TILE
    nblocks = width // LANES
    upper = parity() == 0
    start = jnp.where(upper, 0, half)
    cuts = [cut * nblocks // CUTS[-1] * LANES for cut in CUTS]

    def bring(sem, which, at, size, cols):
        index = (slice(None), pl.ds(pl.multiple_of(at, TILE), size), cols)
        source, target = ((inno_hbm, inno_ref), (back_hbm, back_ref))[which]
        return pltpu.make_async_copy(source.at[index], target.at[index], sem)

    weights = pltpu.make_async_copy(lw_hbm, lw_ref, lw_sem)
    copies = []
    for q, cut in enumerate(cuts[:-1]):
        cols = pl.ds(cut, cuts[q + 1] - cut)
        copies.append(
            [
                bring(sems.at[1, q], 1, jnp.where(upper, 0, rows - deep), deep, cols),
                bring(sems.at[0, q], 0, start, half, cols),
            ]
        )
    copies[-1].append(bring(rest_sems.at[1], 1, jnp.where(upper, deep, 0), rows - deep, pl.ds(0, width)))
    other = bring(rest_sems.at[0], 0, half - start, half, pl.ds(0, width))
    weights.start()
    for copy in sum(copies, []) + [other]:
        copy.start()
    diff_y, diff_x = differences(upper, half)
    sum_ref[...] = one_hot(iota(sum_ref.shape, 0) >> SHIFT_X == iota(sum_ref.shape, 1))
    groups = rows >> SHIFT_Y
    shape = (groups, rows)
    sum_y = one_hot(iota(shape, 1) >> SHIFT_Y == iota(shape, 0))
    weights.wait()
    waited = 0
    at = nblocks * rows
    for first in range(0, nblocks, 2):
        while cuts[waited] < window(first, nblocks)[1] * LANES:
            for copy in copies[waited]:
                copy.wait()
            waited += 1
        found = raw_pair(first, lambda k: lw_ref[k], inno_ref, back_ref, upper, diff_y, diff_x, None, raw_refs)
        for comp, (high, _) in enumerate(found):
            for j in range(2):
                msg_ref[pl.ds((first + j) * rows + comp * half, half), :] = high[:, j * LANES : (j + 1) * LANES]
    totals = []
    for span in range(0, nblocks, SPAN // LANES):
        blocks = range(span, span + SPAN // LANES)
        lows = [jnp.concatenate(half_of(block_of(raw_refs, k), rows, start, 1), axis=0) for k in blocks]
        totals.append(dot(jnp.concatenate(lows, axis=1), sum_ref[...]))
    for total in totals:
        msg_ref[pl.ds(at, groups), :] = dot(sum_y, total.astype(BF16)).astype(BF16)
        at += groups
    kinds = 3 * levels - 2
    shape = (PACK * kinds, PACK * levels * TILE)
    row, col = iota(shape, 0), iota(shape, 1)
    want = row - (col >> 6) * kinds
    level = (col >> 4) & (levels - 1)
    place = col & (TILE - 1)
    outermost = place == jnp.where(upper, 0, TILE - 1)
    next_row = place == jnp.where(upper, 1, TILE - 2)
    of_back = one_hot(((want == level) & outermost) | ((want == levels + level) & next_row))
    of_inno = one_hot((want == 2 * levels + level - 2) & (level >= 2) & outermost)
    edge_at = tile_at(jnp.where(upper, 0, rows - TILE))
    for first in range(0, nblocks, PACK):
        back, inno = [], []
        for k in range(first, first + PACK):
            here = pl.ds(k * LANES, LANES)
            back.append(back_ref[:, edge_at, here].reshape(levels * TILE, LANES))
            inno.append(inno_ref[:, edge_at, here].reshape(levels * TILE, LANES))
        tile = dot(of_back, jnp.concatenate(back, axis=0)) + dot(of_inno, jnp.concatenate(inno, axis=0))
        msg_ref[pl.ds(at, PACK * kinds), :] = tile.astype(BF16)
        at += PACK * kinds
    for level in range(2 * levels):
        weight_ref[level : level + 1, :] = jnp.full((1, weight_ref.shape[1]), lw_ref[level % levels])
    shape = (TILE, levels * TILE)
    pick = one_hot(iota(shape, 1) == iota(shape, 0) * TILE + jnp.where(upper, TILE - 1, 0))
    near_rows = back_ref[:, tile_at(jnp.where(upper, rows - TILE, 0)), :]
    row_ref[...] = dot(pick, near_rows.reshape(levels * TILE, -1)).astype(BF16)
    other.wait()


def outer_rows(rows, nblocks, levels):
    return nblocks * rows + (nblocks * LANES // SPAN) * (rows >> SHIFT_Y) + nblocks * (3 * levels - 2)


def inner_kernel(weight_ref, inno_ref, back_ref, row_ref, band_ref, *refs):
    raw_refs = refs[PIECES : 2 * PIECES]
    msg_ref, rest_ref = refs[2 * PIECES :]
    _, rows, width = inno_ref.shape
    half = rows // 2
    nblocks = width // LANES
    upper = parity() == 1
    start = jnp.where(upper, 0, half)
    diff_y, diff_x = differences(upper, half)
    at = iota((half, 2 * LANES), 0) == jnp.where(upper, 0, half - 1)
    sign = jnp.where(upper, -1.0, 1.0)

    def extra(level, here):
        return jnp.where(at, row_ref[level : level + 1, here].astype(F32) * sign, 0.0)

    def weight(level):
        return weight_ref[level : level + 1, :]

    def load(k):
        block = block_of(raw_refs, k)
        return jnp.concatenate(half_of(block, rows, start, 0) + half_of(block, rows, start, 1), axis=0)

    groups = rows >> SHIFT_Z
    shape = (2 * groups, rows)
    sum_y = one_hot(iota(shape, 1) >> SHIFT_Z == iota(shape, 0))
    for first in range(0, nblocks, 2):
        raw_pair(first, weight, inno_ref, back_ref, upper, diff_y, diff_x, extra, raw_refs)
    for first in range(0, nblocks, 2):
        high, low = split(smooth_x(band_ref, load, first, nblocks))
        rest_ref[:, first * LANES : (first + 2) * LANES] = low
        for j in range(2):
            msg_ref[pl.ds((first + j) * rows, rows), :] = high[:, j * LANES : (j + 1) * LANES]
    sums = dot(sum_y, rest_ref[...])
    per = TILE // groups
    for first in range(0, nblocks, 2 * per):
        for j in range(2):
            parts = [sums[:groups, k * LANES : (k + 1) * LANES] for k in range(first + j, first + 2 * per, 2)]
            tile = nblocks * rows + (first // per + j) * TILE
            msg_ref[pl.ds(tile, TILE), :] = jnp.concatenate(parts, axis=0).astype(BF16)


def inner_rows(rows, nblocks):
    return nblocks * rows + nblocks * (rows >> SHIFT_Z)


def outermost_kernel(weight_ref, own_ref, got_ref, out_ref):
    nblocks = out_ref.shape[1] // LANES
    levels = weight_ref.shape[0] // 2
    kinds = 3 * levels - 2
    base = own_ref.shape[0] - nblocks * kinds
    rows, half = HALF, HALF // 2
    first_core = parity() == 0
    at = iota((8, rows), 0) * half

    def unpacked(ref, upper):
        packs = [ref[pl.ds(base + k * kinds, PACK * kinds), :].astype(F32) for k in range(0, nblocks, PACK)]
        pick = one_hot((iota((8, rows), 1) == at + jnp.where(upper, 0, half - 1)) & (at < rows))
        some = []
        for k in range(0, nblocks, 2):
            pair = [ref[pl.ds((k + j) * rows, rows), :] for j in range(2)]
            some.append(dot(pick, jnp.concatenate(pair, axis=1))[:2])
        found = []
        for low, high in ((0, levels), (levels, 2 * levels), (2 * levels, kinds)):
            parts = [p[j * kinds + low : j * kinds + high] for p in packs for j in range(PACK)]
            found.append(jnp.concatenate(parts, axis=1))
        found[2] = jnp.concatenate([jnp.concatenate(some, axis=1), found[2]], axis=0)
        return found

    own, got = unpacked(own_ref, first_core), unpacked(got_ref, jnp.logical_not(first_core))
    here = jnp.concatenate([own[0], got[0]], axis=0)
    beyond = jnp.concatenate([got[0], own[0]], axis=0)
    before = jnp.concatenate([own[1], got[1]], axis=0)
    inno = jnp.concatenate([own[2], got[2]], axis=0)
    shape = here.shape
    grad_y = jnp.where((iota(shape, 0) < levels) == first_core, before - beyond, beyond - before)
    lane = iota(shape, 1)
    left = jnp.where(lane == 0, 0.0, pltpu.roll(here, 1, 1))
    right = jnp.where(lane == shape[1] - 1, 0.0, pltpu.roll(here, shape[1] - 1, 1))
    grad_x = right - left
    weight = jnp.concatenate([weight_ref[:, :LANES]] * nblocks, axis=1)
    scaled = inno * (0.5 * weight)

    def total(values):
        return [sum(values[k : k + 1] for k in range(f, f + levels)) for f in (0, levels)]

    numer_y, numer_x = total(scaled * grad_y), total(scaled * grad_x)
    denom = total((0.25 * weight) * (grad_y * grad_y + grad_x * grad_x))
    found = []
    for k in range(2):
        inverse = 1.0 / (1.0 + denom[k])
        found += [numer_y[k] * inverse, numer_x[k] * inverse]
    high, low = split(jnp.concatenate(found, axis=0))
    none = jnp.zeros((TILE - 8, shape[1]), F32)
    out_ref[...] = jnp.concatenate([high.astype(F32), low.astype(F32), none], axis=0).astype(BF16)


def far_taps(rows, towards):
    side = 2 * parity() - 1
    half = rows // 2
    start = jnp.where((side < 0) == towards, half, 0)
    return taps(iota((rows, half), 1) + start - iota((rows, half), 0) + side * rows)


def near_kernel(*refs):
    raw_refs, near_refs = refs[:PIECES], refs[PIECES : 2 * PIECES]
    edges_ref, near_edges_ref, msg_ref, band_ref, out_hbm, out_ref, taps_ref, total_ref, sem = refs[2 * PIECES :]
    _, rows, width = out_ref.shape
    nblocks = width // LANES
    half = rows // 2
    par = parity()
    side = 1 - 2 * par
    offset = iota((rows, rows), 1) - iota((rows, rows), 0)
    near_taps = jnp.concatenate([taps(offset), taps(offset + side * rows)], axis=1)
    column = iota(near_taps.shape, 1)
    outermost = (column == par * (rows - 1)) | (column == (2 - par) * rows - 1 + par)
    near_taps = jnp.where(outermost, 0.0, near_taps)
    near_high = near_taps.astype(BF16)
    toward = far_taps(rows, True)
    outermost = iota(toward.shape, 1) == jnp.where(par == 0, half - 1, 0)
    toward_inner = jnp.where(outermost, 0.0, toward)
    shape = (rows, TILE)
    kind = iota(shape, 1)
    own_at = jnp.where(par == 0, 0, rows - 1)
    far_at = jnp.where(par == 0, -1, rows)
    near_at = jnp.where(par == 0, 2 * rows - 1, -rows)
    own_edges = taps(jnp.where(kind & 2 == 0, own_at, far_at) - iota(shape, 0))
    near_edges = jnp.where(kind & 2 == 0, taps(near_at - iota(shape, 0)), 0.0)
    stacked = []
    for comp in range(2):
        here = (kind < 8) & (kind & 1 == comp)
        all_taps = [near_taps, toward_inner, jnp.where(here, own_edges, 0.0), jnp.where(here, near_edges, 0.0)]
        stacked.append(jnp.concatenate(split(jnp.concatenate(all_taps, axis=1)), axis=0))
    groups = half >> SHIFT_Y
    shape = (half, groups)
    mean_y = one_hot(iota(shape, 0) >> SHIFT_Y == iota(shape, 1), 1.0 / (1 << SHIFT_Y))
    group_taps = dot(toward.astype(BF16), mean_y).astype(BF16)
    shape = (LANES, SPAN)
    mean_x = one_hot(iota(shape, 1) >> SHIFT_X == iota(shape, 0), 1.0 / (1 << SHIFT_X))
    rest = []
    for span in range(width // SPAN):
        tile = msg_ref[pl.ds(nblocks * rows + span * 2 * groups, 2 * groups), :]
        rest.append(jnp.concatenate([dot(group_taps, tile[:groups]), dot(group_taps, tile[groups:])], axis=0).astype(BF16))
    for first in range(0, nblocks, 2):
        cols = pl.ds(first * LANES, 2 * LANES)
        place = first * LANES % SPAN
        spread = dot(rest[first * LANES // SPAN], mean_x[:, place : place + 2 * LANES])
        edges = [edges_ref[:, cols], near_edges_ref[:, cols]]
        for comp in range(2):
            here = pl.ds(comp * rows, rows)
            highs, lows = [], []
            for k in (first, first + 1):
                both = (block_of(raw_refs, k), block_of(near_refs, k))
                got = msg_ref[pl.ds(k * rows + comp * half, half), :]
                highs.append(jnp.concatenate([ref[0, here, :] for ref in both] + [got], axis=0))
                lows.append(jnp.concatenate([ref[1, here, :] for ref in both], axis=0))
            part = dot(stacked[comp], jnp.concatenate([jnp.concatenate(highs, axis=1)] + edges, axis=0))
            part = part[:rows] + part[rows:] + dot(near_high, jnp.concatenate(lows, axis=1))
            high, low = split(part + spread[comp * rows : (comp + 1) * rows])
            for j in range(2):
                cut = slice(j * LANES, (j + 1) * LANES)
                total_ref[first + j, pl.ds(comp * rows, rows), :] = high[:, cut]
                total_ref[first + j, pl.ds((2 + comp) * rows, rows), :] = low[:, cut]
    for first in range(0, nblocks, 2):
        result = smooth_x(band_ref, lambda k: total_ref[k], first, nblocks)
        here = pl.ds(first * LANES, 2 * LANES)
        out_ref[0, :, here] = result[:rows]
        out_ref[1, :, here] = result[rows:]
    rest = pl.ds(pl.multiple_of((1 - par) * half, 8), half)
    copies = [pltpu.make_async_copy(out_ref.at[k, rest, :], out_hbm.at[k, rest, :], sem.at[k]) for k in range(2)]
    for copy in copies:
        copy.start()
    for index, matrix in enumerate(last_taps(rows)):
        taps_ref[index] = matrix
    for copy in copies:
        copy.wait()


def last_taps(rows):
    half = rows // 2
    away = far_taps(rows, False)
    high, low = split(jnp.where(parity() == 0, away[:half], away[half:]))
    groups = rows >> SHIFT_Z
    shape = (half, TILE)
    found = []
    for place in range(TILE // groups):
        for comp in range(2):
            of_group = (iota(shape, 0) >> SHIFT_Z) + place * groups + comp * (groups // 2) == iota(shape, 1)
            mean = dot(high, one_hot(of_group, 1.0 / (1 << SHIFT_Z))).astype(BF16)
            found.append(jnp.concatenate([high, low, mean], axis=1))
    return found


def last_kernel(taps_ref, part_ref, msg_ref, out_in, out_hbm, buf, sem):
    _, rows, width = part_ref.shape
    nblocks = width // LANES
    half = rows // 2
    places = TILE // (rows >> SHIFT_Z)
    reached = pl.ds(pl.multiple_of(parity() * half, 8), half)
    copies = []
    for comp in range(2):
        for index, first in enumerate(range(0, nblocks, 2)):
            here = pl.ds(first * LANES, 2 * LANES)
            got, sums = [], []
            for j in range(2):
                got.append(msg_ref[pl.ds((first + j) * rows + comp * half, half), :])
                sums.append(msg_ref[pl.ds(nblocks * rows + (2 * (index // places) + j) * TILE, TILE), :])
            got, sums = jnp.concatenate(got, axis=1), jnp.concatenate(sums, axis=1)
            part = dot(taps_ref[index % places * 2 + comp], jnp.concatenate([got, got, sums], axis=0))
            buf[comp, :, here] = part_ref[comp, reached, here] + part
        copies.append(pltpu.make_async_copy(buf.at[comp], out_hbm.at[comp, reached, :], sem.at[comp]))
        copies[-1].start()
    for copy in copies:
        copy.wait()


def body(innovation, background, level_weight):
    levels, rows, width = innovation.shape
    if rows != HALF or width % SPAN or levels != 4:
        raise NotImplementedError("slab shape")
    nblocks = width // LANES
    both, half = 2 * rows, rows // 2
    count = lax.axis_size("row")
    chip = [(i, i ^ 1) for i in range(count) if i ^ 1 < count]
    away = [(i, j) for i in range(count) for j in [((i + 1) ^ 1) - 1] if 0 <= j < count]
    hbm = [pltpu.with_memory_space_constraint(x, pltpu.HBM) for x in (level_weight, innovation, background)]
    band = jnp.asarray(zonal_band())
    piece = jax.ShapeDtypeStruct((nblocks // PIECES, 2, both, LANES), BF16)
    result = jax.ShapeDtypeStruct((2, rows, width), F32)
    *raws, outer, row, inno, back, weight = pl.pallas_call(
        outer_kernel,
        out_shape=[piece] * PIECES
        + [
            jax.ShapeDtypeStruct((outer_rows(rows, nblocks, levels), LANES), BF16),
            jax.ShapeDtypeStruct((TILE, width), BF16),
            jax.ShapeDtypeStruct(innovation.shape, BF16),
            jax.ShapeDtypeStruct(background.shape, BF16),
            jax.ShapeDtypeStruct((2 * levels, 2 * LANES), F32),
        ],
        in_specs=[HBM] * 3,
        out_specs=[VMEM] * (PIECES + 5),
        scratch_shapes=[
            pltpu.SMEM((levels,), F32),
            pltpu.VMEM((SPAN, LANES), BF16),
            pltpu.SemaphoreType.DMA((2, len(CUTS) - 1)),
            pltpu.SemaphoreType.DMA((2,)),
            pltpu.SemaphoreType.DMA,
        ],
        compiler_params=PARAMS,
        name="outer_half",
    )(*hbm)
    outer_got = lax.ppermute(outer, "row", away)
    row = lax.ppermute(row, "row", chip)
    *raws, inner = pl.pallas_call(
        inner_kernel,
        out_shape=[piece] * PIECES + [jax.ShapeDtypeStruct((inner_rows(rows, nblocks), LANES), BF16)],
        in_specs=[VMEM] * (5 + PIECES),
        out_specs=[VMEM] * (PIECES + 1),
        scratch_shapes=[pltpu.VMEM((rows, width), BF16)],
        input_output_aliases={5 + k: k for k in range(PIECES)},
        compiler_params=PARAMS,
        name="inner_half",
    )(weight, inno, back, row, band, *raws)
    inner_got = lax.ppermute(inner, "row", away)
    nears = [lax.ppermute(r, "row", chip) for r in raws]
    edges = pl.pallas_call(
        outermost_kernel,
        out_shape=jax.ShapeDtypeStruct((TILE, width), BF16),
        in_specs=[VMEM] * 3,
        out_specs=VMEM,
        compiler_params=PARAMS,
        name="outermost_rows",
    )(weight, outer, outer_got)
    near_edges = lax.ppermute(edges, "row", chip)
    out, part, last = pl.pallas_call(
        near_kernel,
        out_shape=[result, result, jax.ShapeDtypeStruct((2 * TILE // (rows >> SHIFT_Z), half, rows + TILE), BF16)],
        in_specs=[VMEM] * (2 * PIECES + 4),
        out_specs=[HBM] + [VMEM] * 2,
        scratch_shapes=[pltpu.VMEM((nblocks, 2 * both, LANES), BF16), pltpu.SemaphoreType.DMA((2,))],
        compiler_params=PARAMS,
        name="near_part",
    )(*raws, *nears, edges, near_edges, outer_got, band)
    return pl.pallas_call(
        last_kernel,
        out_shape=result,
        in_specs=[VMEM] * 3 + [HBM],
        out_specs=HBM,
        input_output_aliases={3: 0},
        scratch_shapes=[pltpu.VMEM((2, half, width), F32), pltpu.SemaphoreType.DMA((2,))],
        compiler_params=PARAMS,
        name="last_part",
    )(last, part, inner_got, out)


def solution(mesh):
    placed = (P("member", "row", None), P("member", "row", None), P())
    return jax.shard_map(
        body, mesh=mesh, in_specs=placed, out_specs=P("member", "row", None), check_vma=False
    )
```

```python
import math

import jax
import jax.numpy as jnp
import numpy as np
from jax import lax
from jax.experimental import pallas as pl
from jax.experimental.pallas import tpu as pltpu
from jax.sharding import PartitionSpec as P

HALF = 64
SIGMA = 64
LANES = 128
TILE = 16
SHIFT_Y, SHIFT_X, SHIFT_Z = 2, 3, 4
SPAN = LANES << SHIFT_X
PACK = 8
CUTS = (0, 8, 16)
PIECES = 4
F32 = jnp.float32
BF16 = jnp.bfloat16
NORM = math.sqrt(sum(math.exp(-k * k / (SIGMA * SIGMA)) for k in range(-HALF, HALF + 1)))

VMEM = pl.BlockSpec(memory_space=pltpu.VMEM)
HBM = pl.BlockSpec(memory_space=pltpu.HBM)
PARAMS = pltpu.CompilerParams(vmem_limit_bytes=40 * 1024 * 1024)


def split(values):
    high = values.astype(BF16)
    return high, (values - high.astype(F32)).astype(BF16)


def dot(left, right):
    return jnp.dot(left, right, preferred_element_type=F32)


def iota(shape, dim):
    return lax.broadcasted_iota(jnp.int32, shape, dim)


def one_hot(mask, value=1.0):
    return jnp.where(mask, value, 0.0).astype(BF16)


def difference(off):
    return (jnp.where(off == 1, 1.0, 0.0) - jnp.where(off == -1, 1.0, 0.0)).astype(BF16)


def taps(offset):
    off = offset.astype(F32)
    value = jnp.exp(off * off * (-0.5 / (SIGMA * SIGMA))) * (1.0 / NORM)
    return jnp.where(jnp.abs(offset) <= HALF, value, 0.0)


def zonal_band():
    offset = np.arange(4 * LANES)[:, None] - LANES - np.arange(2 * LANES)[None, :]
    band = np.exp(-offset * offset / (2.0 * SIGMA * SIGMA)) / NORM
    band = np.where(np.abs(offset) <= HALF, band, 0.0).astype(np.float32)
    high = band.astype(BF16)
    return np.stack([high, (band - high.astype(np.float32)).astype(BF16)])


def window(first, nblocks):
    low, high = max(first - 1, 0), min(first + 3, nblocks)
    return low, high, (low - first + 1) * LANES, (high - first + 1) * LANES


def smooth_x(band_ref, load, first, nblocks):
    low, high, top, bottom = window(first, nblocks)
    both = jnp.concatenate([load(k) for k in range(low, high)], axis=1)
    rows = both.shape[0] // 2
    found = dot(both, band_ref[0, top:bottom, :])
    return found[:rows] + found[rows:] + dot(both[:rows], band_ref[1, top:bottom, :])


def parity():
    return lax.rem(lax.axis_index("row"), 2)


def block_of(refs, k):
    per = refs[0].shape[0]
    return refs[k // per].at[k % per]


def tile_at(row):
    return pl.ds(pl.multiple_of(row, TILE), TILE)


def half_of(ref, comp_rows, start, part):
    half = comp_rows // 2
    return [ref[part, pl.ds(pl.multiple_of(comp * comp_rows + start, TILE), half), :] for comp in range(2)]


def raw_pair(first, weight, inno_ref, back_ref, upper, diff_y, diff_x, extra, raw_refs):
    levels, rows, width = inno_ref.shape
    half = rows // 2
    start = pl.multiple_of(jnp.where(upper, 0, half), TILE)
    exact = pl.ds(start, half)
    deep = pl.ds(pl.multiple_of(jnp.where(upper, 0, half - TILE), TILE), half + TILE)
    here = pl.ds(first * LANES, 2 * LANES)
    low, high, top, bottom = window(first, width // LANES)
    around = back_ref[:, exact, low * LANES : high * LANES]
    grad_xs = dot(around.reshape(levels * half, -1), diff_x[top:bottom])
    numer_y = numer_x = 0.0
    denom = 1.0
    for level in range(levels):
        grad_y = dot(diff_y, back_ref[level, deep, here])
        if extra is not None:
            grad_y += extra(level, here)
        grad_x = grad_xs[level * half : (level + 1) * half]
        scaled = inno_ref[level, exact, here].astype(F32) * (0.5 * weight(level))
        numer_y += scaled * grad_y
        numer_x += scaled * grad_x
        denom += (0.25 * weight(level)) * (grad_y * grad_y + grad_x * grad_x)
    inverse = 1.0 / denom
    found = []
    for comp, numer in enumerate((numer_y, numer_x)):
        raw = numer * inverse
        if extra is None:
            other = inno_ref[comp, exact, here].astype(F32)
            raw = jnp.where(iota(raw.shape, 0) == jnp.where(upper, 0, half - 1), other, raw)
        found.append(split(raw))
        at = pl.ds(pl.multiple_of(comp * rows + start, TILE), half)
        for part, values in enumerate(found[-1]):
            for j in range(2):
                block_of(raw_refs, first + j)[part, at, :] = values[:, j * LANES : (j + 1) * LANES]
    return found


def differences(upper, half):
    deep = half + TILE
    diff_y = difference(iota((half, deep), 1) - iota((half, deep), 0) - jnp.where(upper, 0, TILE))
    shape = (4 * LANES, 2 * LANES)
    return diff_y, difference(iota(shape, 0) - LANES - iota(shape, 1))


def outer_kernel(lw_hbm, inno_hbm, back_hbm, *refs):
    *raw_refs, msg_ref, row_ref, inno_ref, back_ref, weight_ref, lw_ref, sum_ref, pick_ref, total_ref, sems, rest_sems, lw_sem = refs
    levels, rows, width = inno_ref.shape
    half = rows // 2
    deep = half + TILE
    nblocks = width // LANES
    upper = parity() == 0
    start = jnp.where(upper, 0, half)
    cuts = [cut * nblocks // CUTS[-1] * LANES for cut in CUTS]

    def bring(sem, which, at, size, cols):
        index = (slice(None), pl.ds(pl.multiple_of(at, TILE), size), cols)
        source, target = ((inno_hbm, inno_ref), (back_hbm, back_ref))[which]
        return pltpu.make_async_copy(source.at[index], target.at[index], sem)

    weights = pltpu.make_async_copy(lw_hbm, lw_ref, lw_sem)
    copies = []
    for q, cut in enumerate(cuts[:-1]):
        cols = pl.ds(cut, cuts[q + 1] - cut)
        copies.append(
            [
                bring(sems.at[1, q], 1, jnp.where(upper, 0, rows - deep), deep, cols),
                bring(sems.at[0, q], 0, start, half, cols),
            ]
        )
    copies[-1].append(bring(rest_sems.at[1], 1, jnp.where(upper, deep, 0), rows - deep, pl.ds(0, width)))
    other = bring(rest_sems.at[0], 0, half - start, half, pl.ds(0, width))
    weights.start()
    for copy in sum(copies, []) + [other]:
        copy.start()
    diff_y, diff_x = differences(upper, half)
    sum_ref[...] = one_hot(iota(sum_ref.shape, 0) >> SHIFT_X == iota(sum_ref.shape, 1))
    groups = rows >> SHIFT_Y
    kinds = 3 * levels - 2
    row, col = iota(pick_ref.shape[1:], 0), iota(pick_ref.shape[1:], 1)
    want = row - (col >> 6) * kinds
    level = (col >> 4) & (levels - 1)
    place = col & (TILE - 1)
    outermost = place == jnp.where(upper, 0, TILE - 1)
    next_row = place == jnp.where(upper, 1, TILE - 2)
    pick_ref[0] = one_hot(((want == level) & outermost) | ((want == levels + level) & next_row))
    pick_ref[1] = one_hot((want == 2 * levels + level - 2) & (level >= 2) & outermost)
    shape = (TILE, levels * TILE)
    pick_near = one_hot(iota(shape, 1) == iota(shape, 0) * TILE + jnp.where(upper, TILE - 1, 0))
    weights.wait()
    for level in range(2 * levels):
        weight_ref[level : level + 1, :] = jnp.full((1, weight_ref.shape[1]), lw_ref[level % levels])
    base = nblocks * rows
    spans = range(0, nblocks, SPAN // LANES)

    def input_rows():
        near_rows = back_ref[:, tile_at(jnp.where(upper, rows - TILE, 0)), :]
        row_ref[...] = dot(pick_near, near_rows.reshape(levels * TILE, -1)).astype(BF16)
        edge_at = tile_at(jnp.where(upper, 0, rows - TILE))
        for first in range(0, nblocks, PACK):
            back, inno = [], []
            for k in range(first, first + PACK):
                here = pl.ds(k * LANES, LANES)
                back.append(back_ref[:, edge_at, here].reshape(levels * TILE, LANES))
                inno.append(inno_ref[:, edge_at, here].reshape(levels * TILE, LANES))
            tile = dot(pick_ref[0], jnp.concatenate(back, axis=0)) + dot(pick_ref[1], jnp.concatenate(inno, axis=0))
            at = base + len(spans) * groups + first * kinds
            msg_ref[pl.ds(at, PACK * kinds), :] = tile.astype(BF16)

    def residuals(span):
        lows = [
            jnp.concatenate(half_of(block_of(raw_refs, k), rows, start, 1), axis=0)
            for k in range(span, span + SPAN // LANES)
        ]
        total_ref[...] = dot(jnp.concatenate(lows, axis=1), sum_ref[...])
        found = sum(total_ref[pl.ds(k, groups, stride=1 << SHIFT_Y), :] for k in range(1 << SHIFT_Y))
        msg_ref[pl.ds(base + span // (SPAN // LANES) * groups, groups), :] = found.astype(BF16)

    waited = 0
    for first in range(0, nblocks, 2):
        while cuts[waited] < window(first, nblocks)[1] * LANES:
            for copy in copies[waited]:
                copy.wait()
            waited += 1
        found = raw_pair(first, lambda k: lw_ref[k], inno_ref, back_ref, upper, diff_y, diff_x, None, raw_refs)
        for comp, (high, _) in enumerate(found):
            for j in range(2):
                msg_ref[pl.ds((first + j) * rows + comp * half, half), :] = high[:, j * LANES : (j + 1) * LANES]
        if first == spans[-1]:
            for span in spans[:-1]:
                residuals(span)
    input_rows()
    residuals(spans[-1])
    other.wait()


def outer_rows(rows, nblocks, levels):
    return nblocks * rows + (nblocks * LANES // SPAN) * (rows >> SHIFT_Y) + nblocks * (3 * levels - 2)


def inner_kernel(weight_ref, inno_ref, back_ref, row_ref, band_ref, *refs):
    raw_refs = refs[PIECES : 2 * PIECES]
    msg_ref, rest_ref = refs[2 * PIECES :]
    _, rows, width = inno_ref.shape
    half = rows // 2
    nblocks = width // LANES
    upper = parity() == 1
    start = jnp.where(upper, 0, half)
    diff_y, diff_x = differences(upper, half)
    at = iota((half, 2 * LANES), 0) == jnp.where(upper, 0, half - 1)
    sign = jnp.where(upper, -1.0, 1.0)

    def extra(level, here):
        return jnp.where(at, row_ref[level : level + 1, here].astype(F32) * sign, 0.0)

    def weight(level):
        return weight_ref[level : level + 1, :]

    def load(k):
        block = block_of(raw_refs, k)
        return jnp.concatenate(half_of(block, rows, start, 0) + half_of(block, rows, start, 1), axis=0)

    groups = rows >> SHIFT_Z
    shape = (2 * groups, rows)
    sum_y = one_hot(iota(shape, 1) >> SHIFT_Z == iota(shape, 0))
    for first in range(0, nblocks, 2):
        raw_pair(first, weight, inno_ref, back_ref, upper, diff_y, diff_x, extra, raw_refs)
    for first in range(0, nblocks, 2):
        high, low = split(smooth_x(band_ref, load, first, nblocks))
        rest_ref[:, first * LANES : (first + 2) * LANES] = low
        for j in range(2):
            msg_ref[pl.ds((first + j) * rows, rows), :] = high[:, j * LANES : (j + 1) * LANES]
    sums = dot(sum_y, rest_ref[...])
    per = TILE // groups
    for first in range(0, nblocks, 2 * per):
        for j in range(2):
            parts = [sums[:groups, k * LANES : (k + 1) * LANES] for k in range(first + j, first + 2 * per, 2)]
            tile = nblocks * rows + (first // per + j) * TILE
            msg_ref[pl.ds(tile, TILE), :] = jnp.concatenate(parts, axis=0).astype(BF16)


def inner_rows(rows, nblocks):
    return nblocks * rows + nblocks * (rows >> SHIFT_Z)


def outermost_kernel(weight_ref, own_ref, got_ref, out_ref):
    nblocks = out_ref.shape[1] // LANES
    levels = weight_ref.shape[0] // 2
    kinds = 3 * levels - 2
    base = own_ref.shape[0] - nblocks * kinds
    rows, half = HALF, HALF // 2
    first_core = parity() == 0
    at = iota((8, rows), 0) * half

    def unpacked(ref, upper):
        packs = [ref[pl.ds(base + k * kinds, PACK * kinds), :].astype(F32) for k in range(0, nblocks, PACK)]
        pick = one_hot((iota((8, rows), 1) == at + jnp.where(upper, 0, half - 1)) & (at < rows))
        some = []
        for k in range(0, nblocks, 2):
            pair = [ref[pl.ds((k + j) * rows, rows), :] for j in range(2)]
            some.append(dot(pick, jnp.concatenate(pair, axis=1))[:2])
        found = []
        for low, high in ((0, levels), (levels, 2 * levels), (2 * levels, kinds)):
            parts = [p[j * kinds + low : j * kinds + high] for p in packs for j in range(PACK)]
            found.append(jnp.concatenate(parts, axis=1))
        found[2] = jnp.concatenate([jnp.concatenate(some, axis=1), found[2]], axis=0)
        return found

    own, got = unpacked(own_ref, first_core), unpacked(got_ref, jnp.logical_not(first_core))
    here = jnp.concatenate([own[0], got[0]], axis=0)
    beyond = jnp.concatenate([got[0], own[0]], axis=0)
    before = jnp.concatenate([own[1], got[1]], axis=0)
    inno = jnp.concatenate([own[2], got[2]], axis=0)
    shape = here.shape
    grad_y = jnp.where((iota(shape, 0) < levels) == first_core, before - beyond, beyond - before)
    lane = iota(shape, 1)
    left = jnp.where(lane == 0, 0.0, pltpu.roll(here, 1, 1))
    right = jnp.where(lane == shape[1] - 1, 0.0, pltpu.roll(here, shape[1] - 1, 1))
    grad_x = right - left
    weight = jnp.concatenate([weight_ref[:, :LANES]] * nblocks, axis=1)
    scaled = inno * (0.5 * weight)

    def total(values):
        return [sum(values[k : k + 1] for k in range(f, f + levels)) for f in (0, levels)]

    numer_y, numer_x = total(scaled * grad_y), total(scaled * grad_x)
    denom = total((0.25 * weight) * (grad_y * grad_y + grad_x * grad_x))
    found = []
    for k in range(2):
        inverse = 1.0 / (1.0 + denom[k])
        found += [numer_y[k] * inverse, numer_x[k] * inverse]
    high, low = split(jnp.concatenate(found, axis=0))
    none = jnp.zeros((TILE - 8, shape[1]), F32)
    out_ref[...] = jnp.concatenate([high.astype(F32), low.astype(F32), none], axis=0).astype(BF16)


def far_taps(rows, towards):
    side = 2 * parity() - 1
    half = rows // 2
    start = jnp.where((side < 0) == towards, half, 0)
    return taps(iota((rows, half), 1) + start - iota((rows, half), 0) + side * rows)


def near_kernel(*refs):
    raw_refs, near_refs = refs[:PIECES], refs[PIECES : 2 * PIECES]
    edges_ref, near_edges_ref, msg_ref, band_ref, out_hbm, out_ref, taps_ref, total_ref, sem = refs[2 * PIECES :]
    _, rows, width = out_ref.shape
    nblocks = width // LANES
    half = rows // 2
    par = parity()
    side = 1 - 2 * par
    offset = iota((rows, rows), 1) - iota((rows, rows), 0)
    near_taps = jnp.concatenate([taps(offset), taps(offset + side * rows)], axis=1)
    column = iota(near_taps.shape, 1)
    outermost = (column == par * (rows - 1)) | (column == (2 - par) * rows - 1 + par)
    near_taps = jnp.where(outermost, 0.0, near_taps)
    near_high = near_taps.astype(BF16)
    toward = far_taps(rows, True)
    outermost = iota(toward.shape, 1) == jnp.where(par == 0, half - 1, 0)
    toward_inner = jnp.where(outermost, 0.0, toward)
    shape = (rows, TILE)
    kind = iota(shape, 1)
    own_at = jnp.where(par == 0, 0, rows - 1)
    far_at = jnp.where(par == 0, -1, rows)
    near_at = jnp.where(par == 0, 2 * rows - 1, -rows)
    own_edges = taps(jnp.where(kind & 2 == 0, own_at, far_at) - iota(shape, 0))
    near_edges = jnp.where(kind & 2 == 0, taps(near_at - iota(shape, 0)), 0.0)
    stacked = []
    for comp in range(2):
        here = (kind < 8) & (kind & 1 == comp)
        all_taps = [near_taps, toward_inner, jnp.where(here, own_edges, 0.0), jnp.where(here, near_edges, 0.0)]
        stacked.append(jnp.concatenate(split(jnp.concatenate(all_taps, axis=1)), axis=0))
    groups = half >> SHIFT_Y
    shape = (half, groups)
    mean_y = one_hot(iota(shape, 0) >> SHIFT_Y == iota(shape, 1), 1.0 / (1 << SHIFT_Y))
    group_taps = dot(toward.astype(BF16), mean_y).astype(BF16)
    shape = (LANES, SPAN)
    mean_x = one_hot(iota(shape, 1) >> SHIFT_X == iota(shape, 0), 1.0 / (1 << SHIFT_X))
    rest = []
    for span in range(width // SPAN):
        tile = msg_ref[pl.ds(nblocks * rows + span * 2 * groups, 2 * groups), :]
        rest.append(jnp.concatenate([dot(group_taps, tile[:groups]), dot(group_taps, tile[groups:])], axis=0).astype(BF16))
    for first in range(0, nblocks, 2):
        cols = pl.ds(first * LANES, 2 * LANES)
        place = first * LANES % SPAN
        spread = dot(rest[first * LANES // SPAN], mean_x[:, place : place + 2 * LANES])
        edges = [edges_ref[:, cols], near_edges_ref[:, cols]]
        for comp in range(2):
            here = pl.ds(comp * rows, rows)
            highs, lows = [], []
            for k in (first, first + 1):
                both = (block_of(raw_refs, k), block_of(near_refs, k))
                got = msg_ref[pl.ds(k * rows + comp * half, half), :]
                highs.append(jnp.concatenate([ref[0, here, :] for ref in both] + [got], axis=0))
                lows.append(jnp.concatenate([ref[1, here, :] for ref in both], axis=0))
            part = dot(stacked[comp], jnp.concatenate([jnp.concatenate(highs, axis=1)] + edges, axis=0))
            part = part[:rows] + part[rows:] + dot(near_high, jnp.concatenate(lows, axis=1))
            high, low = split(part + spread[comp * rows : (comp + 1) * rows])
            for j in range(2):
                cut = slice(j * LANES, (j + 1) * LANES)
                total_ref[first + j, pl.ds(comp * rows, rows), :] = high[:, cut]
                total_ref[first + j, pl.ds((2 + comp) * rows, rows), :] = low[:, cut]
    for first in range(0, nblocks, 2):
        result = smooth_x(band_ref, lambda k: total_ref[k], first, nblocks)
        here = pl.ds(first * LANES, 2 * LANES)
        out_ref[0, :, here] = result[:rows]
        out_ref[1, :, here] = result[rows:]
    rest = pl.ds(pl.multiple_of((1 - par) * half, 8), half)
    copies = [pltpu.make_async_copy(out_ref.at[k, rest, :], out_hbm.at[k, rest, :], sem.at[k]) for k in range(2)]
    for copy in copies:
        copy.start()
    for index, matrix in enumerate(last_taps(rows)):
        taps_ref[index] = matrix
    for copy in copies:
        copy.wait()


def last_taps(rows):
    half = rows // 2
    away = far_taps(rows, False)
    high, low = split(jnp.where(parity() == 0, away[:half], away[half:]))
    groups = rows >> SHIFT_Z
    shape = (half, TILE)
    found = []
    for place in range(TILE // groups):
        for comp in range(2):
            of_group = (iota(shape, 0) >> SHIFT_Z) + place * groups + comp * (groups // 2) == iota(shape, 1)
            mean = dot(high, one_hot(of_group, 1.0 / (1 << SHIFT_Z))).astype(BF16)
            found.append(jnp.concatenate([high, low, mean], axis=1))
    return found


def last_kernel(taps_ref, part_ref, msg_ref, out_in, out_hbm, buf, sem):
    _, rows, width = part_ref.shape
    nblocks = width // LANES
    half = rows // 2
    places = TILE // (rows >> SHIFT_Z)
    reached = pl.ds(pl.multiple_of(parity() * half, 8), half)
    copies = []
    for comp in range(2):
        for index, first in enumerate(range(0, nblocks, 2)):
            here = pl.ds(first * LANES, 2 * LANES)
            got, sums = [], []
            for j in range(2):
                got.append(msg_ref[pl.ds((first + j) * rows + comp * half, half), :])
                sums.append(msg_ref[pl.ds(nblocks * rows + (2 * (index // places) + j) * TILE, TILE), :])
            got, sums = jnp.concatenate(got, axis=1), jnp.concatenate(sums, axis=1)
            part = dot(taps_ref[index % places * 2 + comp], jnp.concatenate([got, got, sums], axis=0))
            buf[comp, :, here] = part_ref[comp, reached, here] + part
        copies.append(pltpu.make_async_copy(buf.at[comp], out_hbm.at[comp, reached, :], sem.at[comp]))
        copies[-1].start()
    for copy in copies:
        copy.wait()


def body(innovation, background, level_weight):
    levels, rows, width = innovation.shape
    if rows != HALF or width % SPAN or levels != 4:
        raise NotImplementedError("slab shape")
    nblocks = width // LANES
    both, half = 2 * rows, rows // 2
    count = lax.axis_size("row")
    chip = [(i, i ^ 1) for i in range(count) if i ^ 1 < count]
    away = [(i, j) for i in range(count) for j in [((i + 1) ^ 1) - 1] if 0 <= j < count]
    hbm = [pltpu.with_memory_space_constraint(x, pltpu.HBM) for x in (level_weight, innovation, background)]
    band = jnp.asarray(zonal_band())
    piece = jax.ShapeDtypeStruct((nblocks // PIECES, 2, both, LANES), BF16)
    result = jax.ShapeDtypeStruct((2, rows, width), F32)
    *raws, outer, row, inno, back, weight = pl.pallas_call(
        outer_kernel,
        out_shape=[piece] * PIECES
        + [
            jax.ShapeDtypeStruct((outer_rows(rows, nblocks, levels), LANES), BF16),
            jax.ShapeDtypeStruct((TILE, width), BF16),
            jax.ShapeDtypeStruct(innovation.shape, BF16),
            jax.ShapeDtypeStruct(background.shape, BF16),
            jax.ShapeDtypeStruct((2 * levels, 2 * LANES), F32),
        ],
        in_specs=[HBM] * 3,
        out_specs=[VMEM] * (PIECES + 5),
        scratch_shapes=[
            pltpu.SMEM((levels,), F32),
            pltpu.VMEM((SPAN, LANES), BF16),
            pltpu.VMEM((2, PACK * (3 * levels - 2), PACK * levels * TILE), BF16),
            pltpu.VMEM((rows, LANES), F32),
            pltpu.SemaphoreType.DMA((2, len(CUTS) - 1)),
            pltpu.SemaphoreType.DMA((2,)),
            pltpu.SemaphoreType.DMA,
        ],
        compiler_params=PARAMS,
        name="outer_half",
    )(*hbm)
    outer_got = lax.ppermute(outer, "row", away)
    row = lax.ppermute(row, "row", chip)
    *raws, inner = pl.pallas_call(
        inner_kernel,
        out_shape=[piece] * PIECES + [jax.ShapeDtypeStruct((inner_rows(rows, nblocks), LANES), BF16)],
        in_specs=[VMEM] * (5 + PIECES),
        out_specs=[VMEM] * (PIECES + 1),
        scratch_shapes=[pltpu.VMEM((rows, width), BF16)],
        input_output_aliases={5 + k: k for k in range(PIECES)},
        compiler_params=PARAMS,
        name="inner_half",
    )(weight, inno, back, row, band, *raws)
    inner_got = lax.ppermute(inner, "row", away)
    nears = [lax.ppermute(r, "row", chip) for r in raws]
    edges = pl.pallas_call(
        outermost_kernel,
        out_shape=jax.ShapeDtypeStruct((TILE, width), BF16),
        in_specs=[VMEM] * 3,
        out_specs=VMEM,
        compiler_params=PARAMS,
        name="outermost_rows",
    )(weight, outer, outer_got)
    near_edges = lax.ppermute(edges, "row", chip)
    out, part, last = pl.pallas_call(
        near_kernel,
        out_shape=[result, result, jax.ShapeDtypeStruct((2 * TILE // (rows >> SHIFT_Z), half, rows + TILE), BF16)],
        in_specs=[VMEM] * (2 * PIECES + 4),
        out_specs=[HBM] + [VMEM] * 2,
        scratch_shapes=[pltpu.VMEM((nblocks, 2 * both, LANES), BF16), pltpu.SemaphoreType.DMA((2,))],
        compiler_params=PARAMS,
        name="near_part",
    )(*raws, *nears, edges, near_edges, outer_got, band)
    return pl.pallas_call(
        last_kernel,
        out_shape=result,
        in_specs=[VMEM] * 3 + [HBM],
        out_specs=HBM,
        input_output_aliases={3: 0},
        scratch_shapes=[pltpu.VMEM((2, half, width), F32), pltpu.SemaphoreType.DMA((2,))],
        compiler_params=PARAMS,
        name="last_part",
    )(last, part, inner_got, out)


def solution(mesh):
    placed = (P("member", "row", None), P("member", "row", None), P())
    return jax.shard_map(
        body, mesh=mesh, in_specs=placed, out_specs=P("member", "row", None), check_vma=False
    )
```

```python
import math

import jax
import jax.numpy as jnp
import numpy as np
from jax import lax
from jax.experimental import pallas as pl
from jax.experimental.pallas import tpu as pltpu
from jax.sharding import PartitionSpec as P

HALF = 64
SIGMA = 64
LANES = 128
TILE = 16
SPREAD, LOWEST = 250.0, 125.0
PACK = 8
CUTS = (0, 8, 16)
PIECES = 4
F32 = jnp.float32
BF16 = jnp.bfloat16
NORM = math.sqrt(sum(math.exp(-k * k / (SIGMA * SIGMA)) for k in range(-HALF, HALF + 1)))

VMEM = pl.BlockSpec(memory_space=pltpu.VMEM)
HBM = pl.BlockSpec(memory_space=pltpu.HBM)
PARAMS = pltpu.CompilerParams(vmem_limit_bytes=40 * 1024 * 1024)


def split(values):
    high = values.astype(BF16)
    return high, (values - high.astype(F32)).astype(BF16)


def encode(parts):
    top = jnp.max(jnp.concatenate([jnp.abs(x) for x in parts], axis=0), axis=0, keepdims=True)
    top = (top * 1.01).astype(BF16).astype(F32)
    scale = SPREAD / jnp.maximum(top, 1e-35)
    codes = []
    for x in parts:
        size = jnp.exp2(jnp.abs(x) * scale - LOWEST)
        codes.append(jnp.where(x < 0, -size, size))
    return codes, top


def decode(codes, top):
    codes = codes.astype(F32)
    size = (jnp.log2(jnp.maximum(jnp.abs(codes), 2.0**-LOWEST)) + LOWEST) * (top * (1.0 / SPREAD))
    return jnp.where(codes < 0, -size, size)


def dot(left, right):
    return jnp.dot(left, right, preferred_element_type=F32)


def iota(shape, dim):
    return lax.broadcasted_iota(jnp.int32, shape, dim)


def one_hot(mask, value=1.0):
    return jnp.where(mask, value, 0.0).astype(BF16)


def difference(off):
    return (jnp.where(off == 1, 1.0, 0.0) - jnp.where(off == -1, 1.0, 0.0)).astype(BF16)


def taps(offset):
    off = offset.astype(F32)
    value = jnp.exp(off * off * (-0.5 / (SIGMA * SIGMA))) * (1.0 / NORM)
    return jnp.where(jnp.abs(offset) <= HALF, value, 0.0)


def zonal_band():
    offset = np.arange(4 * LANES)[:, None] - LANES - np.arange(2 * LANES)[None, :]
    band = np.exp(-offset * offset / (2.0 * SIGMA * SIGMA)) / NORM
    band = np.where(np.abs(offset) <= HALF, band, 0.0).astype(np.float32)
    high = band.astype(BF16)
    return np.stack([high, (band - high.astype(np.float32)).astype(BF16)])


def window(first, nblocks):
    low, high = max(first - 1, 0), min(first + 3, nblocks)
    return low, high, (low - first + 1) * LANES, (high - first + 1) * LANES


def smooth_x(band_ref, load, first, nblocks):
    low, high, top, bottom = window(first, nblocks)
    both = jnp.concatenate([load(k) for k in range(low, high)], axis=1)
    rows = both.shape[0] // 2
    found = dot(both, band_ref[0, top:bottom, :])
    return found[:rows] + found[rows:] + dot(both[:rows], band_ref[1, top:bottom, :])


def parity():
    return lax.rem(lax.axis_index("row"), 2)


def block_of(refs, k):
    per = refs[0].shape[0]
    return refs[k // per].at[k % per]


def tile_at(row):
    return pl.ds(pl.multiple_of(row, TILE), TILE)


def half_of(ref, comp_rows, start, part):
    half = comp_rows // 2
    return [ref[part, pl.ds(pl.multiple_of(comp * comp_rows + start, TILE), half), :] for comp in range(2)]


def raw_pair(first, weight, inno_ref, back_ref, upper, diff_y, diff_x, extra, raw_refs):
    levels, rows, width = inno_ref.shape
    half = rows // 2
    start = pl.multiple_of(jnp.where(upper, 0, half), TILE)
    exact = pl.ds(start, half)
    deep = pl.ds(pl.multiple_of(jnp.where(upper, 0, half - TILE), TILE), half + TILE)
    here = pl.ds(first * LANES, 2 * LANES)
    low, high, top, bottom = window(first, width // LANES)
    around = back_ref[:, exact, low * LANES : high * LANES]
    grad_xs = dot(around.reshape(levels * half, -1), diff_x[top:bottom])
    numer_y = numer_x = 0.0
    denom = 1.0
    for level in range(levels):
        grad_y = dot(diff_y, back_ref[level, deep, here])
        if extra is not None:
            grad_y += extra(level, here)
        grad_x = grad_xs[level * half : (level + 1) * half]
        scaled = inno_ref[level, exact, here].astype(F32) * (0.5 * weight(level))
        numer_y += scaled * grad_y
        numer_x += scaled * grad_x
        denom += (0.25 * weight(level)) * (grad_y * grad_y + grad_x * grad_x)
    inverse = 1.0 / denom
    found = []
    for comp, numer in enumerate((numer_y, numer_x)):
        raw = numer * inverse
        if extra is None:
            raw = jnp.where(iota(raw.shape, 0) == jnp.where(upper, 0, half - 1), 0.0, raw)
        found.append(raw)
        at = pl.ds(pl.multiple_of(comp * rows + start, TILE), half)
        for part, values in enumerate(split(raw)):
            for j in range(2):
                block_of(raw_refs, first + j)[part, at, :] = values[:, j * LANES : (j + 1) * LANES]
    return found


def differences(upper, half):
    deep = half + TILE
    diff_y = difference(iota((half, deep), 1) - iota((half, deep), 0) - jnp.where(upper, 0, TILE))
    shape = (4 * LANES, 2 * LANES)
    return diff_y, difference(iota(shape, 0) - LANES - iota(shape, 1))


def outer_kernel(lw_hbm, inno_hbm, back_hbm, *refs):
    *raw_refs, msg_ref, row_ref, inno_ref, back_ref, weight_ref, lw_ref, pick_ref, top_ref, sems, rest_sems, lw_sem = refs
    levels, rows, width = inno_ref.shape
    half = rows // 2
    deep = half + TILE
    nblocks = width // LANES
    upper = parity() == 0
    start = jnp.where(upper, 0, half)
    cuts = [cut * nblocks // CUTS[-1] * LANES for cut in CUTS]

    def bring(sem, which, at, size, cols):
        index = (slice(None), pl.ds(pl.multiple_of(at, TILE), size), cols)
        source, target = ((inno_hbm, inno_ref), (back_hbm, back_ref))[which]
        return pltpu.make_async_copy(source.at[index], target.at[index], sem)

    weights = pltpu.make_async_copy(lw_hbm, lw_ref, lw_sem)
    copies = []
    for q, cut in enumerate(cuts[:-1]):
        cols = pl.ds(cut, cuts[q + 1] - cut)
        copies.append(
            [
                bring(sems.at[1, q], 1, jnp.where(upper, 0, rows - deep), deep, cols),
                bring(sems.at[0, q], 0, start, half, cols),
            ]
        )
    copies[-1].append(bring(rest_sems.at[1], 1, jnp.where(upper, deep, 0), rows - deep, pl.ds(0, width)))
    other = bring(rest_sems.at[0], 0, half - start, half, pl.ds(0, width))
    weights.start()
    for copy in sum(copies, []) + [other]:
        copy.start()
    diff_y, diff_x = differences(upper, half)
    outermost_row = iota((half, 2 * LANES), 0) == jnp.where(upper, 0, half - 1)
    kinds = 3 * levels - 2
    row, col = iota(pick_ref.shape[1:], 0), iota(pick_ref.shape[1:], 1)
    want = row - (col >> 6) * kinds
    level = (col >> 4) & (levels - 1)
    place = col & (TILE - 1)
    outermost = place == jnp.where(upper, 0, TILE - 1)
    next_row = place == jnp.where(upper, 1, TILE - 2)
    pick_ref[0] = one_hot(((want == level) & outermost) | ((want == levels + level) & next_row))
    pick_ref[1] = one_hot((want == 2 * levels + level - 2) & (level >= 2) & outermost)
    shape = (TILE, levels * TILE)
    pick_near = one_hot(iota(shape, 1) == iota(shape, 0) * TILE + jnp.where(upper, TILE - 1, 0))
    weights.wait()
    for level in range(2 * levels):
        weight_ref[level : level + 1, :] = jnp.full((1, weight_ref.shape[1]), lw_ref[level % levels])
    base = nblocks * rows

    def input_rows():
        near_rows = back_ref[:, tile_at(jnp.where(upper, rows - TILE, 0)), :]
        row_ref[...] = dot(pick_near, near_rows.reshape(levels * TILE, -1)).astype(BF16)
        edge_at = tile_at(jnp.where(upper, 0, rows - TILE))
        for first in range(0, nblocks, PACK):
            back, inno = [], []
            for k in range(first, first + PACK):
                here = pl.ds(k * LANES, LANES)
                back.append(back_ref[:, edge_at, here].reshape(levels * TILE, LANES))
                inno.append(inno_ref[:, edge_at, here].reshape(levels * TILE, LANES))
            tile = dot(pick_ref[0], jnp.concatenate(back, axis=0)) + dot(pick_ref[1], jnp.concatenate(inno, axis=0))
            at = base + nblocks + first * kinds
            msg_ref[pl.ds(at, PACK * kinds), :] = tile.astype(BF16)

    waited = 0
    for first in range(0, nblocks, 2):
        while cuts[waited] < window(first, nblocks)[1] * LANES:
            for copy in copies[waited]:
                copy.wait()
            waited += 1
        found = raw_pair(first, lambda k: lw_ref[k], inno_ref, back_ref, upper, diff_y, diff_x, None, raw_refs)
        codes, top = encode(found)
        for comp, code in enumerate(codes):
            inno = inno_ref[comp, pl.ds(pl.multiple_of(start, TILE), half), pl.ds(first * LANES, 2 * LANES)]
            code = jnp.where(outermost_row, inno.astype(F32), code).astype(BF16)
            for j in range(2):
                msg_ref[pl.ds((first + j) * rows + comp * half, half), :] = code[:, j * LANES : (j + 1) * LANES]
        for j in range(2):
            top_ref[first + j : first + j + 1, :] = top[:, j * LANES : (j + 1) * LANES]
    input_rows()
    msg_ref[pl.ds(base, nblocks), :] = top_ref[...].astype(BF16)
    other.wait()


def outer_rows(rows, nblocks, levels):
    return nblocks * rows + nblocks + nblocks * (3 * levels - 2)


def inner_kernel(weight_ref, inno_ref, back_ref, row_ref, band_ref, *refs):
    raw_refs = refs[PIECES : 2 * PIECES]
    msg_ref, top_ref = refs[2 * PIECES :]
    _, rows, width = inno_ref.shape
    half = rows // 2
    nblocks = width // LANES
    upper = parity() == 1
    start = jnp.where(upper, 0, half)
    diff_y, diff_x = differences(upper, half)
    at = iota((half, 2 * LANES), 0) == jnp.where(upper, 0, half - 1)
    sign = jnp.where(upper, -1.0, 1.0)

    def extra(level, here):
        return jnp.where(at, row_ref[level : level + 1, here].astype(F32) * sign, 0.0)

    def weight(level):
        return weight_ref[level : level + 1, :]

    def load(k):
        block = block_of(raw_refs, k)
        return jnp.concatenate(half_of(block, rows, start, 0) + half_of(block, rows, start, 1), axis=0)

    for first in range(0, nblocks, 2):
        raw_pair(first, weight, inno_ref, back_ref, upper, diff_y, diff_x, extra, raw_refs)
    for first in range(0, nblocks, 2):
        (code,), top = encode([smooth_x(band_ref, load, first, nblocks)])
        code = code.astype(BF16)
        for j in range(2):
            msg_ref[pl.ds((first + j) * rows, rows), :] = code[:, j * LANES : (j + 1) * LANES]
            top_ref[first + j : first + j + 1, :] = top[:, j * LANES : (j + 1) * LANES]
    msg_ref[pl.ds(nblocks * rows, nblocks), :] = top_ref[...].astype(BF16)


def inner_rows(rows, nblocks):
    return nblocks * rows + nblocks


def outermost_kernel(weight_ref, own_ref, got_ref, out_ref):
    nblocks = out_ref.shape[1] // LANES
    levels = weight_ref.shape[0] // 2
    kinds = 3 * levels - 2
    base = own_ref.shape[0] - nblocks * kinds
    rows, half = HALF, HALF // 2
    first_core = parity() == 0
    at = iota((8, rows), 0) * half

    def unpacked(ref, upper):
        packs = [ref[pl.ds(base + k * kinds, PACK * kinds), :].astype(F32) for k in range(0, nblocks, PACK)]
        pick = one_hot((iota((8, rows), 1) == at + jnp.where(upper, 0, half - 1)) & (at < rows))
        some = []
        for k in range(0, nblocks, 2):
            pair = [ref[pl.ds((k + j) * rows, rows), :] for j in range(2)]
            some.append(dot(pick, jnp.concatenate(pair, axis=1))[:2])
        found = []
        for low, high in ((0, levels), (levels, 2 * levels), (2 * levels, kinds)):
            parts = [p[j * kinds + low : j * kinds + high] for p in packs for j in range(PACK)]
            found.append(jnp.concatenate(parts, axis=1))
        found[2] = jnp.concatenate([jnp.concatenate(some, axis=1), found[2]], axis=0)
        return found

    own, got = unpacked(own_ref, first_core), unpacked(got_ref, jnp.logical_not(first_core))
    here = jnp.concatenate([own[0], got[0]], axis=0)
    beyond = jnp.concatenate([got[0], own[0]], axis=0)
    before = jnp.concatenate([own[1], got[1]], axis=0)
    inno = jnp.concatenate([own[2], got[2]], axis=0)
    shape = here.shape
    grad_y = jnp.where((iota(shape, 0) < levels) == first_core, before - beyond, beyond - before)
    lane = iota(shape, 1)
    left = jnp.where(lane == 0, 0.0, pltpu.roll(here, 1, 1))
    right = jnp.where(lane == shape[1] - 1, 0.0, pltpu.roll(here, shape[1] - 1, 1))
    grad_x = right - left
    weight = jnp.concatenate([weight_ref[:, :LANES]] * nblocks, axis=1)
    scaled = inno * (0.5 * weight)

    def total(values):
        return [sum(values[k : k + 1] for k in range(f, f + levels)) for f in (0, levels)]

    numer_y, numer_x = total(scaled * grad_y), total(scaled * grad_x)
    denom = total((0.25 * weight) * (grad_y * grad_y + grad_x * grad_x))
    found = []
    for k in range(2):
        inverse = 1.0 / (1.0 + denom[k])
        found += [numer_y[k] * inverse, numer_x[k] * inverse]
    high, low = split(jnp.concatenate(found, axis=0))
    none = jnp.zeros((TILE - 8, shape[1]), F32)
    out_ref[...] = jnp.concatenate([high.astype(F32), low.astype(F32), none], axis=0).astype(BF16)


def far_taps(rows, towards):
    side = 2 * parity() - 1
    half = rows // 2
    start = jnp.where((side < 0) == towards, half, 0)
    return taps(iota((rows, half), 1) + start - iota((rows, half), 0) + side * rows)


def near_kernel(*refs):
    raw_refs, near_refs = refs[:PIECES], refs[PIECES : 2 * PIECES]
    edges_ref, near_edges_ref, msg_ref, band_ref, out_hbm, out_ref, taps_ref, total_ref, sem = refs[2 * PIECES :]
    _, rows, width = out_ref.shape
    nblocks = width // LANES
    half = rows // 2
    par = parity()
    side = 1 - 2 * par
    offset = iota((rows, rows), 1) - iota((rows, rows), 0)
    near_taps = jnp.concatenate([taps(offset), taps(offset + side * rows)], axis=1)
    column = iota(near_taps.shape, 1)
    outermost = (column == par * (rows - 1)) | (column == (2 - par) * rows - 1 + par)
    near_taps = jnp.where(outermost, 0.0, near_taps)
    toward = far_taps(rows, True)
    outermost = iota(toward.shape, 1) == jnp.where(par == 0, half - 1, 0)
    toward = jnp.where(outermost, 0.0, toward)
    outermost = iota((half, 2 * LANES), 0) == jnp.where(par == 0, half - 1, 0)
    low_taps = jnp.concatenate([near_taps, toward], axis=1).astype(BF16)
    shape = (rows, TILE)
    kind = iota(shape, 1)
    own_at = jnp.where(par == 0, 0, rows - 1)
    far_at = jnp.where(par == 0, -1, rows)
    near_at = jnp.where(par == 0, 2 * rows - 1, -rows)
    own_edges = taps(jnp.where(kind & 2 == 0, own_at, far_at) - iota(shape, 0))
    near_edges = jnp.where(kind & 2 == 0, taps(near_at - iota(shape, 0)), 0.0)
    stacked = []
    for comp in range(2):
        here = (kind < 8) & (kind & 1 == comp)
        all_taps = [near_taps, toward, jnp.where(here, own_edges, 0.0), jnp.where(here, near_edges, 0.0)]
        stacked.append(jnp.concatenate(split(jnp.concatenate(all_taps, axis=1)), axis=0))
    tops = msg_ref[pl.ds(nblocks * rows, nblocks), :].astype(F32)
    for first in range(0, nblocks, 2):
        cols = pl.ds(first * LANES, 2 * LANES)
        top = jnp.concatenate([tops[k : k + 1] for k in (first, first + 1)], axis=1)
        edges = [edges_ref[:, cols], near_edges_ref[:, cols]]
        for comp in range(2):
            here = pl.ds(comp * rows, rows)
            both, got = [], []
            for k in (first, first + 1):
                refs = (block_of(raw_refs, k), block_of(near_refs, k))
                both.append([jnp.concatenate([ref[part, here, :] for ref in refs], axis=0) for part in range(2)])
                got.append(msg_ref[pl.ds(k * rows + comp * half, half), :])
            got = decode(jnp.concatenate(got, axis=1), top)
            got = split(jnp.where(outermost, 0.0, got))
            highs, lows = (
                jnp.concatenate([jnp.concatenate([x[part] for x in both], axis=1), got[part]], axis=0) for part in range(2)
            )
            part = dot(stacked[comp], jnp.concatenate([highs] + edges, axis=0))
            high, low = split(part[:rows] + part[rows:] + dot(low_taps, lows))
            for j in range(2):
                cut = slice(j * LANES, (j + 1) * LANES)
                total_ref[first + j, pl.ds(comp * rows, rows), :] = high[:, cut]
                total_ref[first + j, pl.ds((2 + comp) * rows, rows), :] = low[:, cut]
    for first in range(0, nblocks, 2):
        result = smooth_x(band_ref, lambda k: total_ref[k], first, nblocks)
        here = pl.ds(first * LANES, 2 * LANES)
        out_ref[0, :, here] = result[:rows]
        out_ref[1, :, here] = result[rows:]
    rest = pl.ds(pl.multiple_of((1 - par) * half, 8), half)
    copies = [pltpu.make_async_copy(out_ref.at[k, rest, :], out_hbm.at[k, rest, :], sem.at[k]) for k in range(2)]
    for copy in copies:
        copy.start()
    away = far_taps(rows, False)
    high, low = split(jnp.where(par == 0, away[:half], away[half:]))
    taps_ref[...] = jnp.concatenate([high, low, high], axis=1)
    for copy in copies:
        copy.wait()


def last_kernel(taps_ref, part_ref, msg_ref, out_in, out_hbm, buf, sem):
    _, rows, width = part_ref.shape
    nblocks = width // LANES
    half = rows // 2
    tops = msg_ref[pl.ds(nblocks * rows, nblocks), :].astype(F32)
    reached = pl.ds(pl.multiple_of(parity() * half, 8), half)
    copies = []
    for comp in range(2):
        for first in range(0, nblocks, 2):
            here = pl.ds(first * LANES, 2 * LANES)
            top = jnp.concatenate([tops[k : k + 1] for k in (first, first + 1)], axis=1)
            got = [msg_ref[pl.ds((first + j) * rows + comp * half, half), :] for j in range(2)]
            high, low = split(decode(jnp.concatenate(got, axis=1), top))
            part = dot(taps_ref[...], jnp.concatenate([high, high, low], axis=0))
            buf[comp, :, here] = part_ref[comp, reached, here] + part
        copies.append(pltpu.make_async_copy(buf.at[comp], out_hbm.at[comp, reached, :], sem.at[comp]))
        copies[-1].start()
    for copy in copies:
        copy.wait()


def body(innovation, background, level_weight):
    levels, rows, width = innovation.shape
    if rows != HALF or width % (PACK * LANES) or levels != 4:
        raise NotImplementedError("slab shape")
    nblocks = width // LANES
    both, half = 2 * rows, rows // 2
    count = lax.axis_size("row")
    chip = [(i, i ^ 1) for i in range(count) if i ^ 1 < count]
    away = [(i, j) for i in range(count) for j in [((i + 1) ^ 1) - 1] if 0 <= j < count]
    hbm = [pltpu.with_memory_space_constraint(x, pltpu.HBM) for x in (level_weight, innovation, background)]
    band = jnp.asarray(zonal_band())
    piece = jax.ShapeDtypeStruct((nblocks // PIECES, 2, both, LANES), BF16)
    result = jax.ShapeDtypeStruct((2, rows, width), F32)
    *raws, outer, row, inno, back, weight = pl.pallas_call(
        outer_kernel,
        out_shape=[piece] * PIECES
        + [
            jax.ShapeDtypeStruct((outer_rows(rows, nblocks, levels), LANES), BF16),
            jax.ShapeDtypeStruct((TILE, width), BF16),
            jax.ShapeDtypeStruct(innovation.shape, BF16),
            jax.ShapeDtypeStruct(background.shape, BF16),
            jax.ShapeDtypeStruct((2 * levels, 2 * LANES), F32),
        ],
        in_specs=[HBM] * 3,
        out_specs=[VMEM] * (PIECES + 5),
        scratch_shapes=[
            pltpu.SMEM((levels,), F32),
            pltpu.VMEM((2, PACK * (3 * levels - 2), PACK * levels * TILE), BF16),
            pltpu.VMEM((nblocks, LANES), F32),
            pltpu.SemaphoreType.DMA((2, len(CUTS) - 1)),
            pltpu.SemaphoreType.DMA((2,)),
            pltpu.SemaphoreType.DMA,
        ],
        compiler_params=PARAMS,
        name="outer_half",
    )(*hbm)
    outer_got = lax.ppermute(outer, "row", away)
    row = lax.ppermute(row, "row", chip)
    *raws, inner = pl.pallas_call(
        inner_kernel,
        out_shape=[piece] * PIECES + [jax.ShapeDtypeStruct((inner_rows(rows, nblocks), LANES), BF16)],
        in_specs=[VMEM] * (5 + PIECES),
        out_specs=[VMEM] * (PIECES + 1),
        scratch_shapes=[pltpu.VMEM((nblocks, LANES), F32)],
        input_output_aliases={5 + k: k for k in range(PIECES)},
        compiler_params=PARAMS,
        name="inner_half",
    )(weight, inno, back, row, band, *raws)
    inner_got = lax.ppermute(inner, "row", away)
    nears = [lax.ppermute(r, "row", chip) for r in raws]
    edges = pl.pallas_call(
        outermost_kernel,
        out_shape=jax.ShapeDtypeStruct((TILE, width), BF16),
        in_specs=[VMEM] * 3,
        out_specs=VMEM,
        compiler_params=PARAMS,
        name="outermost_rows",
    )(weight, outer, outer_got)
    near_edges = lax.ppermute(edges, "row", chip)
    out, part, last = pl.pallas_call(
        near_kernel,
        out_shape=[result, result, jax.ShapeDtypeStruct((half, 3 * half), BF16)],
        in_specs=[VMEM] * (2 * PIECES + 4),
        out_specs=[HBM] + [VMEM] * 2,
        scratch_shapes=[pltpu.VMEM((nblocks, 2 * both, LANES), BF16), pltpu.SemaphoreType.DMA((2,))],
        compiler_params=PARAMS,
        name="near_part",
    )(*raws, *nears, edges, near_edges, outer_got, band)
    return pl.pallas_call(
        last_kernel,
        out_shape=result,
        in_specs=[VMEM] * 3 + [HBM],
        out_specs=HBM,
        input_output_aliases={3: 0},
        scratch_shapes=[pltpu.VMEM((2, half, width), F32), pltpu.SemaphoreType.DMA((2,))],
        compiler_params=PARAMS,
        name="last_part",
    )(last, part, inner_got, out)


def solution(mesh):
    placed = (P("member", "row", None), P("member", "row", None), P())
    return jax.shard_map(
        body, mesh=mesh, in_specs=placed, out_specs=P("member", "row", None), check_vma=False
    )
```

```python
import math

import jax
import jax.numpy as jnp
import numpy as np
from jax import lax
from jax.experimental import pallas as pl
from jax.experimental.pallas import tpu as pltpu
from jax.sharding import PartitionSpec as P

HALF = 64
SIGMA = 64
LANES = 128
TILE = 16
SPREAD, LOWEST, LEAST = 250.0, 125.0, 1e-35
PACK = 8
CUTS = (0, 8, 16)
PIECES = 4
F32 = jnp.float32
BF16 = jnp.bfloat16
NORM = math.sqrt(sum(math.exp(-k * k / (SIGMA * SIGMA)) for k in range(-HALF, HALF + 1)))

VMEM = pl.BlockSpec(memory_space=pltpu.VMEM)
HBM = pl.BlockSpec(memory_space=pltpu.HBM)
PARAMS = pltpu.CompilerParams(vmem_limit_bytes=40 * 1024 * 1024)


def split(values):
    high = values.astype(BF16)
    return high, (values - high.astype(F32)).astype(BF16)


def encode(parts):
    top = jnp.max(jnp.concatenate([jnp.abs(x) for x in parts], axis=0), axis=0, keepdims=True)
    top = (top * 1.01).astype(BF16).astype(F32)
    scale = SPREAD / jnp.maximum(top, LEAST)
    codes = []
    for x in parts:
        size = jnp.exp2(jnp.abs(x) * scale - LOWEST)
        codes.append(jnp.where(x < 0, -size, size))
    return codes, top


def decode(codes, top):
    codes = codes.astype(F32)
    size = (jnp.log2(jnp.maximum(jnp.abs(codes), 2.0**-LOWEST)) + LOWEST) * (jnp.maximum(top, LEAST) * (1.0 / SPREAD))
    return jnp.where(codes < 0, -size, size)


def dot(left, right):
    return jnp.dot(left, right, preferred_element_type=F32)


def iota(shape, dim):
    return lax.broadcasted_iota(jnp.int32, shape, dim)


def one_hot(mask, value=1.0):
    return jnp.where(mask, value, 0.0).astype(BF16)


def difference(off):
    return (jnp.where(off == 1, 1.0, 0.0) - jnp.where(off == -1, 1.0, 0.0)).astype(BF16)


def taps(offset):
    off = offset.astype(F32)
    value = jnp.exp(off * off * (-0.5 / (SIGMA * SIGMA))) * (1.0 / NORM)
    return jnp.where(jnp.abs(offset) <= HALF, value, 0.0)


def zonal_band():
    offset = np.arange(4 * LANES)[:, None] - LANES - np.arange(2 * LANES)[None, :]
    band = np.exp(-offset * offset / (2.0 * SIGMA * SIGMA)) / NORM
    band = np.where(np.abs(offset) <= HALF, band, 0.0).astype(np.float32)
    high = band.astype(BF16)
    return np.stack([high, (band - high.astype(np.float32)).astype(BF16)])


def window(first, nblocks):
    low, high = max(first - 1, 0), min(first + 3, nblocks)
    return low, high, (low - first + 1) * LANES, (high - first + 1) * LANES


def smooth_x(band_ref, load, first, nblocks):
    low, high, top, bottom = window(first, nblocks)
    both = jnp.concatenate([load(k) for k in range(low, high)], axis=1)
    rows = both.shape[0] // 2
    found = dot(both, band_ref[0, top:bottom, :])
    return found[:rows] + found[rows:] + dot(both[:rows], band_ref[1, top:bottom, :])


def parity():
    return lax.rem(lax.axis_index("row"), 2)


def block_of(refs, k):
    per = refs[0].shape[0]
    return refs[k // per].at[k % per]


def tile_at(row):
    return pl.ds(pl.multiple_of(row, TILE), TILE)


def half_of(ref, comp_rows, start, part):
    half = comp_rows // 2
    return [ref[part, pl.ds(pl.multiple_of(comp * comp_rows + start, TILE), half), :] for comp in range(2)]


def raw_pair(first, weight, inno_ref, back_ref, upper, diff_y, diff_x, extra, raw_refs):
    levels, rows, width = inno_ref.shape
    half = rows // 2
    start = pl.multiple_of(jnp.where(upper, 0, half), TILE)
    exact = pl.ds(start, half)
    deep = pl.ds(pl.multiple_of(jnp.where(upper, 0, half - TILE), TILE), half + TILE)
    here = pl.ds(first * LANES, 2 * LANES)
    low, high, top, bottom = window(first, width // LANES)
    around = back_ref[:, exact, low * LANES : high * LANES]
    grad_xs = dot(around.reshape(levels * half, -1), diff_x[top:bottom])
    numer_y = numer_x = 0.0
    denom = 1.0
    for level in range(levels):
        grad_y = dot(diff_y, back_ref[level, deep, here])
        if extra is not None:
            grad_y += extra(level, here)
        grad_x = grad_xs[level * half : (level + 1) * half]
        scaled = inno_ref[level, exact, here].astype(F32) * (0.5 * weight(level))
        numer_y += scaled * grad_y
        numer_x += scaled * grad_x
        denom += (0.25 * weight(level)) * (grad_y * grad_y + grad_x * grad_x)
    inverse = 1.0 / denom
    found = []
    for comp, numer in enumerate((numer_y, numer_x)):
        raw = numer * inverse
        if extra is None:
            raw = jnp.where(iota(raw.shape, 0) == jnp.where(upper, 0, half - 1), 0.0, raw)
        found.append(raw)
        at = pl.ds(pl.multiple_of(comp * rows + start, TILE), half)
        for part, values in enumerate(split(raw)):
            for j in range(2):
                block_of(raw_refs, first + j)[part, at, :] = values[:, j * LANES : (j + 1) * LANES]
    return found


def differences(upper, half):
    deep = half + TILE
    diff_y = difference(iota((half, deep), 1) - iota((half, deep), 0) - jnp.where(upper, 0, TILE))
    shape = (4 * LANES, 2 * LANES)
    return diff_y, difference(iota(shape, 0) - LANES - iota(shape, 1))


def outer_kernel(lw_hbm, inno_hbm, back_hbm, *refs):
    *raw_refs, msg_ref, row_ref, inno_ref, back_ref, weight_ref, lw_ref, pick_ref, top_ref, sems, rest_sems, lw_sem = refs
    levels, rows, width = inno_ref.shape
    half = rows // 2
    deep = half + TILE
    nblocks = width // LANES
    upper = parity() == 0
    start = jnp.where(upper, 0, half)
    cuts = [cut * nblocks // CUTS[-1] * LANES for cut in CUTS]

    def bring(sem, which, at, size, cols):
        index = (slice(None), pl.ds(pl.multiple_of(at, TILE), size), cols)
        source, target = ((inno_hbm, inno_ref), (back_hbm, back_ref))[which]
        return pltpu.make_async_copy(source.at[index], target.at[index], sem)

    weights = pltpu.make_async_copy(lw_hbm, lw_ref, lw_sem)
    copies = []
    for q, cut in enumerate(cuts[:-1]):
        cols = pl.ds(cut, cuts[q + 1] - cut)
        copies.append(
            [
                bring(sems.at[1, q], 1, jnp.where(upper, 0, rows - deep), deep, cols),
                bring(sems.at[0, q], 0, start, half, cols),
            ]
        )
    copies[-1].append(bring(rest_sems.at[1], 1, jnp.where(upper, deep, 0), rows - deep, pl.ds(0, width)))
    other = bring(rest_sems.at[0], 0, half - start, half, pl.ds(0, width))
    weights.start()
    for copy in sum(copies, []) + [other]:
        copy.start()
    diff_y, diff_x = differences(upper, half)
    outermost_row = iota((half, 2 * LANES), 0) == jnp.where(upper, 0, half - 1)
    kinds = 3 * levels - 2
    row, col = iota(pick_ref.shape[1:], 0), iota(pick_ref.shape[1:], 1)
    want = row - (col >> 6) * kinds
    level = (col >> 4) & (levels - 1)
    place = col & (TILE - 1)
    outermost = place == jnp.where(upper, 0, TILE - 1)
    next_row = place == jnp.where(upper, 1, TILE - 2)
    pick_ref[0] = one_hot(((want == level) & outermost) | ((want == levels + level) & next_row))
    pick_ref[1] = one_hot((want == 2 * levels + level - 2) & (level >= 2) & outermost)
    shape = (TILE, levels * TILE)
    pick_near = one_hot(iota(shape, 1) == iota(shape, 0) * TILE + jnp.where(upper, TILE - 1, 0))
    weights.wait()
    for level in range(2 * levels):
        weight_ref[level : level + 1, :] = jnp.full((1, weight_ref.shape[1]), lw_ref[level % levels])
    base = nblocks * rows

    def input_rows():
        near_rows = back_ref[:, tile_at(jnp.where(upper, rows - TILE, 0)), :]
        row_ref[...] = dot(pick_near, near_rows.reshape(levels * TILE, -1)).astype(BF16)
        edge_at = tile_at(jnp.where(upper, 0, rows - TILE))
        for first in range(0, nblocks, PACK):
            back, inno = [], []
            for k in range(first, first + PACK):
                here = pl.ds(k * LANES, LANES)
                back.append(back_ref[:, edge_at, here].reshape(levels * TILE, LANES))
                inno.append(inno_ref[:, edge_at, here].reshape(levels * TILE, LANES))
            tile = dot(pick_ref[0], jnp.concatenate(back, axis=0)) + dot(pick_ref[1], jnp.concatenate(inno, axis=0))
            at = base + nblocks + first * kinds
            msg_ref[pl.ds(at, PACK * kinds), :] = tile.astype(BF16)

    waited = 0
    for first in range(0, nblocks, 2):
        while cuts[waited] < window(first, nblocks)[1] * LANES:
            for copy in copies[waited]:
                copy.wait()
            waited += 1
        if first == cuts[-2] // LANES:
            input_rows()
        found = raw_pair(first, lambda k: lw_ref[k], inno_ref, back_ref, upper, diff_y, diff_x, None, raw_refs)
        codes, top = encode(found)
        for comp, code in enumerate(codes):
            inno = inno_ref[comp, pl.ds(pl.multiple_of(start, TILE), half), pl.ds(first * LANES, 2 * LANES)]
            code = jnp.where(outermost_row, inno.astype(F32), code).astype(BF16)
            for j in range(2):
                msg_ref[pl.ds((first + j) * rows + comp * half, half), :] = code[:, j * LANES : (j + 1) * LANES]
        for j in range(2):
            top_ref[first + j : first + j + 1, :] = top[:, j * LANES : (j + 1) * LANES]
    msg_ref[pl.ds(base, nblocks), :] = top_ref[...].astype(BF16)
    other.wait()


def outer_rows(rows, nblocks, levels):
    return nblocks * rows + nblocks + nblocks * (3 * levels - 2)


def inner_kernel(weight_ref, inno_ref, back_ref, row_ref, band_ref, *refs):
    raw_refs = refs[PIECES : 2 * PIECES]
    msg_ref, top_ref = refs[2 * PIECES :]
    _, rows, width = inno_ref.shape
    half = rows // 2
    nblocks = width // LANES
    upper = parity() == 1
    start = jnp.where(upper, 0, half)
    diff_y, diff_x = differences(upper, half)
    at = iota((half, 2 * LANES), 0) == jnp.where(upper, 0, half - 1)
    sign = jnp.where(upper, -1.0, 1.0)

    def extra(level, here):
        return jnp.where(at, row_ref[level : level + 1, here].astype(F32) * sign, 0.0)

    def weight(level):
        return weight_ref[level : level + 1, :]

    def load(k):
        block = block_of(raw_refs, k)
        return jnp.concatenate(half_of(block, rows, start, 0) + half_of(block, rows, start, 1), axis=0)

    for first in range(0, nblocks, 2):
        raw_pair(first, weight, inno_ref, back_ref, upper, diff_y, diff_x, extra, raw_refs)
    for first in range(0, nblocks, 2):
        (code,), top = encode([smooth_x(band_ref, load, first, nblocks)])
        code = code.astype(BF16)
        for j in range(2):
            msg_ref[pl.ds((first + j) * rows, rows), :] = code[:, j * LANES : (j + 1) * LANES]
            top_ref[first + j : first + j + 1, :] = top[:, j * LANES : (j + 1) * LANES]
    msg_ref[pl.ds(nblocks * rows, nblocks), :] = top_ref[...].astype(BF16)


def inner_rows(rows, nblocks):
    return nblocks * rows + nblocks


def outermost_kernel(weight_ref, own_ref, got_ref, out_ref):
    nblocks = out_ref.shape[1] // LANES
    levels = weight_ref.shape[0] // 2
    kinds = 3 * levels - 2
    base = own_ref.shape[0] - nblocks * kinds
    rows, half = HALF, HALF // 2
    first_core = parity() == 0
    at = iota((8, rows), 0) * half

    def unpacked(ref, upper):
        packs = [ref[pl.ds(base + k * kinds, PACK * kinds), :].astype(F32) for k in range(0, nblocks, PACK)]
        pick = one_hot((iota((8, rows), 1) == at + jnp.where(upper, 0, half - 1)) & (at < rows))
        some = []
        for k in range(0, nblocks, 2):
            pair = [ref[pl.ds((k + j) * rows, rows), :] for j in range(2)]
            some.append(dot(pick, jnp.concatenate(pair, axis=1))[:2])
        found = []
        for low, high in ((0, levels), (levels, 2 * levels), (2 * levels, kinds)):
            parts = [p[j * kinds + low : j * kinds + high] for p in packs for j in range(PACK)]
            found.append(jnp.concatenate(parts, axis=1))
        found[2] = jnp.concatenate([jnp.concatenate(some, axis=1), found[2]], axis=0)
        return found

    own, got = unpacked(own_ref, first_core), unpacked(got_ref, jnp.logical_not(first_core))
    here = jnp.concatenate([own[0], got[0]], axis=0)
    beyond = jnp.concatenate([got[0], own[0]], axis=0)
    before = jnp.concatenate([own[1], got[1]], axis=0)
    inno = jnp.concatenate([own[2], got[2]], axis=0)
    shape = here.shape
    grad_y = jnp.where((iota(shape, 0) < levels) == first_core, before - beyond, beyond - before)
    lane = iota(shape, 1)
    left = jnp.where(lane == 0, 0.0, pltpu.roll(here, 1, 1))
    right = jnp.where(lane == shape[1] - 1, 0.0, pltpu.roll(here, shape[1] - 1, 1))
    grad_x = right - left
    weight = jnp.concatenate([weight_ref[:, :LANES]] * nblocks, axis=1)
    scaled = inno * (0.5 * weight)

    def total(values):
        return [sum(values[k : k + 1] for k in range(f, f + levels)) for f in (0, levels)]

    numer_y, numer_x = total(scaled * grad_y), total(scaled * grad_x)
    denom = total((0.25 * weight) * (grad_y * grad_y + grad_x * grad_x))
    found = []
    for k in range(2):
        inverse = 1.0 / (1.0 + denom[k])
        found += [numer_y[k] * inverse, numer_x[k] * inverse]
    high, low = split(jnp.concatenate(found, axis=0))
    none = jnp.zeros((TILE - 8, shape[1]), F32)
    out_ref[...] = jnp.concatenate([high.astype(F32), low.astype(F32), none], axis=0).astype(BF16)


def far_taps(rows, towards):
    side = 2 * parity() - 1
    half = rows // 2
    start = jnp.where((side < 0) == towards, half, 0)
    return taps(iota((rows, half), 1) + start - iota((rows, half), 0) + side * rows)


def near_kernel(*refs):
    raw_refs, near_refs = refs[:PIECES], refs[PIECES : 2 * PIECES]
    edges_ref, near_edges_ref, msg_ref, band_ref, out_ref, taps_ref, total_ref = refs[2 * PIECES :]
    _, rows, width = out_ref.shape
    nblocks = width // LANES
    half = rows // 2
    par = parity()
    side = 1 - 2 * par
    offset = iota((rows, rows), 1) - iota((rows, rows), 0)
    near_taps = jnp.concatenate([taps(offset), taps(offset + side * rows)], axis=1)
    column = iota(near_taps.shape, 1)
    outermost = (column == par * (rows - 1)) | (column == (2 - par) * rows - 1 + par)
    near_taps = jnp.where(outermost, 0.0, near_taps)
    toward = far_taps(rows, True)
    outermost = iota(toward.shape, 1) == jnp.where(par == 0, half - 1, 0)
    toward = jnp.where(outermost, 0.0, toward)
    outermost = iota((half, 2 * LANES), 0) == jnp.where(par == 0, half - 1, 0)
    low_taps = jnp.concatenate([near_taps, toward], axis=1).astype(BF16)
    shape = (rows, TILE)
    kind = iota(shape, 1)
    own_at = jnp.where(par == 0, 0, rows - 1)
    far_at = jnp.where(par == 0, -1, rows)
    near_at = jnp.where(par == 0, 2 * rows - 1, -rows)
    own_edges = taps(jnp.where(kind & 2 == 0, own_at, far_at) - iota(shape, 0))
    near_edges = jnp.where(kind & 2 == 0, taps(near_at - iota(shape, 0)), 0.0)
    stacked = []
    for comp in range(2):
        here = (kind < 8) & (kind & 1 == comp)
        all_taps = [near_taps, toward, jnp.where(here, own_edges, 0.0), jnp.where(here, near_edges, 0.0)]
        stacked.append(jnp.concatenate(split(jnp.concatenate(all_taps, axis=1)), axis=0))
    tops = msg_ref[pl.ds(nblocks * rows, nblocks), :].astype(F32)
    for first in range(0, nblocks, 2):
        cols = pl.ds(first * LANES, 2 * LANES)
        top = jnp.concatenate([tops[k : k + 1] for k in (first, first + 1)], axis=1)
        edges = [edges_ref[:, cols], near_edges_ref[:, cols]]
        for comp in range(2):
            here = pl.ds(comp * rows, rows)
            both, got = [], []
            for k in (first, first + 1):
                refs = (block_of(raw_refs, k), block_of(near_refs, k))
                both.append([jnp.concatenate([ref[part, here, :] for ref in refs], axis=0) for part in range(2)])
                got.append(msg_ref[pl.ds(k * rows + comp * half, half), :])
            got = decode(jnp.concatenate(got, axis=1), top)
            got = split(jnp.where(outermost, 0.0, got))
            highs, lows = (
                jnp.concatenate([jnp.concatenate([x[part] for x in both], axis=1), got[part]], axis=0) for part in range(2)
            )
            part = dot(stacked[comp], jnp.concatenate([highs] + edges, axis=0))
            high, low = split(part[:rows] + part[rows:] + dot(low_taps, lows))
            for j in range(2):
                cut = slice(j * LANES, (j + 1) * LANES)
                total_ref[first + j, pl.ds(comp * rows, rows), :] = high[:, cut]
                total_ref[first + j, pl.ds((2 + comp) * rows, rows), :] = low[:, cut]
    for first in range(0, nblocks, 2):
        result = smooth_x(band_ref, lambda k: total_ref[k], first, nblocks)
        here = pl.ds(first * LANES, 2 * LANES)
        out_ref[0, :, here] = result[:rows]
        out_ref[1, :, here] = result[rows:]
    away = far_taps(rows, False)
    high, low = split(jnp.where(par == 0, away[:half], away[half:]))
    taps_ref[...] = jnp.concatenate([high, low, high], axis=1)


def last_kernel(taps_ref, part_ref, msg_ref, out_hbm, buf, sem):
    _, rows, width = part_ref.shape
    nblocks = width // LANES
    half = rows // 2
    tops = msg_ref[pl.ds(nblocks * rows, nblocks), :].astype(F32)
    reached = pl.ds(pl.multiple_of(parity() * half, 8), half)
    rest = pl.ds(pl.multiple_of((1 - parity()) * half, 8), half)
    copies = [pltpu.make_async_copy(part_ref.at[k, rest, :], out_hbm.at[k, rest, :], sem.at[2 + k]) for k in range(2)]
    for copy in copies:
        copy.start()
    for comp in range(2):
        for first in range(0, nblocks, 2):
            here = pl.ds(first * LANES, 2 * LANES)
            top = jnp.concatenate([tops[k : k + 1] for k in (first, first + 1)], axis=1)
            got = [msg_ref[pl.ds((first + j) * rows + comp * half, half), :] for j in range(2)]
            high, low = split(decode(jnp.concatenate(got, axis=1), top))
            part = dot(taps_ref[...], jnp.concatenate([high, high, low], axis=0))
            buf[comp, :, here] = part_ref[comp, reached, here] + part
        copies.append(pltpu.make_async_copy(buf.at[comp], out_hbm.at[comp, reached, :], sem.at[comp]))
        copies[-1].start()
    for copy in copies:
        copy.wait()


def body(innovation, background, level_weight):
    levels, rows, width = innovation.shape
    if rows != HALF or width % (PACK * LANES) or levels != 4:
        raise NotImplementedError("slab shape")
    nblocks = width // LANES
    both, half = 2 * rows, rows // 2
    count = lax.axis_size("row")
    chip = [(i, i ^ 1) for i in range(count) if i ^ 1 < count]
    away = [(i, j) for i in range(count) for j in [((i + 1) ^ 1) - 1] if 0 <= j < count]
    hbm = [pltpu.with_memory_space_constraint(x, pltpu.HBM) for x in (level_weight, innovation, background)]
    band = jnp.asarray(zonal_band())
    piece = jax.ShapeDtypeStruct((nblocks // PIECES, 2, both, LANES), BF16)
    result = jax.ShapeDtypeStruct((2, rows, width), F32)
    *raws, outer, row, inno, back, weight = pl.pallas_call(
        outer_kernel,
        out_shape=[piece] * PIECES
        + [
            jax.ShapeDtypeStruct((outer_rows(rows, nblocks, levels), LANES), BF16),
            jax.ShapeDtypeStruct((TILE, width), BF16),
            jax.ShapeDtypeStruct(innovation.shape, BF16),
            jax.ShapeDtypeStruct(background.shape, BF16),
            jax.ShapeDtypeStruct((2 * levels, 2 * LANES), F32),
        ],
        in_specs=[HBM] * 3,
        out_specs=[VMEM] * (PIECES + 5),
        scratch_shapes=[
            pltpu.SMEM((levels,), F32),
            pltpu.VMEM((2, PACK * (3 * levels - 2), PACK * levels * TILE), BF16),
            pltpu.VMEM((nblocks, LANES), F32),
            pltpu.SemaphoreType.DMA((2, len(CUTS) - 1)),
            pltpu.SemaphoreType.DMA((2,)),
            pltpu.SemaphoreType.DMA,
        ],
        compiler_params=PARAMS,
        name="outer_half",
    )(*hbm)
    outer_got = lax.ppermute(outer, "row", away)
    row = lax.ppermute(row, "row", chip)
    *raws, inner = pl.pallas_call(
        inner_kernel,
        out_shape=[piece] * PIECES + [jax.ShapeDtypeStruct((inner_rows(rows, nblocks), LANES), BF16)],
        in_specs=[VMEM] * (5 + PIECES),
        out_specs=[VMEM] * (PIECES + 1),
        scratch_shapes=[pltpu.VMEM((nblocks, LANES), F32)],
        input_output_aliases={5 + k: k for k in range(PIECES)},
        compiler_params=PARAMS,
        name="inner_half",
    )(weight, inno, back, row, band, *raws)
    inner_got = lax.ppermute(inner, "row", away)
    nears = [lax.ppermute(r, "row", chip) for r in raws]
    edges = pl.pallas_call(
        outermost_kernel,
        out_shape=jax.ShapeDtypeStruct((TILE, width), BF16),
        in_specs=[VMEM] * 3,
        out_specs=VMEM,
        compiler_params=PARAMS,
        name="outermost_rows",
    )(weight, outer, outer_got)
    near_edges = lax.ppermute(edges, "row", chip)
    part, last = pl.pallas_call(
        near_kernel,
        out_shape=[result, jax.ShapeDtypeStruct((half, 3 * half), BF16)],
        in_specs=[VMEM] * (2 * PIECES + 4),
        out_specs=[VMEM] * 2,
        scratch_shapes=[pltpu.VMEM((nblocks, 2 * both, LANES), BF16)],
        compiler_params=PARAMS,
        name="near_part",
    )(*raws, *nears, edges, near_edges, outer_got, band)
    return pl.pallas_call(
        last_kernel,
        out_shape=result,
        in_specs=[VMEM] * 3,
        out_specs=HBM,
        scratch_shapes=[pltpu.VMEM((2, half, width), F32), pltpu.SemaphoreType.DMA((4,))],
        compiler_params=PARAMS,
        name="last_part",
    )(last, part, inner_got)


def solution(mesh):
    placed = (P("member", "row", None), P("member", "row", None), P())
    return jax.shard_map(
        body, mesh=mesh, in_specs=placed, out_specs=P("member", "row", None), check_vma=False
    )
```

```python
import math

import jax
import jax.numpy as jnp
import numpy as np
from jax import lax
from jax.experimental import pallas as pl
from jax.experimental.pallas import tpu as pltpu
from jax.sharding import PartitionSpec as P

HALF = 64
SIGMA = 64
LANES = 128
TILE = 16
SPREAD, LOWEST, LEAST = 250.0, 125.0, 1e-35
PACK = 8
CUTS = (0, 8, 16)
PIECES = 4
F32 = jnp.float32
BF16 = jnp.bfloat16
NORM = math.sqrt(sum(math.exp(-k * k / (SIGMA * SIGMA)) for k in range(-HALF, HALF + 1)))

VMEM = pl.BlockSpec(memory_space=pltpu.VMEM)
HBM = pl.BlockSpec(memory_space=pltpu.HBM)
PARAMS = pltpu.CompilerParams(vmem_limit_bytes=40 * 1024 * 1024)


def split(values):
    high = values.astype(BF16)
    return high, (values - high.astype(F32)).astype(BF16)


def encode(parts):
    top = jnp.max(jnp.concatenate([jnp.abs(x) for x in parts], axis=0), axis=0, keepdims=True)
    top = (top * 1.01).astype(BF16).astype(F32)
    scale = SPREAD / jnp.maximum(top, LEAST)
    codes = []
    for x in parts:
        size = jnp.exp2(jnp.abs(x) * scale - LOWEST)
        codes.append(jnp.where(x < 0, -size, size))
    return codes, top


def decode(codes, top):
    codes = codes.astype(F32)
    size = (jnp.log2(jnp.maximum(jnp.abs(codes), 2.0**-LOWEST)) + LOWEST) * (jnp.maximum(top, LEAST) * (1.0 / SPREAD))
    return jnp.where(codes < 0, -size, size)


def dot(left, right):
    return jnp.dot(left, right, preferred_element_type=F32)


def iota(shape, dim):
    return lax.broadcasted_iota(jnp.int32, shape, dim)


def one_hot(mask, value=1.0):
    return jnp.where(mask, value, 0.0).astype(BF16)


def difference(off):
    return (jnp.where(off == 1, 1.0, 0.0) - jnp.where(off == -1, 1.0, 0.0)).astype(BF16)


def taps(offset):
    off = offset.astype(F32)
    value = jnp.exp(off * off * (-0.5 / (SIGMA * SIGMA))) * (1.0 / NORM)
    return jnp.where(jnp.abs(offset) <= HALF, value, 0.0)


def zonal_band():
    offset = np.arange(4 * LANES)[:, None] - LANES - np.arange(2 * LANES)[None, :]
    band = np.exp(-offset * offset / (2.0 * SIGMA * SIGMA)) / NORM
    band = np.where(np.abs(offset) <= HALF, band, 0.0).astype(np.float32)
    high = band.astype(BF16)
    return np.stack([high, (band - high.astype(np.float32)).astype(BF16)])


def window(first, nblocks):
    low, high = max(first - 1, 0), min(first + 3, nblocks)
    return low, high, (low - first + 1) * LANES, (high - first + 1) * LANES


def smooth_x(band_ref, load, first, nblocks):
    low, high, top, bottom = window(first, nblocks)
    both = jnp.concatenate([load(k) for k in range(low, high)], axis=1)
    rows = both.shape[0] // 2
    found = dot(both, band_ref[0, top:bottom, :])
    return found[:rows] + found[rows:] + dot(both[:rows], band_ref[1, top:bottom, :])


def parity():
    return lax.rem(lax.axis_index("row"), 2)


def block_of(refs, k):
    per = refs[0].shape[0]
    return refs[k // per].at[k % per]


def tile_at(row):
    return pl.ds(pl.multiple_of(row, TILE), TILE)


def raw_pair(first, weight, inno_ref, back_ref, upper, diff_y, diff_x, extra, raw_refs):
    levels, rows, width = inno_ref.shape
    half = rows // 2
    start = pl.multiple_of(jnp.where(upper, 0, half), TILE)
    exact = pl.ds(start, half)
    deep = pl.ds(pl.multiple_of(jnp.where(upper, 0, half - TILE), TILE), half + TILE)
    here = pl.ds(first * LANES, 2 * LANES)
    low, high, top, bottom = window(first, width // LANES)
    around = back_ref[:, exact, low * LANES : high * LANES]
    grad_xs = dot(around.reshape(levels * half, -1), diff_x[top:bottom])
    numer_y = numer_x = 0.0
    denom = 1.0
    for level in range(levels):
        grad_y = dot(diff_y, back_ref[level, deep, here])
        if extra is not None:
            grad_y += extra(level, here)
        grad_x = grad_xs[level * half : (level + 1) * half]
        scaled = inno_ref[level, exact, here].astype(F32) * (0.5 * weight(level))
        numer_y += scaled * grad_y
        numer_x += scaled * grad_x
        denom += (0.25 * weight(level)) * (grad_y * grad_y + grad_x * grad_x)
    inverse = 1.0 / denom
    found = []
    for comp, numer in enumerate((numer_y, numer_x)):
        raw = numer * inverse
        if extra is None:
            raw = jnp.where(iota(raw.shape, 0) == jnp.where(upper, 0, half - 1), 0.0, raw)
        found.append(raw)
        at = pl.ds(pl.multiple_of(comp * rows + start, TILE), half)
        for j in range(2):
            block_of(raw_refs, first + j)[at, :] = raw[:, j * LANES : (j + 1) * LANES]
    return found


def differences(upper, half):
    deep = half + TILE
    diff_y = difference(iota((half, deep), 1) - iota((half, deep), 0) - jnp.where(upper, 0, TILE))
    shape = (4 * LANES, 2 * LANES)
    return diff_y, difference(iota(shape, 0) - LANES - iota(shape, 1))


def outer_kernel(lw_hbm, inno_hbm, back_hbm, *refs):
    *raw_refs, msg_ref, row_ref, inno_ref, back_ref, weight_ref, lw_ref, pick_ref, top_ref, sems, rest_sems, lw_sem = refs
    levels, rows, width = inno_ref.shape
    half = rows // 2
    deep = half + TILE
    nblocks = width // LANES
    upper = parity() == 0
    start = jnp.where(upper, 0, half)
    cuts = [cut * nblocks // CUTS[-1] * LANES for cut in CUTS]

    def bring(sem, which, at, size, cols):
        index = (slice(None), pl.ds(pl.multiple_of(at, TILE), size), cols)
        source, target = ((inno_hbm, inno_ref), (back_hbm, back_ref))[which]
        return pltpu.make_async_copy(source.at[index], target.at[index], sem)

    weights = pltpu.make_async_copy(lw_hbm, lw_ref, lw_sem)
    copies = []
    for q, cut in enumerate(cuts[:-1]):
        cols = pl.ds(cut, cuts[q + 1] - cut)
        copies.append(
            [
                bring(sems.at[1, q], 1, jnp.where(upper, 0, rows - deep), deep, cols),
                bring(sems.at[0, q], 0, start, half, cols),
            ]
        )
    copies[-1].append(bring(rest_sems.at[1], 1, jnp.where(upper, deep, 0), rows - deep, pl.ds(0, width)))
    other = bring(rest_sems.at[0], 0, half - start, half, pl.ds(0, width))
    weights.start()
    for copy in sum(copies, []) + [other]:
        copy.start()
    diff_y, diff_x = differences(upper, half)
    outermost_row = iota((half, 2 * LANES), 0) == jnp.where(upper, 0, half - 1)
    kinds = 3 * levels - 2
    row, col = iota(pick_ref.shape[1:], 0), iota(pick_ref.shape[1:], 1)
    want = row - (col >> 6) * kinds
    level = (col >> 4) & (levels - 1)
    place = col & (TILE - 1)
    outermost = place == jnp.where(upper, 0, TILE - 1)
    next_row = place == jnp.where(upper, 1, TILE - 2)
    pick_ref[0] = one_hot(((want == level) & outermost) | ((want == levels + level) & next_row))
    pick_ref[1] = one_hot((want == 2 * levels + level - 2) & (level >= 2) & outermost)
    shape = (TILE, levels * TILE)
    pick_near = one_hot(iota(shape, 1) == iota(shape, 0) * TILE + jnp.where(upper, TILE - 1, 0))
    weights.wait()
    for level in range(2 * levels):
        weight_ref[level : level + 1, :] = jnp.full((1, weight_ref.shape[1]), lw_ref[level % levels])
    base = nblocks * rows

    def input_rows():
        near_rows = back_ref[:, tile_at(jnp.where(upper, rows - TILE, 0)), :]
        row_ref[...] = dot(pick_near, near_rows.reshape(levels * TILE, -1)).astype(BF16)
        edge_at = tile_at(jnp.where(upper, 0, rows - TILE))
        for first in range(0, nblocks, PACK):
            back, inno = [], []
            for k in range(first, first + PACK):
                here = pl.ds(k * LANES, LANES)
                back.append(back_ref[:, edge_at, here].reshape(levels * TILE, LANES))
                inno.append(inno_ref[:, edge_at, here].reshape(levels * TILE, LANES))
            tile = dot(pick_ref[0], jnp.concatenate(back, axis=0)) + dot(pick_ref[1], jnp.concatenate(inno, axis=0))
            at = base + nblocks + first * kinds
            msg_ref[pl.ds(at, PACK * kinds), :] = tile.astype(BF16)

    waited = 0
    for first in range(0, nblocks, 2):
        while cuts[waited] < window(first, nblocks)[1] * LANES:
            for copy in copies[waited]:
                copy.wait()
            waited += 1
        if first == cuts[-2] // LANES:
            input_rows()
        found = raw_pair(first, lambda k: lw_ref[k], inno_ref, back_ref, upper, diff_y, diff_x, None, raw_refs)
        codes, top = encode(found)
        for comp, code in enumerate(codes):
            inno = inno_ref[comp, pl.ds(pl.multiple_of(start, TILE), half), pl.ds(first * LANES, 2 * LANES)]
            code = jnp.where(outermost_row, inno.astype(F32), code).astype(BF16)
            for j in range(2):
                msg_ref[pl.ds((first + j) * rows + comp * half, half), :] = code[:, j * LANES : (j + 1) * LANES]
        for j in range(2):
            top_ref[first + j : first + j + 1, :] = top[:, j * LANES : (j + 1) * LANES]
    msg_ref[pl.ds(base, nblocks), :] = top_ref[...].astype(BF16)
    other.wait()


def outer_rows(rows, nblocks, levels):
    return nblocks * rows + nblocks + nblocks * (3 * levels - 2)


def inner_kernel(weight_ref, inno_ref, back_ref, row_ref, band_ref, *refs):
    raw_refs = refs[PIECES : 2 * PIECES]
    msg_ref, top_ref, both_ref = refs[2 * PIECES :]
    _, rows, width = inno_ref.shape
    half = rows // 2
    nblocks = width // LANES
    upper = parity() == 1
    start = jnp.where(upper, 0, half)
    diff_y, diff_x = differences(upper, half)
    at = iota((half, 2 * LANES), 0) == jnp.where(upper, 0, half - 1)
    sign = jnp.where(upper, -1.0, 1.0)

    def extra(level, here):
        return jnp.where(at, row_ref[level : level + 1, here].astype(F32) * sign, 0.0)

    def weight(level):
        return weight_ref[level : level + 1, :]

    for first in range(0, nblocks, 2):
        found = raw_pair(first, weight, inno_ref, back_ref, upper, diff_y, diff_x, extra, raw_refs)
        both = jnp.concatenate(split(jnp.concatenate(found, axis=0)), axis=0)
        for j in range(2):
            both_ref[first + j] = both[:, j * LANES : (j + 1) * LANES]
    for first in range(0, nblocks, 2):
        (code,), top = encode([smooth_x(band_ref, lambda k: both_ref[k], first, nblocks)])
        code = code.astype(BF16)
        for j in range(2):
            msg_ref[pl.ds((first + j) * rows, rows), :] = code[:, j * LANES : (j + 1) * LANES]
            top_ref[first + j : first + j + 1, :] = top[:, j * LANES : (j + 1) * LANES]
    msg_ref[pl.ds(nblocks * rows, nblocks), :] = top_ref[...].astype(BF16)


def inner_rows(rows, nblocks):
    return nblocks * rows + nblocks


def outermost_kernel(weight_ref, own_ref, got_ref, out_ref):
    nblocks = out_ref.shape[1] // LANES
    levels = weight_ref.shape[0] // 2
    kinds = 3 * levels - 2
    base = own_ref.shape[0] - nblocks * kinds
    rows, half = HALF, HALF // 2
    first_core = parity() == 0
    at = iota((8, rows), 0) * half

    def unpacked(ref, upper):
        packs = [ref[pl.ds(base + k * kinds, PACK * kinds), :].astype(F32) for k in range(0, nblocks, PACK)]
        pick = one_hot((iota((8, rows), 1) == at + jnp.where(upper, 0, half - 1)) & (at < rows))
        some = []
        for k in range(0, nblocks, 2):
            pair = [ref[pl.ds((k + j) * rows, rows), :] for j in range(2)]
            some.append(dot(pick, jnp.concatenate(pair, axis=1))[:2])
        found = []
        for low, high in ((0, levels), (levels, 2 * levels), (2 * levels, kinds)):
            parts = [p[j * kinds + low : j * kinds + high] for p in packs for j in range(PACK)]
            found.append(jnp.concatenate(parts, axis=1))
        found[2] = jnp.concatenate([jnp.concatenate(some, axis=1), found[2]], axis=0)
        return found

    own, got = unpacked(own_ref, first_core), unpacked(got_ref, jnp.logical_not(first_core))
    here = jnp.concatenate([own[0], got[0]], axis=0)
    beyond = jnp.concatenate([got[0], own[0]], axis=0)
    before = jnp.concatenate([own[1], got[1]], axis=0)
    inno = jnp.concatenate([own[2], got[2]], axis=0)
    shape = here.shape
    grad_y = jnp.where((iota(shape, 0) < levels) == first_core, before - beyond, beyond - before)
    lane = iota(shape, 1)
    left = jnp.where(lane == 0, 0.0, pltpu.roll(here, 1, 1))
    right = jnp.where(lane == shape[1] - 1, 0.0, pltpu.roll(here, shape[1] - 1, 1))
    grad_x = right - left
    weight = jnp.concatenate([weight_ref[:, :LANES]] * nblocks, axis=1)
    scaled = inno * (0.5 * weight)

    def total(values):
        return [sum(values[k : k + 1] for k in range(f, f + levels)) for f in (0, levels)]

    numer_y, numer_x = total(scaled * grad_y), total(scaled * grad_x)
    denom = total((0.25 * weight) * (grad_y * grad_y + grad_x * grad_x))
    found = []
    for k in range(2):
        inverse = 1.0 / (1.0 + denom[k])
        found += [numer_y[k] * inverse, numer_x[k] * inverse]
    high, low = split(jnp.concatenate(found, axis=0))
    none = jnp.zeros((TILE - 8, shape[1]), F32)
    out_ref[...] = jnp.concatenate([high.astype(F32), low.astype(F32), none], axis=0).astype(BF16)


def far_taps(rows, towards):
    side = 2 * parity() - 1
    half = rows // 2
    start = jnp.where((side < 0) == towards, half, 0)
    return taps(iota((rows, half), 1) + start - iota((rows, half), 0) + side * rows)


def near_kernel(*refs):
    raw_refs, near_refs = refs[:PIECES], refs[PIECES : 2 * PIECES]
    edges_ref, near_edges_ref, msg_ref, band_ref, out_ref, taps_ref, total_ref = refs[2 * PIECES :]
    _, rows, width = out_ref.shape
    nblocks = width // LANES
    half = rows // 2
    par = parity()
    side = 1 - 2 * par
    offset = iota((rows, rows), 1) - iota((rows, rows), 0)
    near_taps = jnp.concatenate([taps(offset), taps(offset + side * rows)], axis=1)
    column = iota(near_taps.shape, 1)
    outermost = (column == par * (rows - 1)) | (column == (2 - par) * rows - 1 + par)
    near_taps = jnp.where(outermost, 0.0, near_taps)
    toward = far_taps(rows, True)
    outermost = iota(toward.shape, 1) == jnp.where(par == 0, half - 1, 0)
    toward = jnp.where(outermost, 0.0, toward)
    outermost = iota((half, 2 * LANES), 0) == jnp.where(par == 0, half - 1, 0)
    low_taps = jnp.concatenate([near_taps, toward], axis=1).astype(BF16)
    shape = (rows, TILE)
    kind = iota(shape, 1)
    own_at = jnp.where(par == 0, 0, rows - 1)
    far_at = jnp.where(par == 0, -1, rows)
    near_at = jnp.where(par == 0, 2 * rows - 1, -rows)
    own_edges = taps(jnp.where(kind & 2 == 0, own_at, far_at) - iota(shape, 0))
    near_edges = jnp.where(kind & 2 == 0, taps(near_at - iota(shape, 0)), 0.0)
    stacked = []
    for comp in range(2):
        here = (kind < 8) & (kind & 1 == comp)
        all_taps = [near_taps, toward, jnp.where(here, own_edges, 0.0), jnp.where(here, near_edges, 0.0)]
        stacked.append(jnp.concatenate(split(jnp.concatenate(all_taps, axis=1)), axis=0))
    tops = msg_ref[pl.ds(nblocks * rows, nblocks), :].astype(F32)
    for first in range(0, nblocks, 2):
        cols = pl.ds(first * LANES, 2 * LANES)
        top = jnp.concatenate([tops[k : k + 1] for k in (first, first + 1)], axis=1)
        edges = [edges_ref[:, cols], near_edges_ref[:, cols]]
        for comp in range(2):
            here = pl.ds(comp * rows, rows)
            both, got = [], []
            for k in (first, first + 1):
                refs = (block_of(raw_refs, k), block_of(near_refs, k))
                both.append(jnp.concatenate([ref[here, :] for ref in refs], axis=0))
                got.append(msg_ref[pl.ds(k * rows + comp * half, half), :])
            got = decode(jnp.concatenate(got, axis=1), top)
            got = split(jnp.where(outermost, 0.0, got))
            highs, lows = (
                jnp.concatenate([x, y], axis=0) for x, y in zip(split(jnp.concatenate(both, axis=1)), got)
            )
            part = dot(stacked[comp], jnp.concatenate([highs] + edges, axis=0))
            high, low = split(part[:rows] + part[rows:] + dot(low_taps, lows))
            for j in range(2):
                cut = slice(j * LANES, (j + 1) * LANES)
                total_ref[first + j, pl.ds(comp * rows, rows), :] = high[:, cut]
                total_ref[first + j, pl.ds((2 + comp) * rows, rows), :] = low[:, cut]
    for first in range(0, nblocks, 2):
        result = smooth_x(band_ref, lambda k: total_ref[k], first, nblocks)
        here = pl.ds(first * LANES, 2 * LANES)
        out_ref[0, :, here] = result[:rows]
        out_ref[1, :, here] = result[rows:]
    away = far_taps(rows, False)
    high, low = split(jnp.where(par == 0, away[:half], away[half:]))
    taps_ref[...] = jnp.concatenate([high, low, high], axis=1)


def last_kernel(taps_ref, part_ref, msg_ref, out_hbm, buf, sem):
    _, rows, width = part_ref.shape
    nblocks = width // LANES
    half = rows // 2
    tops = msg_ref[pl.ds(nblocks * rows, nblocks), :].astype(F32)
    reached = pl.ds(pl.multiple_of(parity() * half, 8), half)
    rest = pl.ds(pl.multiple_of((1 - parity()) * half, 8), half)
    copies = [pltpu.make_async_copy(part_ref.at[k, rest, :], out_hbm.at[k, rest, :], sem.at[2 + k]) for k in range(2)]
    for copy in copies:
        copy.start()
    for comp in range(2):
        for first in range(0, nblocks, 2):
            here = pl.ds(first * LANES, 2 * LANES)
            top = jnp.concatenate([tops[k : k + 1] for k in (first, first + 1)], axis=1)
            got = [msg_ref[pl.ds((first + j) * rows + comp * half, half), :] for j in range(2)]
            high, low = split(decode(jnp.concatenate(got, axis=1), top))
            part = dot(taps_ref[...], jnp.concatenate([high, high, low], axis=0))
            buf[comp, :, here] = part_ref[comp, reached, here] + part
        copies.append(pltpu.make_async_copy(buf.at[comp], out_hbm.at[comp, reached, :], sem.at[comp]))
        copies[-1].start()
    for copy in copies:
        copy.wait()


def body(innovation, background, level_weight):
    levels, rows, width = innovation.shape
    if rows != HALF or width % (PACK * LANES) or levels != 4:
        raise NotImplementedError("slab shape")
    nblocks = width // LANES
    both, half = 2 * rows, rows // 2
    count = lax.axis_size("row")
    chip = [(i, i ^ 1) for i in range(count) if i ^ 1 < count]
    away = [(i, j) for i in range(count) for j in [((i + 1) ^ 1) - 1] if 0 <= j < count]
    hbm = [pltpu.with_memory_space_constraint(x, pltpu.HBM) for x in (level_weight, innovation, background)]
    band = jnp.asarray(zonal_band())
    piece = jax.ShapeDtypeStruct((nblocks // PIECES, both, LANES), F32)
    result = jax.ShapeDtypeStruct((2, rows, width), F32)
    *raws, outer, row, inno, back, weight = pl.pallas_call(
        outer_kernel,
        out_shape=[piece] * PIECES
        + [
            jax.ShapeDtypeStruct((outer_rows(rows, nblocks, levels), LANES), BF16),
            jax.ShapeDtypeStruct((TILE, width), BF16),
            jax.ShapeDtypeStruct(innovation.shape, BF16),
            jax.ShapeDtypeStruct(background.shape, BF16),
            jax.ShapeDtypeStruct((2 * levels, 2 * LANES), F32),
        ],
        in_specs=[HBM] * 3,
        out_specs=[VMEM] * (PIECES + 5),
        scratch_shapes=[
            pltpu.SMEM((levels,), F32),
            pltpu.VMEM((2, PACK * (3 * levels - 2), PACK * levels * TILE), BF16),
            pltpu.VMEM((nblocks, LANES), F32),
            pltpu.SemaphoreType.DMA((2, len(CUTS) - 1)),
            pltpu.SemaphoreType.DMA((2,)),
            pltpu.SemaphoreType.DMA,
        ],
        compiler_params=PARAMS,
        name="outer_half",
    )(*hbm)
    outer_got = lax.ppermute(outer, "row", away)
    row = lax.ppermute(row, "row", chip)
    *raws, inner = pl.pallas_call(
        inner_kernel,
        out_shape=[piece] * PIECES + [jax.ShapeDtypeStruct((inner_rows(rows, nblocks), LANES), BF16)],
        in_specs=[VMEM] * (5 + PIECES),
        out_specs=[VMEM] * (PIECES + 1),
        scratch_shapes=[pltpu.VMEM((nblocks, LANES), F32), pltpu.VMEM((nblocks, both, LANES), BF16)],
        input_output_aliases={5 + k: k for k in range(PIECES)},
        compiler_params=PARAMS,
        name="inner_half",
    )(weight, inno, back, row, band, *raws)
    inner_got = lax.ppermute(inner, "row", away)
    nears = [lax.ppermute(r, "row", chip) for r in raws]
    edges = pl.pallas_call(
        outermost_kernel,
        out_shape=jax.ShapeDtypeStruct((TILE, width), BF16),
        in_specs=[VMEM] * 3,
        out_specs=VMEM,
        compiler_params=PARAMS,
        name="outermost_rows",
    )(weight, outer, outer_got)
    near_edges = lax.ppermute(edges, "row", chip)
    part, last = pl.pallas_call(
        near_kernel,
        out_shape=[result, jax.ShapeDtypeStruct((half, 3 * half), BF16)],
        in_specs=[VMEM] * (2 * PIECES + 4),
        out_specs=[VMEM] * 2,
        scratch_shapes=[pltpu.VMEM((nblocks, 2 * both, LANES), BF16)],
        compiler_params=PARAMS,
        name="near_part",
    )(*raws, *nears, edges, near_edges, outer_got, band)
    return pl.pallas_call(
        last_kernel,
        out_shape=result,
        in_specs=[VMEM] * 3,
        out_specs=HBM,
        scratch_shapes=[pltpu.VMEM((2, half, width), F32), pltpu.SemaphoreType.DMA((4,))],
        compiler_params=PARAMS,
        name="last_part",
    )(last, part, inner_got)


def solution(mesh):
    placed = (P("member", "row", None), P("member", "row", None), P())
    return jax.shard_map(
        body, mesh=mesh, in_specs=placed, out_specs=P("member", "row", None), check_vma=False
    )
```

```python
import math

import jax
import jax.numpy as jnp
import numpy as np
from jax import lax
from jax.experimental import pallas as pl
from jax.experimental.pallas import tpu as pltpu
from jax.sharding import PartitionSpec as P

HALF = 64
SIGMA = 64
LANES = 128
TILE = 16
SPREAD, LOWEST, LEAST = 250.0, 125.0, 1e-35
PACK = 8
CUTS = (0, 8, 16)
PIECES = 4
F32 = jnp.float32
BF16 = jnp.bfloat16
NORM = math.sqrt(sum(math.exp(-k * k / (SIGMA * SIGMA)) for k in range(-HALF, HALF + 1)))

VMEM = pl.BlockSpec(memory_space=pltpu.VMEM)
HBM = pl.BlockSpec(memory_space=pltpu.HBM)
PARAMS = pltpu.CompilerParams(vmem_limit_bytes=40 * 1024 * 1024)


def split(values):
    high = values.astype(BF16)
    return high, (values - high.astype(F32)).astype(BF16)


def encode(parts):
    top = jnp.max(jnp.concatenate([jnp.abs(x) for x in parts], axis=0), axis=0, keepdims=True)
    top = (top * 1.01).astype(BF16).astype(F32)
    scale = SPREAD / jnp.maximum(top, LEAST)
    codes = []
    for x in parts:
        size = jnp.exp2(jnp.abs(x) * scale - LOWEST)
        codes.append(jnp.where(x < 0, -size, size))
    return codes, top


def decode(codes, top):
    codes = codes.astype(F32)
    size = (jnp.log2(jnp.maximum(jnp.abs(codes), 2.0**-LOWEST)) + LOWEST) * (jnp.maximum(top, LEAST) * (1.0 / SPREAD))
    return jnp.where(codes < 0, -size, size)


def dot(left, right):
    return jnp.dot(left, right, preferred_element_type=F32)


def iota(shape, dim):
    return lax.broadcasted_iota(jnp.int32, shape, dim)


def one_hot(mask, value=1.0):
    return jnp.where(mask, value, 0.0).astype(BF16)


def difference(off):
    return (jnp.where(off == 1, 1.0, 0.0) - jnp.where(off == -1, 1.0, 0.0)).astype(BF16)


def taps(offset):
    off = offset.astype(F32)
    value = jnp.exp(off * off * (-0.5 / (SIGMA * SIGMA))) * (1.0 / NORM)
    return jnp.where(jnp.abs(offset) <= HALF, value, 0.0)


def zonal_band():
    offset = np.arange(4 * LANES)[:, None] - LANES - np.arange(2 * LANES)[None, :]
    band = np.exp(-offset * offset / (2.0 * SIGMA * SIGMA)) / NORM
    band = np.where(np.abs(offset) <= HALF, band, 0.0).astype(np.float32)
    high = band.astype(BF16)
    return np.stack([high, (band - high.astype(np.float32)).astype(BF16)])


def window(first, nblocks):
    low, high = max(first - 1, 0), min(first + 3, nblocks)
    return low, high, (low - first + 1) * LANES, (high - first + 1) * LANES


def smooth_x(band_ref, load, first, nblocks):
    low, high, top, bottom = window(first, nblocks)
    both = jnp.concatenate([load(k) for k in range(low, high)], axis=1)
    rows = both.shape[0] // 2
    found = dot(both, band_ref[0, top:bottom, :])
    return found[:rows] + found[rows:] + dot(both[:rows], band_ref[1, top:bottom, :])


def parity():
    return lax.rem(lax.axis_index("row"), 2)


def block_of(refs, k):
    per = refs[0].shape[0]
    return refs[k // per].at[k % per]


def tile_at(row):
    return pl.ds(pl.multiple_of(row, TILE), TILE)


def raw_pair(first, weight, inno_ref, back_ref, upper, diff_y, diff_x, extra, raw_refs):
    levels, rows, width = inno_ref.shape
    half = rows // 2
    start = pl.multiple_of(jnp.where(upper, 0, half), TILE)
    exact = pl.ds(start, half)
    deep = pl.ds(pl.multiple_of(jnp.where(upper, 0, half - TILE), TILE), half + TILE)
    here = pl.ds(first * LANES, 2 * LANES)
    low, high, top, bottom = window(first, width // LANES)
    around = back_ref[:, exact, low * LANES : high * LANES]
    grad_xs = dot(around.reshape(levels * half, -1), diff_x[top:bottom])
    numer_y = numer_x = 0.0
    denom = 1.0
    for level in range(levels):
        grad_y = dot(diff_y, back_ref[level, deep, here])
        if extra is not None:
            grad_y += extra(level, here)
        grad_x = grad_xs[level * half : (level + 1) * half]
        scaled = inno_ref[level, exact, here].astype(F32) * (0.5 * weight(level))
        numer_y += scaled * grad_y
        numer_x += scaled * grad_x
        denom += (0.25 * weight(level)) * (grad_y * grad_y + grad_x * grad_x)
    inverse = 1.0 / denom
    found = []
    for comp, numer in enumerate((numer_y, numer_x)):
        raw = numer * inverse
        if extra is None:
            raw = jnp.where(iota(raw.shape, 0) == jnp.where(upper, 0, half - 1), 0.0, raw)
        found.append(raw)
        at = pl.ds(pl.multiple_of(comp * rows + start, TILE), half)
        for j in range(2):
            block_of(raw_refs, first + j)[at, :] = raw[:, j * LANES : (j + 1) * LANES]
    return found


def differences(upper, half):
    deep = half + TILE
    diff_y = difference(iota((half, deep), 1) - iota((half, deep), 0) - jnp.where(upper, 0, TILE))
    shape = (4 * LANES, 2 * LANES)
    return diff_y, difference(iota(shape, 0) - LANES - iota(shape, 1))


def outer_kernel(lw_hbm, inno_hbm, back_hbm, *refs):
    *raw_refs, msg_ref, row_ref, inno_ref, back_ref, weight_ref, lw_ref, pick_ref, top_ref, sems, rest_sems, lw_sem = refs
    levels, rows, width = inno_ref.shape
    half = rows // 2
    deep = half + TILE
    nblocks = width // LANES
    upper = parity() == 0
    start = jnp.where(upper, 0, half)
    cuts = [cut * nblocks // CUTS[-1] * LANES for cut in CUTS]

    def bring(sem, which, at, size, cols):
        index = (slice(None), pl.ds(pl.multiple_of(at, TILE), size), cols)
        source, target = ((inno_hbm, inno_ref), (back_hbm, back_ref))[which]
        return pltpu.make_async_copy(source.at[index], target.at[index], sem)

    weights = pltpu.make_async_copy(lw_hbm, lw_ref, lw_sem)
    copies = []
    for q, cut in enumerate(cuts[:-1]):
        cols = pl.ds(cut, cuts[q + 1] - cut)
        copies.append(
            [
                bring(sems.at[1, q], 1, jnp.where(upper, 0, rows - deep), deep, cols),
                bring(sems.at[0, q], 0, start, half, cols),
            ]
        )
    copies[-1].append(bring(rest_sems.at[1], 1, jnp.where(upper, deep, 0), rows - deep, pl.ds(0, width)))
    other = bring(rest_sems.at[0], 0, half - start, half, pl.ds(0, width))
    weights.start()
    for copy in sum(copies, []) + [other]:
        copy.start()
    diff_y, diff_x = differences(upper, half)
    outermost_row = iota((half, 2 * LANES), 0) == jnp.where(upper, 0, half - 1)
    kinds = 3 * levels - 2
    row, col = iota(pick_ref.shape[1:], 0), iota(pick_ref.shape[1:], 1)
    want = row - (col >> 6) * kinds
    level = (col >> 4) & (levels - 1)
    place = col & (TILE - 1)
    outermost = place == jnp.where(upper, 0, TILE - 1)
    next_row = place == jnp.where(upper, 1, TILE - 2)
    pick_ref[0] = one_hot(((want == level) & outermost) | ((want == levels + level) & next_row))
    half_cols = PACK * (levels - 2) * TILE
    row, col = iota((PACK * kinds, half_cols), 0), iota((PACK * kinds, half_cols), 1)
    want = row - (col >> 5) * kinds
    level = (col >> 4) & 1
    pick_ref[1, :, :half_cols] = one_hot((want == 2 * levels + level) & (col & (TILE - 1) == jnp.where(upper, 0, TILE - 1)))
    shape = (TILE, levels * TILE)
    pick_near = one_hot(iota(shape, 1) == iota(shape, 0) * TILE + jnp.where(upper, TILE - 1, 0))
    weights.wait()
    for level in range(2 * levels):
        weight_ref[level : level + 1, :] = jnp.full((1, weight_ref.shape[1]), lw_ref[level % levels])
    base = nblocks * rows

    def input_rows():
        near_rows = back_ref[:, tile_at(jnp.where(upper, rows - TILE, 0)), :]
        row_ref[...] = dot(pick_near, near_rows.reshape(levels * TILE, -1)).astype(BF16)
        edge_at = tile_at(jnp.where(upper, 0, rows - TILE))
        for first in range(0, nblocks, PACK):
            back, inno = [], []
            for k in range(first, first + PACK):
                here = pl.ds(k * LANES, LANES)
                back.append(back_ref[:, edge_at, here].reshape(levels * TILE, LANES))
                inno.append(inno_ref[2:, edge_at, here].reshape((levels - 2) * TILE, LANES))
            tile = dot(pick_ref[0], jnp.concatenate(back, axis=0)) + dot(pick_ref[1, :, :half_cols], jnp.concatenate(inno, axis=0))
            at = base + nblocks + first * kinds
            msg_ref[pl.ds(at, PACK * kinds), :] = tile.astype(BF16)

    waited = 0
    for first in range(0, nblocks, 2):
        while cuts[waited] < window(first, nblocks)[1] * LANES:
            for copy in copies[waited]:
                copy.wait()
            waited += 1
        if first == cuts[-2] // LANES:
            input_rows()
        found = raw_pair(first, lambda k: lw_ref[k], inno_ref, back_ref, upper, diff_y, diff_x, None, raw_refs)
        codes, top = encode(found)
        for comp, code in enumerate(codes):
            inno = inno_ref[comp, pl.ds(pl.multiple_of(start, TILE), half), pl.ds(first * LANES, 2 * LANES)]
            code = jnp.where(outermost_row, inno.astype(F32), code).astype(BF16)
            for j in range(2):
                msg_ref[pl.ds((first + j) * rows + comp * half, half), :] = code[:, j * LANES : (j + 1) * LANES]
        for j in range(2):
            top_ref[first + j : first + j + 1, :] = top[:, j * LANES : (j + 1) * LANES]
    msg_ref[pl.ds(base, nblocks), :] = top_ref[...].astype(BF16)
    other.wait()


def outer_rows(rows, nblocks, levels):
    return nblocks * rows + nblocks + nblocks * (3 * levels - 2)


def inner_kernel(weight_ref, inno_ref, back_ref, row_ref, band_ref, *refs):
    raw_refs = refs[PIECES : 2 * PIECES]
    msg_ref, top_ref, both_ref = refs[2 * PIECES :]
    _, rows, width = inno_ref.shape
    half = rows // 2
    nblocks = width // LANES
    upper = parity() == 1
    start = jnp.where(upper, 0, half)
    diff_y, diff_x = differences(upper, half)
    at = iota((half, 2 * LANES), 0) == jnp.where(upper, 0, half - 1)
    sign = jnp.where(upper, -1.0, 1.0)

    def extra(level, here):
        return jnp.where(at, row_ref[level : level + 1, here].astype(F32) * sign, 0.0)

    def weight(level):
        return weight_ref[level : level + 1, :]

    for first in range(0, nblocks, 2):
        found = raw_pair(first, weight, inno_ref, back_ref, upper, diff_y, diff_x, extra, raw_refs)
        both = jnp.concatenate(split(jnp.concatenate(found, axis=0)), axis=0)
        for j in range(2):
            both_ref[first + j] = both[:, j * LANES : (j + 1) * LANES]
    for first in range(0, nblocks, 2):
        (code,), top = encode([smooth_x(band_ref, lambda k: both_ref[k], first, nblocks)])
        code = code.astype(BF16)
        for j in range(2):
            msg_ref[pl.ds((first + j) * rows, rows), :] = code[:, j * LANES : (j + 1) * LANES]
            top_ref[first + j : first + j + 1, :] = top[:, j * LANES : (j + 1) * LANES]
    msg_ref[pl.ds(nblocks * rows, nblocks), :] = top_ref[...].astype(BF16)


def inner_rows(rows, nblocks):
    return nblocks * rows + nblocks


def outermost_kernel(weight_ref, own_ref, got_ref, out_ref):
    nblocks = out_ref.shape[1] // LANES
    levels = weight_ref.shape[0] // 2
    kinds = 3 * levels - 2
    base = own_ref.shape[0] - nblocks * kinds
    rows, half = HALF, HALF // 2
    first_core = parity() == 0
    at = iota((8, rows), 0) * half

    def unpacked(ref, upper):
        packs = [ref[pl.ds(base + k * kinds, PACK * kinds), :].astype(F32) for k in range(0, nblocks, PACK)]
        pick = one_hot((iota((8, rows), 1) == at + jnp.where(upper, 0, half - 1)) & (at < rows))
        some = []
        for k in range(0, nblocks, 2):
            pair = [ref[pl.ds((k + j) * rows, rows), :] for j in range(2)]
            some.append(dot(pick, jnp.concatenate(pair, axis=1))[:2])
        found = []
        for low, high in ((0, levels), (levels, 2 * levels), (2 * levels, kinds)):
            parts = [p[j * kinds + low : j * kinds + high] for p in packs for j in range(PACK)]
            found.append(jnp.concatenate(parts, axis=1))
        found[2] = jnp.concatenate([jnp.concatenate(some, axis=1), found[2]], axis=0)
        return found

    own, got = unpacked(own_ref, first_core), unpacked(got_ref, jnp.logical_not(first_core))
    here = jnp.concatenate([own[0], got[0]], axis=0)
    beyond = jnp.concatenate([got[0], own[0]], axis=0)
    before = jnp.concatenate([own[1], got[1]], axis=0)
    inno = jnp.concatenate([own[2], got[2]], axis=0)
    shape = here.shape
    grad_y = jnp.where((iota(shape, 0) < levels) == first_core, before - beyond, beyond - before)
    lane = iota(shape, 1)
    left = jnp.where(lane == 0, 0.0, pltpu.roll(here, 1, 1))
    right = jnp.where(lane == shape[1] - 1, 0.0, pltpu.roll(here, shape[1] - 1, 1))
    grad_x = right - left
    weight = jnp.concatenate([weight_ref[:, :LANES]] * nblocks, axis=1)
    scaled = inno * (0.5 * weight)

    def total(values):
        return [sum(values[k : k + 1] for k in range(f, f + levels)) for f in (0, levels)]

    numer_y, numer_x = total(scaled * grad_y), total(scaled * grad_x)
    denom = total((0.25 * weight) * (grad_y * grad_y + grad_x * grad_x))
    found = []
    for k in range(2):
        inverse = 1.0 / (1.0 + denom[k])
        found += [numer_y[k] * inverse, numer_x[k] * inverse]
    high, low = split(jnp.concatenate(found, axis=0))
    none = jnp.zeros((TILE - 8, shape[1]), F32)
    out_ref[...] = jnp.concatenate([high.astype(F32), low.astype(F32), none], axis=0).astype(BF16)


def far_taps(rows, towards):
    side = 2 * parity() - 1
    half = rows // 2
    start = jnp.where((side < 0) == towards, half, 0)
    return taps(iota((rows, half), 1) + start - iota((rows, half), 0) + side * rows)


def near_kernel(*refs):
    raw_refs, near_refs = refs[:PIECES], refs[PIECES : 2 * PIECES]
    edges_ref, near_edges_ref, msg_ref, band_ref, out_ref, taps_ref, total_ref = refs[2 * PIECES :]
    _, rows, width = out_ref.shape
    nblocks = width // LANES
    half = rows // 2
    par = parity()
    side = 1 - 2 * par
    offset = iota((rows, rows), 1) - iota((rows, rows), 0)
    near_taps = jnp.concatenate([taps(offset), taps(offset + side * rows)], axis=1)
    column = iota(near_taps.shape, 1)
    outermost = (column == par * (rows - 1)) | (column == (2 - par) * rows - 1 + par)
    near_taps = jnp.where(outermost, 0.0, near_taps)
    toward = far_taps(rows, True)
    outermost = iota(toward.shape, 1) == jnp.where(par == 0, half - 1, 0)
    toward = jnp.where(outermost, 0.0, toward)
    outermost = iota((half, 2 * LANES), 0) == jnp.where(par == 0, half - 1, 0)
    low_taps = jnp.concatenate([near_taps, toward], axis=1).astype(BF16)
    shape = (rows, TILE)
    kind = iota(shape, 1)
    own_at = jnp.where(par == 0, 0, rows - 1)
    far_at = jnp.where(par == 0, -1, rows)
    near_at = jnp.where(par == 0, 2 * rows - 1, -rows)
    own_edges = taps(jnp.where(kind & 2 == 0, own_at, far_at) - iota(shape, 0))
    near_edges = jnp.where(kind & 2 == 0, taps(near_at - iota(shape, 0)), 0.0)
    stacked = []
    for comp in range(2):
        here = (kind < 8) & (kind & 1 == comp)
        all_taps = [near_taps, toward, jnp.where(here, own_edges, 0.0), jnp.where(here, near_edges, 0.0)]
        stacked.append(jnp.concatenate(split(jnp.concatenate(all_taps, axis=1)), axis=0))
    tops = msg_ref[pl.ds(nblocks * rows, nblocks), :].astype(F32)
    for first in range(0, nblocks, 2):
        cols = pl.ds(first * LANES, 2 * LANES)
        top = jnp.concatenate([tops[k : k + 1] for k in (first, first + 1)], axis=1)
        edges = [edges_ref[:, cols], near_edges_ref[:, cols]]
        for comp in range(2):
            here = pl.ds(comp * rows, rows)
            both, got = [], []
            for k in (first, first + 1):
                refs = (block_of(raw_refs, k), block_of(near_refs, k))
                both.append(jnp.concatenate([ref[here, :] for ref in refs], axis=0))
                got.append(msg_ref[pl.ds(k * rows + comp * half, half), :])
            got = decode(jnp.concatenate(got, axis=1), top)
            got = split(jnp.where(outermost, 0.0, got))
            highs, lows = (
                jnp.concatenate([x, y], axis=0) for x, y in zip(split(jnp.concatenate(both, axis=1)), got)
            )
            part = dot(stacked[comp], jnp.concatenate([highs] + edges, axis=0))
            high, low = split(part[:rows] + part[rows:] + dot(low_taps, lows))
            for j in range(2):
                cut = slice(j * LANES, (j + 1) * LANES)
                total_ref[first + j, pl.ds(comp * rows, rows), :] = high[:, cut]
                total_ref[first + j, pl.ds((2 + comp) * rows, rows), :] = low[:, cut]
    for first in range(0, nblocks, 2):
        result = smooth_x(band_ref, lambda k: total_ref[k], first, nblocks)
        here = pl.ds(first * LANES, 2 * LANES)
        out_ref[0, :, here] = result[:rows]
        out_ref[1, :, here] = result[rows:]
    away = far_taps(rows, False)
    high, low = split(jnp.where(par == 0, away[:half], away[half:]))
    taps_ref[...] = jnp.concatenate([high, low, high], axis=1)


def last_kernel(taps_ref, part_ref, msg_ref, out_hbm, buf, sem):
    _, rows, width = part_ref.shape
    nblocks = width // LANES
    half = rows // 2
    tops = msg_ref[pl.ds(nblocks * rows, nblocks), :].astype(F32)
    reached = pl.ds(pl.multiple_of(parity() * half, 8), half)
    rest = pl.ds(pl.multiple_of((1 - parity()) * half, 8), half)
    copies = [pltpu.make_async_copy(part_ref.at[k, rest, :], out_hbm.at[k, rest, :], sem.at[2 + k]) for k in range(2)]
    for copy in copies:
        copy.start()
    for comp in range(2):
        for first in range(0, nblocks, 2):
            here = pl.ds(first * LANES, 2 * LANES)
            top = jnp.concatenate([tops[k : k + 1] for k in (first, first + 1)], axis=1)
            got = [msg_ref[pl.ds((first + j) * rows + comp * half, half), :] for j in range(2)]
            high, low = split(decode(jnp.concatenate(got, axis=1), top))
            part = dot(taps_ref[...], jnp.concatenate([high, high, low], axis=0))
            buf[comp, :, here] = part_ref[comp, reached, here] + part
        copies.append(pltpu.make_async_copy(buf.at[comp], out_hbm.at[comp, reached, :], sem.at[comp]))
        copies[-1].start()
    for copy in copies:
        copy.wait()


def body(innovation, background, level_weight):
    levels, rows, width = innovation.shape
    if rows != HALF or width % (PACK * LANES) or levels != 4:
        raise NotImplementedError("slab shape")
    nblocks = width // LANES
    both, half = 2 * rows, rows // 2
    count = lax.axis_size("row")
    chip = [(i, i ^ 1) for i in range(count) if i ^ 1 < count]
    away = [(i, j) for i in range(count) for j in [((i + 1) ^ 1) - 1] if 0 <= j < count]
    hbm = [pltpu.with_memory_space_constraint(x, pltpu.HBM) for x in (level_weight, innovation, background)]
    band = jnp.asarray(zonal_band())
    piece = jax.ShapeDtypeStruct((nblocks // PIECES, both, LANES), F32)
    result = jax.ShapeDtypeStruct((2, rows, width), F32)
    *raws, outer, row, inno, back, weight = pl.pallas_call(
        outer_kernel,
        out_shape=[piece] * PIECES
        + [
            jax.ShapeDtypeStruct((outer_rows(rows, nblocks, levels), LANES), BF16),
            jax.ShapeDtypeStruct((TILE, width), BF16),
            jax.ShapeDtypeStruct(innovation.shape, BF16),
            jax.ShapeDtypeStruct(background.shape, BF16),
            jax.ShapeDtypeStruct((2 * levels, 2 * LANES), F32),
        ],
        in_specs=[HBM] * 3,
        out_specs=[VMEM] * (PIECES + 5),
        scratch_shapes=[
            pltpu.SMEM((levels,), F32),
            pltpu.VMEM((2, PACK * (3 * levels - 2), PACK * levels * TILE), BF16),
            pltpu.VMEM((nblocks, LANES), F32),
            pltpu.SemaphoreType.DMA((2, len(CUTS) - 1)),
            pltpu.SemaphoreType.DMA((2,)),
            pltpu.SemaphoreType.DMA,
        ],
        compiler_params=PARAMS,
        name="outer_half",
    )(*hbm)
    outer_got = lax.ppermute(outer, "row", away)
    row = lax.ppermute(row, "row", chip)
    *raws, inner = pl.pallas_call(
        inner_kernel,
        out_shape=[piece] * PIECES + [jax.ShapeDtypeStruct((inner_rows(rows, nblocks), LANES), BF16)],
        in_specs=[VMEM] * (5 + PIECES),
        out_specs=[VMEM] * (PIECES + 1),
        scratch_shapes=[pltpu.VMEM((nblocks, LANES), F32), pltpu.VMEM((nblocks, both, LANES), BF16)],
        input_output_aliases={5 + k: k for k in range(PIECES)},
        compiler_params=PARAMS,
        name="inner_half",
    )(weight, inno, back, row, band, *raws)
    inner_got = lax.ppermute(inner, "row", away)
    nears = [lax.ppermute(r, "row", chip) for r in raws]
    edges = pl.pallas_call(
        outermost_kernel,
        out_shape=jax.ShapeDtypeStruct((TILE, width), BF16),
        in_specs=[VMEM] * 3,
        out_specs=VMEM,
        compiler_params=PARAMS,
        name="outermost_rows",
    )(weight, outer, outer_got)
    near_edges = lax.ppermute(edges, "row", chip)
    part, last = pl.pallas_call(
        near_kernel,
        out_shape=[result, jax.ShapeDtypeStruct((half, 3 * half), BF16)],
        in_specs=[VMEM] * (2 * PIECES + 4),
        out_specs=[VMEM] * 2,
        scratch_shapes=[pltpu.VMEM((nblocks, 2 * both, LANES), BF16)],
        compiler_params=PARAMS,
        name="near_part",
    )(*raws, *nears, edges, near_edges, outer_got, band)
    return pl.pallas_call(
        last_kernel,
        out_shape=result,
        in_specs=[VMEM] * 3,
        out_specs=HBM,
        scratch_shapes=[pltpu.VMEM((2, half, width), F32), pltpu.SemaphoreType.DMA((4,))],
        compiler_params=PARAMS,
        name="last_part",
    )(last, part, inner_got)


def solution(mesh):
    placed = (P("member", "row", None), P("member", "row", None), P())
    return jax.shard_map(
        body, mesh=mesh, in_specs=placed, out_specs=P("member", "row", None), check_vma=False
    )
```

```python
import math

import jax
import jax.numpy as jnp
import numpy as np
from jax import lax
from jax.experimental import pallas as pl
from jax.experimental.pallas import tpu as pltpu
from jax.sharding import PartitionSpec as P

HALF = 64
SIGMA = 64
LANES = 128
TILE = 16
SPREAD, LOWEST, LEAST = 250.0, 125.0, 1e-35
PACK = 8
CUTS = (0, 8, 16)
PIECES = 4
F32 = jnp.float32
BF16 = jnp.bfloat16
NORM = math.sqrt(sum(math.exp(-k * k / (SIGMA * SIGMA)) for k in range(-HALF, HALF + 1)))

VMEM = pl.BlockSpec(memory_space=pltpu.VMEM)
HBM = pl.BlockSpec(memory_space=pltpu.HBM)
PARAMS = pltpu.CompilerParams(vmem_limit_bytes=40 * 1024 * 1024)


def split(values):
    high = values.astype(BF16)
    return high, (values - high.astype(F32)).astype(BF16)


def encode(parts):
    top = jnp.max(jnp.concatenate([jnp.abs(x) for x in parts], axis=0), axis=0, keepdims=True)
    top = (top * 1.01).astype(BF16).astype(F32)
    scale = SPREAD / jnp.maximum(top, LEAST)
    codes = []
    for x in parts:
        size = jnp.exp2(jnp.abs(x) * scale - LOWEST)
        codes.append(jnp.where(x < 0, -size, size))
    return codes, top


def decode(codes, top):
    codes = codes.astype(F32)
    size = (jnp.log2(jnp.maximum(jnp.abs(codes), 2.0**-LOWEST)) + LOWEST) * (jnp.maximum(top, LEAST) * (1.0 / SPREAD))
    return jnp.where(codes < 0, -size, size)


def dot(left, right):
    return jnp.dot(left, right, preferred_element_type=F32)


def iota(shape, dim):
    return lax.broadcasted_iota(jnp.int32, shape, dim)


def one_hot(mask, value=1.0):
    return jnp.where(mask, value, 0.0).astype(BF16)


def difference(off):
    return (jnp.where(off == 1, 1.0, 0.0) - jnp.where(off == -1, 1.0, 0.0)).astype(BF16)


def taps(offset):
    off = offset.astype(F32)
    value = jnp.exp(off * off * (-0.5 / (SIGMA * SIGMA))) * (1.0 / NORM)
    return jnp.where(jnp.abs(offset) <= HALF, value, 0.0)


def zonal_band():
    offset = np.arange(4 * LANES)[:, None] - LANES - np.arange(2 * LANES)[None, :]
    band = np.exp(-offset * offset / (2.0 * SIGMA * SIGMA)) / NORM
    band = np.where(np.abs(offset) <= HALF, band, 0.0).astype(np.float32)
    high = band.astype(BF16)
    return np.stack([high, (band - high.astype(np.float32)).astype(BF16)])


def window(first, nblocks):
    low, high = max(first - 1, 0), min(first + 3, nblocks)
    return low, high, (low - first + 1) * LANES, (high - first + 1) * LANES


def smooth_x(band_ref, load, first, nblocks):
    low, high, top, bottom = window(first, nblocks)
    both = jnp.concatenate([load(k) for k in range(low, high)], axis=1)
    rows = both.shape[0] // 2
    found = dot(both, band_ref[0, top:bottom, :])
    return found[:rows] + found[rows:] + dot(both[:rows], band_ref[1, top:bottom, :])


def parity():
    return lax.rem(lax.axis_index("row"), 2)


def block_of(refs, k):
    per = refs[0].shape[0]
    return refs[k // per].at[k % per]


def tile_at(row):
    return pl.ds(pl.multiple_of(row, TILE), TILE)


def raw_pair(first, weight, inno_ref, back_ref, upper, diff_y, diff_x, extra, raw_refs):
    levels, rows, width = inno_ref.shape
    half = rows // 2
    start = pl.multiple_of(jnp.where(upper, 0, half), TILE)
    exact = pl.ds(start, half)
    deep = pl.ds(pl.multiple_of(jnp.where(upper, 0, half - TILE), TILE), half + TILE)
    here = pl.ds(first * LANES, 2 * LANES)
    low, high, top, bottom = window(first, width // LANES)
    around = back_ref[:, exact, low * LANES : high * LANES]
    grad_xs = dot(around.reshape(levels * half, -1), diff_x[top:bottom])
    numer_y = numer_x = 0.0
    denom = 1.0
    for level in range(levels):
        grad_y = dot(diff_y, back_ref[level, deep, here])
        if extra is not None:
            grad_y += extra(level, here)
        grad_x = grad_xs[level * half : (level + 1) * half]
        scaled = inno_ref[level, exact, here].astype(F32) * (0.5 * weight(level))
        numer_y += scaled * grad_y
        numer_x += scaled * grad_x
        denom += (0.25 * weight(level)) * (grad_y * grad_y + grad_x * grad_x)
    inverse = 1.0 / denom
    found = []
    for comp, numer in enumerate((numer_y, numer_x)):
        raw = numer * inverse
        if extra is None:
            raw = jnp.where(iota(raw.shape, 0) == jnp.where(upper, 0, half - 1), 0.0, raw)
        found.append(raw)
        at = pl.ds(pl.multiple_of(comp * rows + start, TILE), half)
        for j in range(2):
            block_of(raw_refs, first + j)[at, :] = raw[:, j * LANES : (j + 1) * LANES]
    return found


def differences(upper, half):
    deep = half + TILE
    diff_y = difference(iota((half, deep), 1) - iota((half, deep), 0) - jnp.where(upper, 0, TILE))
    shape = (4 * LANES, 2 * LANES)
    return diff_y, difference(iota(shape, 0) - LANES - iota(shape, 1))


def outer_kernel(lw_hbm, inno_hbm, back_hbm, *refs):
    *raw_refs, msg_ref, row_ref, inno_ref, back_ref, weight_ref, lw_ref, pick_ref, top_ref, sems, rest_sems, lw_sem = refs
    levels, rows, width = inno_ref.shape
    half = rows // 2
    deep = half + TILE
    nblocks = width // LANES
    upper = parity() == 0
    start = jnp.where(upper, 0, half)
    cuts = [cut * nblocks // CUTS[-1] * LANES for cut in CUTS]

    def bring(sem, which, at, size, cols):
        index = (slice(None), pl.ds(pl.multiple_of(at, TILE), size), cols)
        source, target = ((inno_hbm, inno_ref), (back_hbm, back_ref))[which]
        return pltpu.make_async_copy(source.at[index], target.at[index], sem)

    weights = pltpu.make_async_copy(lw_hbm, lw_ref, lw_sem)
    copies = []
    for q, cut in enumerate(cuts[:-1]):
        cols = pl.ds(cut, cuts[q + 1] - cut)
        copies.append(
            [
                bring(sems.at[1, q], 1, jnp.where(upper, 0, rows - deep), deep, cols),
                bring(sems.at[0, q], 0, start, half, cols),
            ]
        )
    copies[-1].append(bring(rest_sems.at[1], 1, jnp.where(upper, deep, 0), rows - deep, pl.ds(0, width)))
    other = bring(rest_sems.at[0], 0, half - start, half, pl.ds(0, width))
    weights.start()
    for copy in sum(copies, []) + [other]:
        copy.start()
    diff_y, diff_x = differences(upper, half)
    outermost_row = iota((half, 2 * LANES), 0) == jnp.where(upper, 0, half - 1)
    kinds = 3 * levels - 2
    row, col = iota(pick_ref.shape[1:], 0), iota(pick_ref.shape[1:], 1)
    want = row - (col >> 6) * kinds
    level = (col >> 4) & (levels - 1)
    place = col & (TILE - 1)
    outermost = place == jnp.where(upper, 0, TILE - 1)
    next_row = place == jnp.where(upper, 1, TILE - 2)
    pick_ref[0] = one_hot(((want == level) & outermost) | ((want == levels + level) & next_row))
    half_cols = PACK * (levels - 2) * TILE
    row, col = iota((PACK * kinds, half_cols), 0), iota((PACK * kinds, half_cols), 1)
    want = row - (col >> 5) * kinds
    level = (col >> 4) & 1
    pick_ref[1, :, :half_cols] = one_hot((want == 2 * levels + level) & (col & (TILE - 1) == jnp.where(upper, 0, TILE - 1)))
    shape = (TILE, levels * TILE)
    pick_near = one_hot(iota(shape, 1) == iota(shape, 0) * TILE + jnp.where(upper, TILE - 1, 0))
    weights.wait()
    for level in range(2 * levels):
        weight_ref[level : level + 1, :] = jnp.full((1, weight_ref.shape[1]), lw_ref[level % levels])
    base = nblocks * rows

    def input_rows():
        near_rows = back_ref[:, tile_at(jnp.where(upper, rows - TILE, 0)), :]
        row_ref[...] = dot(pick_near, near_rows.reshape(levels * TILE, -1)).astype(BF16)
        edge_at = tile_at(jnp.where(upper, 0, rows - TILE))
        for first in range(0, nblocks, PACK):
            back, inno = [], []
            for k in range(first, first + PACK):
                here = pl.ds(k * LANES, LANES)
                back.append(back_ref[:, edge_at, here].reshape(levels * TILE, LANES))
                inno.append(inno_ref[2:, edge_at, here].reshape((levels - 2) * TILE, LANES))
            tile = dot(pick_ref[0], jnp.concatenate(back, axis=0)) + dot(pick_ref[1, :, :half_cols], jnp.concatenate(inno, axis=0))
            at = base + nblocks + first * kinds
            msg_ref[pl.ds(at, PACK * kinds), :] = tile.astype(BF16)

    waited = 0
    for first in range(0, nblocks, 2):
        while cuts[waited] < window(first, nblocks)[1] * LANES:
            for copy in copies[waited]:
                copy.wait()
            waited += 1
        if first == cuts[-2] // LANES:
            input_rows()
        found = raw_pair(first, lambda k: lw_ref[k], inno_ref, back_ref, upper, diff_y, diff_x, None, raw_refs)
        codes, top = encode(found)
        for comp, code in enumerate(codes):
            inno = inno_ref[comp, pl.ds(pl.multiple_of(start, TILE), half), pl.ds(first * LANES, 2 * LANES)]
            code = jnp.where(outermost_row, inno.astype(F32), code).astype(BF16)
            for j in range(2):
                msg_ref[pl.ds((first + j) * rows + comp * half, half), :] = code[:, j * LANES : (j + 1) * LANES]
        for j in range(2):
            top_ref[first + j : first + j + 1, :] = top[:, j * LANES : (j + 1) * LANES]
    msg_ref[pl.ds(base, nblocks), :] = top_ref[...].astype(BF16)
    other.wait()


def outer_rows(rows, nblocks, levels):
    return nblocks * rows + nblocks + nblocks * (3 * levels - 2)


def inner_kernel(weight_ref, inno_ref, back_ref, row_ref, band_ref, *refs):
    raw_refs = refs[PIECES : 2 * PIECES]
    msg_ref, top_ref, both_ref = refs[2 * PIECES :]
    _, rows, width = inno_ref.shape
    half = rows // 2
    nblocks = width // LANES
    upper = parity() == 1
    start = jnp.where(upper, 0, half)
    diff_y, diff_x = differences(upper, half)
    at = iota((half, 2 * LANES), 0) == jnp.where(upper, 0, half - 1)
    sign = jnp.where(upper, -1.0, 1.0)

    def extra(level, here):
        return jnp.where(at, row_ref[level : level + 1, here].astype(F32) * sign, 0.0)

    def weight(level):
        return weight_ref[level : level + 1, :]

    for first in range(0, nblocks, 2):
        found = raw_pair(first, weight, inno_ref, back_ref, upper, diff_y, diff_x, extra, raw_refs)
        both = jnp.concatenate(split(jnp.concatenate(found, axis=0)), axis=0)
        for j in range(2):
            both_ref[first + j] = both[:, j * LANES : (j + 1) * LANES]
    for first in range(0, nblocks, 2):
        (code,), top = encode([smooth_x(band_ref, lambda k: both_ref[k], first, nblocks)])
        code = code.astype(BF16)
        for j in range(2):
            msg_ref[pl.ds((first + j) * rows, rows), :] = code[:, j * LANES : (j + 1) * LANES]
            top_ref[first + j : first + j + 1, :] = top[:, j * LANES : (j + 1) * LANES]
    msg_ref[pl.ds(nblocks * rows, nblocks), :] = top_ref[...].astype(BF16)


def inner_rows(rows, nblocks):
    return nblocks * rows + nblocks


def outermost_kernel(weight_ref, own_ref, got_ref, out_ref):
    nblocks = out_ref.shape[1] // LANES
    levels = weight_ref.shape[0] // 2
    kinds = 3 * levels - 2
    base = own_ref.shape[0] - nblocks * kinds
    rows, half = HALF, HALF // 2
    first_core = parity() == 0
    at = iota((8, rows), 0) * half

    def unpacked(ref, upper):
        packs = [ref[pl.ds(base + k * kinds, PACK * kinds), :].astype(F32) for k in range(0, nblocks, PACK)]
        pick = one_hot((iota((8, rows), 1) == at + jnp.where(upper, 0, half - 1)) & (at < rows))
        some = []
        for k in range(0, nblocks, 2):
            pair = [ref[pl.ds((k + j) * rows, rows), :] for j in range(2)]
            some.append(dot(pick, jnp.concatenate(pair, axis=1))[:2])
        found = []
        for low, high in ((0, levels), (levels, 2 * levels), (2 * levels, kinds)):
            parts = [p[j * kinds + low : j * kinds + high] for p in packs for j in range(PACK)]
            found.append(jnp.concatenate(parts, axis=1))
        found[2] = jnp.concatenate([jnp.concatenate(some, axis=1), found[2]], axis=0)
        return found

    own, got = unpacked(own_ref, first_core), unpacked(got_ref, jnp.logical_not(first_core))
    here = jnp.concatenate([own[0], got[0]], axis=0)
    beyond = jnp.concatenate([got[0], own[0]], axis=0)
    before = jnp.concatenate([own[1], got[1]], axis=0)
    inno = jnp.concatenate([own[2], got[2]], axis=0)
    shape = here.shape
    grad_y = jnp.where((iota(shape, 0) < levels) == first_core, before - beyond, beyond - before)
    lane = iota(shape, 1)
    left = jnp.where(lane == 0, 0.0, pltpu.roll(here, 1, 1))
    right = jnp.where(lane == shape[1] - 1, 0.0, pltpu.roll(here, shape[1] - 1, 1))
    grad_x = right - left
    weight = jnp.concatenate([weight_ref[:, :LANES]] * nblocks, axis=1)
    scaled = inno * (0.5 * weight)

    def total(values):
        return [sum(values[k : k + 1] for k in range(f, f + levels)) for f in (0, levels)]

    numer_y, numer_x = total(scaled * grad_y), total(scaled * grad_x)
    denom = total((0.25 * weight) * (grad_y * grad_y + grad_x * grad_x))
    found = []
    for k in range(2):
        inverse = 1.0 / (1.0 + denom[k])
        found += [numer_y[k] * inverse, numer_x[k] * inverse]
    high, low = split(jnp.concatenate(found, axis=0))
    none = jnp.zeros((TILE - 8, shape[1]), F32)
    out_ref[...] = jnp.concatenate([high.astype(F32), low.astype(F32), none], axis=0).astype(BF16)


def far_taps(rows, towards):
    side = 2 * parity() - 1
    half = rows // 2
    start = jnp.where((side < 0) == towards, half, 0)
    return taps(iota((rows, half), 1) + start - iota((rows, half), 0) + side * rows)


def near_kernel(*refs):
    raw_refs, near_refs = refs[:PIECES], refs[PIECES : 2 * PIECES]
    edges_ref, near_edges_ref, msg_ref, band_ref, out_ref, taps_ref, total_ref = refs[2 * PIECES :]
    _, rows, width = out_ref.shape
    nblocks = width // LANES
    half = rows // 2
    par = parity()
    side = 1 - 2 * par
    offset = iota((rows, rows), 1) - iota((rows, rows), 0)
    near_taps = jnp.concatenate([taps(offset), taps(offset + side * rows)], axis=1)
    column = iota(near_taps.shape, 1)
    outermost = (column == par * (rows - 1)) | (column == (2 - par) * rows - 1 + par)
    near_taps = jnp.where(outermost, 0.0, near_taps)
    toward = far_taps(rows, True)
    outermost = iota(toward.shape, 1) == jnp.where(par == 0, half - 1, 0)
    toward = jnp.where(outermost, 0.0, toward)
    outermost = iota((half, 2 * LANES), 0) == jnp.where(par == 0, half - 1, 0)
    low_taps = jnp.concatenate([near_taps, toward], axis=1).astype(BF16)
    shape = (rows, TILE)
    kind = iota(shape, 1)
    own_at = jnp.where(par == 0, 0, rows - 1)
    far_at = jnp.where(par == 0, -1, rows)
    near_at = jnp.where(par == 0, 2 * rows - 1, -rows)
    own_edges = taps(jnp.where(kind & 2 == 0, own_at, far_at) - iota(shape, 0))
    near_edges = jnp.where(kind & 2 == 0, taps(near_at - iota(shape, 0)), 0.0)
    stacked = []
    for comp in range(2):
        here = (kind < 8) & (kind & 1 == comp)
        all_taps = [near_taps, toward, jnp.where(here, own_edges, 0.0), jnp.where(here, near_edges, 0.0)]
        stacked.append(jnp.concatenate(split(jnp.concatenate(all_taps, axis=1)), axis=0))
    tops = msg_ref[pl.ds(nblocks * rows, nblocks), :].astype(F32)
    for first in range(0, nblocks, 2):
        cols = pl.ds(first * LANES, 2 * LANES)
        top = jnp.concatenate([tops[k : k + 1] for k in (first, first + 1)], axis=1)
        edges = [edges_ref[:, cols], near_edges_ref[:, cols]]
        for comp in range(2):
            here = pl.ds(comp * rows, rows)
            both, got = [], []
            for k in (first, first + 1):
                refs = (block_of(raw_refs, k), block_of(near_refs, k))
                both.append(jnp.concatenate([ref[here, :] for ref in refs], axis=0))
                got.append(msg_ref[pl.ds(k * rows + comp * half, half), :])
            got = decode(jnp.concatenate(got, axis=1), top)
            got = split(jnp.where(outermost, 0.0, got))
            highs, lows = (
                jnp.concatenate([x, y], axis=0) for x, y in zip(split(jnp.concatenate(both, axis=1)), got)
            )
            part = dot(stacked[comp], jnp.concatenate([highs] + edges, axis=0))
            high, low = split(part[:rows] + part[rows:] + dot(low_taps, lows))
            for j in range(2):
                cut = slice(j * LANES, (j + 1) * LANES)
                total_ref[first + j, pl.ds(comp * rows, rows), :] = high[:, cut]
                total_ref[first + j, pl.ds((2 + comp) * rows, rows), :] = low[:, cut]
    for first in range(0, nblocks, 2):
        result = smooth_x(band_ref, lambda k: total_ref[k], first, nblocks)
        here = pl.ds(first * LANES, 2 * LANES)
        out_ref[0, :, here] = result[:rows]
        out_ref[1, :, here] = result[rows:]
    away = far_taps(rows, False)
    high, low = split(jnp.where(par == 0, away[:half], away[half:]))
    taps_ref[...] = jnp.concatenate([high, low, high], axis=1)


def last_kernel(taps_ref, part_ref, msg_ref, out_hbm, buf, sem):
    _, rows, width = part_ref.shape
    nblocks = width // LANES
    half = rows // 2
    tops = msg_ref[pl.ds(nblocks * rows, nblocks), :].astype(F32)
    reached = pl.ds(pl.multiple_of(parity() * half, 8), half)
    rest = pl.ds(pl.multiple_of((1 - parity()) * half, 8), half)
    copies = [pltpu.make_async_copy(part_ref.at[k, rest, :], out_hbm.at[k, rest, :], sem.at[k]) for k in range(2)]
    for copy in copies:
        copy.start()
    for comp in range(2):
        for first in range(0, nblocks, 2):
            here = pl.ds(first * LANES, 2 * LANES)
            top = jnp.concatenate([tops[k : k + 1] for k in (first, first + 1)], axis=1)
            got = [msg_ref[pl.ds((first + j) * rows + comp * half, half), :] for j in range(2)]
            high, low = split(decode(jnp.concatenate(got, axis=1), top))
            part = dot(taps_ref[...], jnp.concatenate([high, high, low], axis=0))
            buf[comp, :, here] = part_ref[comp, reached, here] + part
            if first + 2 in (nblocks // 2, nblocks):
                cols = pl.ds((first + 2 - nblocks // 2) * LANES, width // 2)
                at = 2 * comp + (first + 2) // nblocks
                copies.append(pltpu.make_async_copy(buf.at[comp, :, cols], out_hbm.at[comp, reached, cols], sem.at[2 + at]))
                copies[-1].start()
    for copy in copies:
        copy.wait()


def body(innovation, background, level_weight):
    levels, rows, width = innovation.shape
    if rows != HALF or width % (PACK * LANES) or levels != 4:
        raise NotImplementedError("slab shape")
    nblocks = width // LANES
    both, half = 2 * rows, rows // 2
    count = lax.axis_size("row")
    chip = [(i, i ^ 1) for i in range(count) if i ^ 1 < count]
    away = [(i, j) for i in range(count) for j in [((i + 1) ^ 1) - 1] if 0 <= j < count]
    hbm = [pltpu.with_memory_space_constraint(x, pltpu.HBM) for x in (level_weight, innovation, background)]
    band = jnp.asarray(zonal_band())
    piece = jax.ShapeDtypeStruct((nblocks // PIECES, both, LANES), F32)
    result = jax.ShapeDtypeStruct((2, rows, width), F32)
    *raws, outer, row, inno, back, weight = pl.pallas_call(
        outer_kernel,
        out_shape=[piece] * PIECES
        + [
            jax.ShapeDtypeStruct((outer_rows(rows, nblocks, levels), LANES), BF16),
            jax.ShapeDtypeStruct((TILE, width), BF16),
            jax.ShapeDtypeStruct(innovation.shape, BF16),
            jax.ShapeDtypeStruct(background.shape, BF16),
            jax.ShapeDtypeStruct((2 * levels, 2 * LANES), F32),
        ],
        in_specs=[HBM] * 3,
        out_specs=[VMEM] * (PIECES + 5),
        scratch_shapes=[
            pltpu.SMEM((levels,), F32),
            pltpu.VMEM((2, PACK * (3 * levels - 2), PACK * levels * TILE), BF16),
            pltpu.VMEM((nblocks, LANES), F32),
            pltpu.SemaphoreType.DMA((2, len(CUTS) - 1)),
            pltpu.SemaphoreType.DMA((2,)),
            pltpu.SemaphoreType.DMA,
        ],
        compiler_params=PARAMS,
        name="outer_half",
    )(*hbm)
    outer_got = lax.ppermute(outer, "row", away)
    row = lax.ppermute(row, "row", chip)
    *raws, inner = pl.pallas_call(
        inner_kernel,
        out_shape=[piece] * PIECES + [jax.ShapeDtypeStruct((inner_rows(rows, nblocks), LANES), BF16)],
        in_specs=[VMEM] * (5 + PIECES),
        out_specs=[VMEM] * (PIECES + 1),
        scratch_shapes=[pltpu.VMEM((nblocks, LANES), F32), pltpu.VMEM((nblocks, both, LANES), BF16)],
        input_output_aliases={5 + k: k for k in range(PIECES)},
        compiler_params=PARAMS,
        name="inner_half",
    )(weight, inno, back, row, band, *raws)
    inner_got = lax.ppermute(inner, "row", away)
    nears = [lax.ppermute(r, "row", chip) for r in raws]
    edges = pl.pallas_call(
        outermost_kernel,
        out_shape=jax.ShapeDtypeStruct((TILE, width), BF16),
        in_specs=[VMEM] * 3,
        out_specs=VMEM,
        compiler_params=PARAMS,
        name="outermost_rows",
    )(weight, outer, outer_got)
    near_edges = lax.ppermute(edges, "row", chip)
    part, last = pl.pallas_call(
        near_kernel,
        out_shape=[result, jax.ShapeDtypeStruct((half, 3 * half), BF16)],
        in_specs=[VMEM] * (2 * PIECES + 4),
        out_specs=[VMEM] * 2,
        scratch_shapes=[pltpu.VMEM((nblocks, 2 * both, LANES), BF16)],
        compiler_params=PARAMS,
        name="near_part",
    )(*raws, *nears, edges, near_edges, outer_got, band)
    return pl.pallas_call(
        last_kernel,
        out_shape=result,
        in_specs=[VMEM] * 3,
        out_specs=HBM,
        scratch_shapes=[pltpu.VMEM((2, half, width), F32), pltpu.SemaphoreType.DMA((6,))],
        compiler_params=PARAMS,
        name="last_part",
    )(last, part, inner_got)


def solution(mesh):
    placed = (P("member", "row", None), P("member", "row", None), P())
    return jax.shard_map(
        body, mesh=mesh, in_specs=placed, out_specs=P("member", "row", None), check_vma=False
    )
```

```python
import math

import jax
import jax.numpy as jnp
import numpy as np
from jax import lax
from jax.experimental import pallas as pl
from jax.experimental.pallas import tpu as pltpu
from jax.sharding import PartitionSpec as P

HALF = 64
SIGMA = 64
LANES = 128
TILE = 16
SPREAD, LOWEST, LEAST = 250.0, 125.0, 1e-35
PACK = 8
CUTS = (0, 8, 16)
PIECES = 4
F32 = jnp.float32
BF16 = jnp.bfloat16
NORM = math.sqrt(sum(math.exp(-k * k / (SIGMA * SIGMA)) for k in range(-HALF, HALF + 1)))

VMEM = pl.BlockSpec(memory_space=pltpu.VMEM)
HBM = pl.BlockSpec(memory_space=pltpu.HBM)
PARAMS = pltpu.CompilerParams(vmem_limit_bytes=40 * 1024 * 1024)


def split(values):
    high = values.astype(BF16)
    return high, (values - high.astype(F32)).astype(BF16)


def encode(parts):
    top = jnp.max(jnp.concatenate([jnp.abs(x) for x in parts], axis=0), axis=0, keepdims=True)
    top = (top * 1.01).astype(BF16).astype(F32)
    scale = SPREAD / jnp.maximum(top, LEAST)
    codes = []
    for x in parts:
        size = jnp.exp2(jnp.abs(x) * scale - LOWEST)
        codes.append(jnp.where(x < 0, -size, size))
    return codes, top


def decode(codes, top):
    codes = codes.astype(F32)
    size = (jnp.log2(jnp.maximum(jnp.abs(codes), 2.0**-LOWEST)) + LOWEST) * (jnp.maximum(top, LEAST) * (1.0 / SPREAD))
    return jnp.where(codes < 0, -size, size)


def dot(left, right):
    return jnp.dot(left, right, preferred_element_type=F32)


def iota(shape, dim):
    return lax.broadcasted_iota(jnp.int32, shape, dim)


def one_hot(mask, value=1.0):
    return jnp.where(mask, value, 0.0).astype(BF16)


def difference(off):
    return (jnp.where(off == 1, 1.0, 0.0) - jnp.where(off == -1, 1.0, 0.0)).astype(BF16)


def taps(offset):
    off = offset.astype(F32)
    value = jnp.exp(off * off * (-0.5 / (SIGMA * SIGMA))) * (1.0 / NORM)
    return jnp.where(jnp.abs(offset) <= HALF, value, 0.0)


def zonal_band():
    offset = np.arange(4 * LANES)[:, None] - LANES - np.arange(2 * LANES)[None, :]
    band = np.exp(-offset * offset / (2.0 * SIGMA * SIGMA)) / NORM
    band = np.where(np.abs(offset) <= HALF, band, 0.0).astype(np.float32)
    high = band.astype(BF16)
    return np.stack([high, (band - high.astype(np.float32)).astype(BF16)])


def window(first, nblocks):
    low, high = max(first - 1, 0), min(first + 3, nblocks)
    return low, high, (low - first + 1) * LANES, (high - first + 1) * LANES


def smooth_x(band_ref, load, first, nblocks):
    low, high, top, bottom = window(first, nblocks)
    both = jnp.concatenate([load(k) for k in range(low, high)], axis=1)
    rows = both.shape[0] // 2
    found = dot(both, band_ref[0, top:bottom, :])
    return found[:rows] + found[rows:] + dot(both[:rows], band_ref[1, top:bottom, :])


def parity():
    return lax.rem(lax.axis_index("row"), 2)


def block_of(refs, k):
    per = refs[0].shape[0]
    return refs[k // per].at[k % per]


def tile_at(row):
    return pl.ds(pl.multiple_of(row, TILE), TILE)


def raw_pair(first, weight, inno_ref, back_ref, upper, diff_y, diff_x, extra, raw_refs):
    levels, rows, width = inno_ref.shape
    half = rows // 2
    start = pl.multiple_of(jnp.where(upper, 0, half), TILE)
    exact = pl.ds(start, half)
    deep = pl.ds(pl.multiple_of(jnp.where(upper, 0, half - TILE), TILE), half + TILE)
    here = pl.ds(first * LANES, 2 * LANES)
    low, high, top, bottom = window(first, width // LANES)
    around = back_ref[:, exact, low * LANES : high * LANES]
    grad_xs = dot(around.reshape(levels * half, -1), diff_x[top:bottom])
    numer_y = numer_x = 0.0
    denom = 1.0
    for level in range(levels):
        grad_y = dot(diff_y, back_ref[level, deep, here])
        if extra is not None:
            grad_y += extra(level, here)
        grad_x = grad_xs[level * half : (level + 1) * half]
        scaled = inno_ref[level, exact, here].astype(F32) * (0.5 * weight(level))
        numer_y += scaled * grad_y
        numer_x += scaled * grad_x
        denom += (0.25 * weight(level)) * (grad_y * grad_y + grad_x * grad_x)
    inverse = 1.0 / denom
    found = []
    for comp, numer in enumerate((numer_y, numer_x)):
        raw = numer * inverse
        if extra is None:
            raw = jnp.where(iota(raw.shape, 0) == jnp.where(upper, 0, half - 1), 0.0, raw)
        found.append(raw)
        at = pl.ds(pl.multiple_of(comp * rows + start, TILE), half)
        for j in range(2):
            block_of(raw_refs, first + j)[at, :] = raw[:, j * LANES : (j + 1) * LANES]
    return found


def differences(upper, half):
    deep = half + TILE
    diff_y = difference(iota((half, deep), 1) - iota((half, deep), 0) - jnp.where(upper, 0, TILE))
    shape = (4 * LANES, 2 * LANES)
    return diff_y, difference(iota(shape, 0) - LANES - iota(shape, 1))


def outer_kernel(lw_hbm, inno_hbm, back_hbm, *refs):
    *raw_refs, msg_ref, row_ref, inno_ref, back_ref, weight_ref, lw_ref, pick_ref, top_ref, sems, rest_sems, lw_sem = refs
    levels, rows, width = inno_ref.shape
    half = rows // 2
    deep = half + TILE
    nblocks = width // LANES
    upper = parity() == 0
    start = jnp.where(upper, 0, half)
    cuts = [cut * nblocks // CUTS[-1] * LANES for cut in CUTS]

    def bring(sem, which, at, size, cols):
        index = (slice(None), pl.ds(pl.multiple_of(at, TILE), size), cols)
        source, target = ((inno_hbm, inno_ref), (back_hbm, back_ref))[which]
        return pltpu.make_async_copy(source.at[index], target.at[index], sem)

    weights = pltpu.make_async_copy(lw_hbm, lw_ref, lw_sem)
    copies = []
    for q, cut in enumerate(cuts[:-1]):
        cols = pl.ds(cut, cuts[q + 1] - cut)
        copies.append(
            [
                bring(sems.at[1, q], 1, jnp.where(upper, 0, rows - deep), deep, cols),
                bring(sems.at[0, q], 0, start, half, cols),
            ]
        )
    copies[-1].append(bring(rest_sems.at[1], 1, jnp.where(upper, deep, 0), rows - deep, pl.ds(0, width)))
    other = bring(rest_sems.at[0], 0, half - start, half, pl.ds(0, width))
    weights.start()
    for copy in sum(copies, []) + [other]:
        copy.start()
    diff_y, diff_x = differences(upper, half)
    outermost_row = iota((half, 2 * LANES), 0) == jnp.where(upper, 0, half - 1)
    kinds = 3 * levels - 2
    row, col = iota(pick_ref.shape[1:], 0), iota(pick_ref.shape[1:], 1)
    want = row - (col >> 6) * kinds
    level = (col >> 4) & (levels - 1)
    place = col & (TILE - 1)
    outermost = place == jnp.where(upper, 0, TILE - 1)
    next_row = place == jnp.where(upper, 1, TILE - 2)
    pick_ref[0] = one_hot(((want == level) & outermost) | ((want == levels + level) & next_row))
    half_cols = PACK * (levels - 2) * TILE
    row, col = iota((PACK * kinds, half_cols), 0), iota((PACK * kinds, half_cols), 1)
    want = row - (col >> 5) * kinds
    level = (col >> 4) & 1
    pick_ref[1, :, :half_cols] = one_hot((want == 2 * levels + level) & (col & (TILE - 1) == jnp.where(upper, 0, TILE - 1)))
    shape = (TILE, levels * TILE)
    pick_near = one_hot(iota(shape, 1) == iota(shape, 0) * TILE + jnp.where(upper, TILE - 1, 0))
    weights.wait()
    for level in range(2 * levels):
        weight_ref[level : level + 1, :] = jnp.full((1, weight_ref.shape[1]), lw_ref[level % levels])
    base = nblocks * rows

    def input_rows():
        near_rows = []
        for level in range(levels):
            ends = [back_ref[level, k : k + 1, :].astype(F32) for k in (rows - 1, 0)]
            near_rows.append(jnp.where(upper, *ends))
        near_rows.append(jnp.zeros((TILE - levels, width), F32))
        row_ref[...] = jnp.concatenate(near_rows, axis=0).astype(BF16)
        edge_at = tile_at(jnp.where(upper, 0, rows - TILE))
        for first in range(0, nblocks, PACK):
            back, inno = [], []
            for k in range(first, first + PACK):
                here = pl.ds(k * LANES, LANES)
                back.append(back_ref[:, edge_at, here].reshape(levels * TILE, LANES))
                inno.append(inno_ref[2:, edge_at, here].reshape((levels - 2) * TILE, LANES))
            tile = dot(pick_ref[0], jnp.concatenate(back, axis=0)) + dot(pick_ref[1, :, :half_cols], jnp.concatenate(inno, axis=0))
            at = base + nblocks + first * kinds
            msg_ref[pl.ds(at, PACK * kinds), :] = tile.astype(BF16)

    waited = 0
    for first in range(0, nblocks, 2):
        while cuts[waited] < window(first, nblocks)[1] * LANES:
            for copy in copies[waited]:
                copy.wait()
            waited += 1
        if first == cuts[-2] // LANES:
            input_rows()
        found = raw_pair(first, lambda k: lw_ref[k], inno_ref, back_ref, upper, diff_y, diff_x, None, raw_refs)
        codes, top = encode(found)
        for comp, code in enumerate(codes):
            inno = inno_ref[comp, pl.ds(pl.multiple_of(start, TILE), half), pl.ds(first * LANES, 2 * LANES)]
            code = jnp.where(outermost_row, inno.astype(F32), code).astype(BF16)
            for j in range(2):
                msg_ref[pl.ds((first + j) * rows + comp * half, half), :] = code[:, j * LANES : (j + 1) * LANES]
        for j in range(2):
            top_ref[first + j : first + j + 1, :] = top[:, j * LANES : (j + 1) * LANES]
    msg_ref[pl.ds(base, nblocks), :] = top_ref[...].astype(BF16)
    other.wait()


def outer_rows(rows, nblocks, levels):
    return nblocks * rows + nblocks + nblocks * (3 * levels - 2)


def inner_kernel(weight_ref, inno_ref, back_ref, row_ref, band_ref, *refs):
    raw_refs = refs[PIECES : 2 * PIECES]
    msg_ref, top_ref, both_ref = refs[2 * PIECES :]
    _, rows, width = inno_ref.shape
    half = rows // 2
    nblocks = width // LANES
    upper = parity() == 1
    start = jnp.where(upper, 0, half)
    diff_y, diff_x = differences(upper, half)
    at = iota((half, 2 * LANES), 0) == jnp.where(upper, 0, half - 1)
    sign = jnp.where(upper, -1.0, 1.0)

    def extra(level, here):
        return jnp.where(at, row_ref[level : level + 1, here].astype(F32) * sign, 0.0)

    def weight(level):
        return weight_ref[level : level + 1, :]

    for first in range(0, nblocks, 2):
        found = raw_pair(first, weight, inno_ref, back_ref, upper, diff_y, diff_x, extra, raw_refs)
        both = jnp.concatenate(split(jnp.concatenate(found, axis=0)), axis=0)
        for j in range(2):
            both_ref[first + j] = both[:, j * LANES : (j + 1) * LANES]
    for first in range(0, nblocks, 2):
        (code,), top = encode([smooth_x(band_ref, lambda k: both_ref[k], first, nblocks)])
        code = code.astype(BF16)
        for j in range(2):
            msg_ref[pl.ds((first + j) * rows, rows), :] = code[:, j * LANES : (j + 1) * LANES]
            top_ref[first + j : first + j + 1, :] = top[:, j * LANES : (j + 1) * LANES]
    msg_ref[pl.ds(nblocks * rows, nblocks), :] = top_ref[...].astype(BF16)


def inner_rows(rows, nblocks):
    return nblocks * rows + nblocks


def outermost_kernel(weight_ref, own_ref, got_ref, out_ref):
    nblocks = out_ref.shape[1] // LANES
    levels = weight_ref.shape[0] // 2
    kinds = 3 * levels - 2
    base = own_ref.shape[0] - nblocks * kinds
    rows, half = HALF, HALF // 2
    first_core = parity() == 0
    at = iota((8, rows), 0) * half

    def unpacked(ref, upper):
        packs = [ref[pl.ds(base + k * kinds, PACK * kinds), :].astype(F32) for k in range(0, nblocks, PACK)]
        pick = one_hot((iota((8, rows), 1) == at + jnp.where(upper, 0, half - 1)) & (at < rows))
        some = []
        for k in range(0, nblocks, 2):
            pair = [ref[pl.ds((k + j) * rows, rows), :] for j in range(2)]
            some.append(dot(pick, jnp.concatenate(pair, axis=1))[:2])
        found = []
        for low, high in ((0, levels), (levels, 2 * levels), (2 * levels, kinds)):
            parts = [p[j * kinds + low : j * kinds + high] for p in packs for j in range(PACK)]
            found.append(jnp.concatenate(parts, axis=1))
        found[2] = jnp.concatenate([jnp.concatenate(some, axis=1), found[2]], axis=0)
        return found

    own, got = unpacked(own_ref, first_core), unpacked(got_ref, jnp.logical_not(first_core))
    here = jnp.concatenate([own[0], got[0]], axis=0)
    beyond = jnp.concatenate([got[0], own[0]], axis=0)
    before = jnp.concatenate([own[1], got[1]], axis=0)
    inno = jnp.concatenate([own[2], got[2]], axis=0)
    shape = here.shape
    grad_y = jnp.where((iota(shape, 0) < levels) == first_core, before - beyond, beyond - before)
    lane = iota(shape, 1)
    left = jnp.where(lane == 0, 0.0, pltpu.roll(here, 1, 1))
    right = jnp.where(lane == shape[1] - 1, 0.0, pltpu.roll(here, shape[1] - 1, 1))
    grad_x = right - left
    weight = jnp.concatenate([weight_ref[:, :LANES]] * nblocks, axis=1)
    scaled = inno * (0.5 * weight)

    def total(values):
        return [sum(values[k : k + 1] for k in range(f, f + levels)) for f in (0, levels)]

    numer_y, numer_x = total(scaled * grad_y), total(scaled * grad_x)
    denom = total((0.25 * weight) * (grad_y * grad_y + grad_x * grad_x))
    found = []
    for k in range(2):
        inverse = 1.0 / (1.0 + denom[k])
        found += [numer_y[k] * inverse, numer_x[k] * inverse]
    high, low = split(jnp.concatenate(found, axis=0))
    none = jnp.zeros((TILE - 8, shape[1]), F32)
    out_ref[...] = jnp.concatenate([high.astype(F32), low.astype(F32), none], axis=0).astype(BF16)


def far_taps(rows, towards):
    side = 2 * parity() - 1
    half = rows // 2
    start = jnp.where((side < 0) == towards, half, 0)
    return taps(iota((rows, half), 1) + start - iota((rows, half), 0) + side * rows)


def near_kernel(*refs):
    raw_refs, near_refs = refs[:PIECES], refs[PIECES : 2 * PIECES]
    edges_ref, near_edges_ref, msg_ref, band_ref, out_ref, taps_ref, total_ref = refs[2 * PIECES :]
    _, rows, width = out_ref.shape
    nblocks = width // LANES
    half = rows // 2
    par = parity()
    side = 1 - 2 * par
    offset = iota((rows, rows), 1) - iota((rows, rows), 0)
    near_taps = jnp.concatenate([taps(offset), taps(offset + side * rows)], axis=1)
    column = iota(near_taps.shape, 1)
    outermost = (column == par * (rows - 1)) | (column == (2 - par) * rows - 1 + par)
    near_taps = jnp.where(outermost, 0.0, near_taps)
    toward = far_taps(rows, True)
    outermost = iota(toward.shape, 1) == jnp.where(par == 0, half - 1, 0)
    toward = jnp.where(outermost, 0.0, toward)
    outermost = iota((half, 2 * LANES), 0) == jnp.where(par == 0, half - 1, 0)
    low_taps = jnp.concatenate([near_taps, toward], axis=1).astype(BF16)
    shape = (rows, TILE)
    kind = iota(shape, 1)
    own_at = jnp.where(par == 0, 0, rows - 1)
    far_at = jnp.where(par == 0, -1, rows)
    near_at = jnp.where(par == 0, 2 * rows - 1, -rows)
    own_edges = taps(jnp.where(kind & 2 == 0, own_at, far_at) - iota(shape, 0))
    near_edges = jnp.where(kind & 2 == 0, taps(near_at - iota(shape, 0)), 0.0)
    stacked = []
    for comp in range(2):
        here = (kind < 8) & (kind & 1 == comp)
        all_taps = [near_taps, toward, jnp.where(here, own_edges, 0.0), jnp.where(here, near_edges, 0.0)]
        stacked.append(jnp.concatenate(split(jnp.concatenate(all_taps, axis=1)), axis=0))
    tops = msg_ref[pl.ds(nblocks * rows, nblocks), :].astype(F32)
    for first in range(0, nblocks, 2):
        cols = pl.ds(first * LANES, 2 * LANES)
        top = jnp.concatenate([tops[k : k + 1] for k in (first, first + 1)], axis=1)
        edges = [edges_ref[:, cols], near_edges_ref[:, cols]]
        for comp in range(2):
            here = pl.ds(comp * rows, rows)
            both, got = [], []
            for k in (first, first + 1):
                refs = (block_of(raw_refs, k), block_of(near_refs, k))
                both.append(jnp.concatenate([ref[here, :] for ref in refs], axis=0))
                got.append(msg_ref[pl.ds(k * rows + comp * half, half), :])
            got = decode(jnp.concatenate(got, axis=1), top)
            got = split(jnp.where(outermost, 0.0, got))
            highs, lows = (
                jnp.concatenate([x, y], axis=0) for x, y in zip(split(jnp.concatenate(both, axis=1)), got)
            )
            part = dot(stacked[comp], jnp.concatenate([highs] + edges, axis=0))
            high, low = split(part[:rows] + part[rows:] + dot(low_taps, lows))
            for j in range(2):
                cut = slice(j * LANES, (j + 1) * LANES)
                total_ref[first + j, pl.ds(comp * rows, rows), :] = high[:, cut]
                total_ref[first + j, pl.ds((2 + comp) * rows, rows), :] = low[:, cut]
    for first in range(0, nblocks, 2):
        result = smooth_x(band_ref, lambda k: total_ref[k], first, nblocks)
        here = pl.ds(first * LANES, 2 * LANES)
        out_ref[0, :, here] = result[:rows]
        out_ref[1, :, here] = result[rows:]
    away = far_taps(rows, False)
    high, low = split(jnp.where(par == 0, away[:half], away[half:]))
    taps_ref[...] = jnp.concatenate([high, low, high], axis=1)


def last_kernel(taps_ref, part_ref, msg_ref, out_hbm, buf, sem):
    _, rows, width = part_ref.shape
    nblocks = width // LANES
    half = rows // 2
    tops = msg_ref[pl.ds(nblocks * rows, nblocks), :].astype(F32)
    reached = pl.ds(pl.multiple_of(parity() * half, 8), half)
    rest = pl.ds(pl.multiple_of((1 - parity()) * half, 8), half)
    copies = [pltpu.make_async_copy(part_ref.at[k, rest, :], out_hbm.at[k, rest, :], sem.at[2 + k]) for k in range(2)]
    for copy in copies:
        copy.start()
    for comp in range(2):
        for first in range(0, nblocks, 2):
            here = pl.ds(first * LANES, 2 * LANES)
            top = jnp.concatenate([tops[k : k + 1] for k in (first, first + 1)], axis=1)
            got = [msg_ref[pl.ds((first + j) * rows + comp * half, half), :] for j in range(2)]
            high, low = split(decode(jnp.concatenate(got, axis=1), top))
            part = dot(taps_ref[...], jnp.concatenate([high, high, low], axis=0))
            buf[comp, :, here] = part_ref[comp, reached, here] + part
        copies.append(pltpu.make_async_copy(buf.at[comp], out_hbm.at[comp, reached, :], sem.at[comp]))
        copies[-1].start()
    for copy in copies:
        copy.wait()


def body(innovation, background, level_weight):
    levels, rows, width = innovation.shape
    if rows != HALF or width % (PACK * LANES) or levels != 4:
        raise NotImplementedError("slab shape")
    nblocks = width // LANES
    both, half = 2 * rows, rows // 2
    count = lax.axis_size("row")
    chip = [(i, i ^ 1) for i in range(count) if i ^ 1 < count]
    away = [(i, j) for i in range(count) for j in [((i + 1) ^ 1) - 1] if 0 <= j < count]
    hbm = [pltpu.with_memory_space_constraint(x, pltpu.HBM) for x in (level_weight, innovation, background)]
    band = jnp.asarray(zonal_band())
    piece = jax.ShapeDtypeStruct((nblocks // PIECES, both, LANES), F32)
    result = jax.ShapeDtypeStruct((2, rows, width), F32)
    *raws, outer, row, inno, back, weight = pl.pallas_call(
        outer_kernel,
        out_shape=[piece] * PIECES
        + [
            jax.ShapeDtypeStruct((outer_rows(rows, nblocks, levels), LANES), BF16),
            jax.ShapeDtypeStruct((TILE, width), BF16),
            jax.ShapeDtypeStruct(innovation.shape, BF16),
            jax.ShapeDtypeStruct(background.shape, BF16),
            jax.ShapeDtypeStruct((2 * levels, 2 * LANES), F32),
        ],
        in_specs=[HBM] * 3,
        out_specs=[VMEM] * (PIECES + 5),
        scratch_shapes=[
            pltpu.SMEM((levels,), F32),
            pltpu.VMEM((2, PACK * (3 * levels - 2), PACK * levels * TILE), BF16),
            pltpu.VMEM((nblocks, LANES), F32),
            pltpu.SemaphoreType.DMA((2, len(CUTS) - 1)),
            pltpu.SemaphoreType.DMA((2,)),
            pltpu.SemaphoreType.DMA,
        ],
        compiler_params=PARAMS,
        name="outer_half",
    )(*hbm)
    outer_got = lax.ppermute(outer, "row", away)
    row = lax.ppermute(row, "row", chip)
    *raws, inner = pl.pallas_call(
        inner_kernel,
        out_shape=[piece] * PIECES + [jax.ShapeDtypeStruct((inner_rows(rows, nblocks), LANES), BF16)],
        in_specs=[VMEM] * (5 + PIECES),
        out_specs=[VMEM] * (PIECES + 1),
        scratch_shapes=[pltpu.VMEM((nblocks, LANES), F32), pltpu.VMEM((nblocks, both, LANES), BF16)],
        input_output_aliases={5 + k: k for k in range(PIECES)},
        compiler_params=PARAMS,
        name="inner_half",
    )(weight, inno, back, row, band, *raws)
    inner_got = lax.ppermute(inner, "row", away)
    nears = [lax.ppermute(r, "row", chip) for r in raws]
    edges = pl.pallas_call(
        outermost_kernel,
        out_shape=jax.ShapeDtypeStruct((TILE, width), BF16),
        in_specs=[VMEM] * 3,
        out_specs=VMEM,
        compiler_params=PARAMS,
        name="outermost_rows",
    )(weight, outer, outer_got)
    near_edges = lax.ppermute(edges, "row", chip)
    part, last = pl.pallas_call(
        near_kernel,
        out_shape=[result, jax.ShapeDtypeStruct((half, 3 * half), BF16)],
        in_specs=[VMEM] * (2 * PIECES + 4),
        out_specs=[VMEM] * 2,
        scratch_shapes=[pltpu.VMEM((nblocks, 2 * both, LANES), BF16)],
        compiler_params=PARAMS,
        name="near_part",
    )(*raws, *nears, edges, near_edges, outer_got, band)
    return pl.pallas_call(
        last_kernel,
        out_shape=result,
        in_specs=[VMEM] * 3,
        out_specs=HBM,
        scratch_shapes=[pltpu.VMEM((2, half, width), F32), pltpu.SemaphoreType.DMA((4,))],
        compiler_params=PARAMS,
        name="last_part",
    )(last, part, inner_got)


def solution(mesh):
    placed = (P("member", "row", None), P("member", "row", None), P())
    return jax.shard_map(
        body, mesh=mesh, in_specs=placed, out_specs=P("member", "row", None), check_vma=False
    )
```
